32 devices in a mesh: gx: 8 (over y, x, core), gy: 4 (over z).
Axes of the slice: x: 2, y: 2, z: 4, core: 2. Of those that a mesh axis runs over, the one named last changes fastest.
Arguments:
- sources: bfloat16 [8, 4, 8, 64, 256], P('gx', 'gy'), may hold values from -12 to 12
- geometry: bfloat16 [8, 4, 8, 4, 256], P('gx', 'gy'), may hold values from -0.5 to 0.5, as said below
- near_lists: int32 [8, 4, 8, 24], P('gx', 'gy'), may hold values from -1 to 255, as said below
- far_lists: int32 [8, 4, 4, 16], P('gx', 'gy'), may hold values from 0 to 7, as said below
- bases_in: bfloat16 [8, 4, 4, 32, 8, 256], P('gx', 'gy')
- bases_out: bfloat16 [8, 4, 4, 32, 8, 256], P('gx', 'gy'), may hold values from -0.25 to 0.25
- couplings: float32 [8, 4, 4, 32, 512], P('gx', 'gy')
Outputs:
- potential: float32 [8, 4, 8, 64, 256], P('gx', 'gy')
The draws below stay inside these ranges and needn't reach their ends.
Inputs may be any that keep to these rules, and one draw needn't show every extreme that they name: `near_lists`: for each leaf the first c entries are live, c between 1 and 24 and equal to 24 on some leaves and to 1 on others; the first is the leaf itself, and every live entry names a leaf on a device whose gx and gy indices differ from the leaf's by at most one, in a slot that differs from the leaf's slot by at most one; the other entries are -1. `far_lists`: level 0 entries are below 4, levels 1 and 2 below 8, level 3 below 2. `geometry`: rows 0 to 2 lie in [-0.5, 0.5], row 3 about 0.006 to 0.04.
All inputs are finite; a program needn't handle non-finite values.
Results may differ from the reference program's by a relative error of at most 0.0029.
Values may be sent and summed in bfloat16 or wider, within the bound.
A program may use at most 64 MiB of HBM per device.

```python
import math
import jax
import jax.numpy as jnp
from jax import lax

LEAF = 256
RHS = 64
RANK = 32
LEVELS = 4
NEAR = 24
FAR = 16
LEAF_DEV = 8
ROW_DEVS = 8
COLUMN_DEVS = 4
N_GX = 8
N_GY = 4


def level_groups(shape):
    level = lax.broadcasted_iota(jnp.int32, shape, 2)
    return jnp.where(level == 0, 1, jnp.where(level == 1, 4, jnp.where(level == 2, COLUMN_DEVS, 4 * COLUMN_DEVS))).astype(jnp.float32)


def draw_geometry(key, part):
    keys = jax.random.split(key, 5)
    shape = (ROW_DEVS, COLUMN_DEVS, LEAF_DEV, 3, LEAF)
    face_pick = 3.0 * jax.random.uniform(keys[0], (ROW_DEVS, COLUMN_DEVS, LEAF_DEV, 1, LEAF), jnp.float32)
    component = lax.broadcasted_iota(jnp.int32, shape, 3).astype(jnp.float32)
    on_face = (face_pick >= component) & (face_pick < component + 1.0)
    side = jnp.where(jax.random.uniform(keys[1], shape, jnp.float32) < 0.5, -1.0, 1.0)
    depth_draw = jax.random.uniform(keys[2], shape, jnp.float32)
    tangent_draw = jax.random.uniform(keys[3], shape, jnp.float32, -1.0, 1.0)
    depth = 0.5 - 0.03 * depth_draw
    tangent = 0.5 * jnp.sign(tangent_draw) * jnp.sqrt(jnp.abs(tangent_draw))
    offsets = jnp.where(on_face, side * depth, tangent)
    areas = jnp.exp(jax.random.uniform(keys[4], (ROW_DEVS, COLUMN_DEVS, LEAF_DEV, 1, LEAF), jnp.float32, math.log(0.006), math.log(0.04)))
    return jnp.concatenate([offsets, areas], axis=3).astype(jnp.bfloat16)


def draw_near_lists(key, part):
    keys = jax.random.split(key, 5)
    shape = (ROW_DEVS, COLUMN_DEVS, LEAF_DEV, NEAR)
    row_pos = lax.broadcasted_iota(jnp.int32, shape, 0)
    col_pos = lax.broadcasted_iota(jnp.int32, shape, 1)
    leaf_pos = lax.broadcasted_iota(jnp.int32, shape, 2)
    slot_pos = lax.broadcasted_iota(jnp.int32, shape, 3)
    base = jax.random.randint(keys[0], (ROW_DEVS, COLUMN_DEVS, 1, 1), max(1, NEAR // 4), NEAR + 1)
    count = base - jax.random.randint(keys[1], (ROW_DEVS, COLUMN_DEVS, LEAF_DEV, 1), 0, base // 2 + 1)
    flat = row_pos * COLUMN_DEVS + col_pos
    count = jnp.where((flat % 5 == 0) & (leaf_pos == 0), NEAR, count)
    count = jnp.where((flat % 5 == 1) & (leaf_pos == 0), 1, count)
    src_row = jnp.clip(row_pos + jax.random.randint(keys[2], shape, -1, 2), 0, ROW_DEVS - 1)
    src_col = jnp.clip(col_pos + jax.random.randint(keys[3], shape, -1, 2), 0, COLUMN_DEVS - 1)
    src_leaf = jnp.clip(leaf_pos + jax.random.randint(keys[4], shape, -1, 2), 0, LEAF_DEV - 1)
    leaf_ids = (src_row * COLUMN_DEVS + src_col) * LEAF_DEV + src_leaf
    itself = flat * LEAF_DEV + leaf_pos
    leaf_ids = jnp.where(slot_pos == 0, itself, leaf_ids)
    return jnp.where(slot_pos < count, leaf_ids, -1).astype(jnp.int32)


def draw_far_lists(key, part):
    shape = (ROW_DEVS, COLUMN_DEVS, LEVELS, FAR)
    row_pos = lax.broadcasted_iota(jnp.int32, shape, 0)
    col_pos = lax.broadcasted_iota(jnp.int32, shape, 1)
    level = lax.broadcasted_iota(jnp.int32, shape, 2)
    slot_pos = lax.broadcasted_iota(jnp.int32, shape, 3)
    limit = jnp.where(level == 0, COLUMN_DEVS, jnp.where(level == 3, ROW_DEVS // 4, ROW_DEVS))
    cluster = jax.random.randint(key, shape, 0, limit)
    flat = row_pos * COLUMN_DEVS + col_pos
    return jnp.where(slot_pos == FAR - 1, flat % limit, cluster).astype(jnp.int32)


def draw_bases_in(key, part):
    shape = (ROW_DEVS, COLUMN_DEVS, LEVELS, RANK, LEAF_DEV, LEAF)
    scale = 0.5 * (level_groups(shape) * LEAF_DEV * LEAF) ** (-0.5)
    values = jax.random.normal(key, shape, jnp.float32)
    return (values * scale).astype(jnp.bfloat16)


def draw_couplings(key, part):
    shape = (ROW_DEVS, COLUMN_DEVS, LEVELS, RANK, FAR * RANK)
    scale = (level_groups(shape) * FAR * RANK) ** (-0.5)
    values = jax.random.normal(key, shape, jnp.float32)
    return values * scale


def block_scale(rng, shape, pieces, low, largest):
    def one(axis_at, shards_of):
        heights = jax.random.uniform(jax.random.fold_in(jax.random.fold_in(rng, 6), axis_at), (shards_of,), jnp.float32, low / len(pieces), largest / len(pieces))
        return jnp.repeat(jnp.exp(heights), shape[axis_at] // shards_of).reshape((-1,) + (1,) * (len(shape) - axis_at - 1))

    level = one(*pieces[0])
    for cut in pieces[1:]:
        level = level * one(*cut)
    return level


def bell_draw(own_key, extent, spread, most, cuts=(), kind=jnp.bfloat16):
    entries = jax.random.normal(own_key, extent, jnp.float32) * spread
    if len(cuts) > 0:
        entries = block_scale(own_key, extent, cuts, -0.22, 0.18) * entries
    return jnp.clip(entries, min=-most, max=most).astype(kind)


def setup_inputs(seed: int = 0) -> dict:
    seeds = jax.random.split(jax.random.key(seed), 8)
    return {
        "sources": bell_draw(seeds[0], (ROW_DEVS, COLUMN_DEVS, LEAF_DEV, RHS, LEAF), 2.0, 12.0, ((0, 8), (1, 4))),
        "geometry": draw_geometry(jax.random.fold_in(seeds[7], 71), 0),
        "near_lists": draw_near_lists(jax.random.fold_in(seeds[7], 71), 0),
        "far_lists": draw_far_lists(jax.random.fold_in(seeds[7], 71), 0),
        "bases_in": draw_bases_in(jax.random.fold_in(seeds[7], 71), 0),
        "bases_out": bell_draw(seeds[5], (ROW_DEVS, COLUMN_DEVS, LEVELS, RANK, LEAF_DEV, LEAF), (16 * RANK) ** -0.5, 0.25, ((0, 8), (1, 4))),
        "couplings": draw_couplings(jax.random.fold_in(seeds[7], 71), 0),
    }


FOUR_PI = 4.0 * math.pi

def leaf_centers(leaf_ids):
    device = leaf_ids // LEAF_DEV
    return jnp.stack([device // N_GY, device % N_GY, leaf_ids % LEAF_DEV], axis=-1).astype(jnp.float32)

def near_block(target_geo, target_center, source_geo, source_center, source_vals, weight):
    target_pos = target_geo[:, :3, :].astype(jnp.float32) + target_center[:, :, None]
    source_pos = source_geo[:, :3, :].astype(jnp.float32) + source_center[:, :, None]
    squared = jnp.zeros((target_pos.shape[0], target_pos.shape[2], source_pos.shape[2]), jnp.float32)
    for component in range(3):
        offset = target_pos[:, component, :, None] - source_pos[:, component, None, :]
        squared = squared + offset * offset
    panel_area = source_geo[:, 3, :].astype(jnp.float32)[:, None, :]
    kernel = (weight[:, None, None] * panel_area / (FOUR_PI * jnp.sqrt(squared + panel_area))).astype(jnp.bfloat16)
    kernel = lax.optimization_barrier(kernel)
    return jnp.einsum('lij,lrj->lri', kernel.astype(jnp.float32), source_vals.astype(jnp.float32))

def reference(sources, geometry, near_lists, far_lists, bases_in, bases_out, couplings):
    devices = N_GX * N_GY
    flat_src = sources.reshape(devices * LEAF_DEV, RHS, LEAF)
    flat_geo = geometry.reshape(devices * LEAF_DEV, 4, LEAF)
    lists = near_lists.reshape(devices, LEAF_DEV, NEAR)

    def one_device(packed):
        device, table = packed
        own = device * LEAF_DEV + jnp.arange(LEAF_DEV, dtype=jnp.int32)
        target_geo = flat_geo[own]
        target_center = leaf_centers(own)
        total = jnp.zeros((LEAF_DEV, RHS, LEAF), jnp.float32)
        for slot in range(NEAR):
            leaf_ids = table[:, slot]
            weight = (leaf_ids >= 0).astype(jnp.float32)
            safe = jnp.maximum(leaf_ids, 0).astype(jnp.int32)
            total = total + near_block(target_geo, target_center, flat_geo[safe], leaf_centers(safe), flat_src[safe], weight)
        return total
    near_field = lax.map(one_device, (jnp.arange(devices, dtype=jnp.int32), lists)).reshape(sources.shape)
    projection = jnp.einsum('xyaqlp,xylrp->xyaqr', bases_in.astype(jnp.float32), sources.astype(jnp.float32))
    level_zero = projection[:, :, 0]
    level_one = projection[:, :, 1].reshape(N_GX, N_GY // 4, 4, RANK, RHS).sum(axis=2)
    level_two = projection[:, :, 2].sum(axis=1)
    level_three = projection[:, :, 3].sum(axis=1).reshape(N_GX // 4, 4, RANK, RHS).sum(axis=1)
    row_index = jnp.arange(N_GX, dtype=jnp.int32)[:, None, None]
    quarter_index = (jnp.arange(N_GY, dtype=jnp.int32) // 4)[None, :, None]
    picked_zero = level_zero[row_index, far_lists[:, :, 0]]
    picked_one = level_one[far_lists[:, :, 1], quarter_index]
    picked_two = level_two[far_lists[:, :, 2]]
    picked_three = level_three[far_lists[:, :, 3]]
    gathered = jnp.stack([picked_zero, picked_one, picked_two, picked_three], axis=2)
    gathered = gathered.reshape(N_GX, N_GY, 4, FAR * RANK, RHS)
    interaction = jnp.einsum('xyaqk,xyakr->xyaqr', couplings, gathered, precision=lax.Precision.HIGHEST)
    summed_zero = interaction[:, :, 0]
    summed_one = jnp.repeat(interaction[:, :, 1].reshape(N_GX, N_GY // 4, 4, RANK, RHS).sum(axis=2), 4, axis=1)
    summed_two = jnp.broadcast_to(interaction[:, :, 2].sum(axis=1, keepdims=True), summed_zero.shape)
    coarse_total = interaction[:, :, 3].sum(axis=1).reshape(N_GX // 4, 4, RANK, RHS).sum(axis=1)
    summed_three = jnp.broadcast_to(jnp.repeat(coarse_total, 4, axis=0)[:, None], summed_zero.shape)
    target_sum = jnp.stack([summed_zero, summed_one, summed_two, summed_three], axis=2).astype(jnp.bfloat16)
    target_sum = lax.optimization_barrier(target_sum)
    far_field = jnp.einsum('xyaqr,xyaqlp->xylrp', target_sum.astype(jnp.float32), bases_out.astype(jnp.float32))
    return near_field + far_field
```

```python
import functools
import math

import jax
import jax.numpy as jnp
from jax import lax
from jax.experimental import pallas as pl
from jax.experimental.pallas import tpu as pltpu
from jax.sharding import PartitionSpec as P

FOUR_PI = 4.0 * math.pi
MESH = pl.DeviceIdType.MESH
BF16 = jnp.bfloat16
F32 = jnp.float32
FEATURES = 48


def dot(a, b, da=1, db=0):
    return lax.dot_general(a, b, (((da,), (db,)), ((), ())), preferred_element_type=F32)


def rounded(v):
    return v.astype(BF16).astype(F32)


def pieces(v):
    high = rounded(v)
    mid = rounded(v - high)
    return high, mid, rounded(v - high - mid)


def total(terms):
    return functools.reduce(jnp.add, terms)


def kernel(
    n_gx, n_gy, src_in, geo, near, far, in_in, out_in, coup_in, out,
    hsrc, gbuf, gf, lists, weight, sfeat, tfeat, acc, res, rbuf,
    base_in, base_out, flat, by_leaf, coup,
    proj, col_buf, row_src, row_buf, tab3, gath, int_src, int_buf, c3_src, c3_buf, target,
    load, geo_s, geo_r, list_s, list_r, src_s, src_r, res_s, res_r,
    p1_s, p1_r, p2_s, p2_r, p3_s, p3_r, p4_s, p4_r,
):
    x = lax.axis_index("gx")
    y = lax.axis_index("gy")
    leaf_dev, rhs, panels = out.shape
    slots = near.shape[1]
    barrier = pltpu.get_barrier_semaphore()
    for k in range(1, n_gx):
        pl.semaphore_signal(
            barrier, inc=1, device_id=(lax.rem(x + k, n_gx), y), device_id_type=MESH
        )
    for k in range(1, n_gy):
        pl.semaphore_signal(
            barrier, inc=1, device_id=(x, lax.rem(y + k, n_gy)), device_id_type=MESH
        )

    loads = [
        pltpu.make_async_copy(a, b, load.at[i])
        for i, (a, b) in enumerate(
            [(src_in, hsrc.at[1]), (in_in, base_in), (coup_in, coup), (out_in, base_out)]
        )
    ]
    for one in loads:
        one.start()

    def remote(src, dst, send, recv, where):
        return pltpu.make_async_remote_copy(
            src_ref=src, dst_ref=dst, send_sem=send, recv_sem=recv,
            device_id=where, device_id_type=MESH,
        )

    def has(d, at, n):
        return at > 0 if d < 0 else at < n - 1

    sides = (-1, 1)

    def geo_y(d):
        return remote(gbuf.at[1], gbuf.at[1 - d], geo_s.at[1 + d], geo_r.at[1 - d], (x, y + d))

    def geo_x(d):
        return remote(
            gbuf.at[1], gbuf.at[4 - d], geo_s.at[4 + d], geo_r.at[4 - d], (x + d, y)
        )

    def list_x(d):
        return remote(lists.at[1], lists.at[1 - d], list_s.at[1 + d], list_r.at[1 - d], (x + d, y))

    def src_y(d):
        return remote(hsrc.at[1], hsrc.at[1 - d], src_s.at[1 + d], src_r.at[1 - d], (x, y + d))

    def res_x(d):
        return remote(res.at[1 + d], rbuf.at[1 - d], res_s.at[1 + d], res_r.at[1 - d], (x + d, y))

    def arrived(make, d):
        if make is geo_y:
            c = remote(gbuf.at[1], gbuf.at[1 + d], geo_s.at[1 + d], geo_r.at[1 + d], (x, y + d))
        elif make is geo_x:
            c = remote(gbuf.at[1], gbuf.at[4 + d], geo_s.at[4 + d], geo_r.at[4 + d], (x + d, y))
        elif make is list_x:
            c = remote(
                lists.at[1], lists.at[1 + d], list_s.at[1 + d], list_r.at[1 + d], (x + d, y)
            )
        elif make is src_y:
            c = remote(hsrc.at[1], hsrc.at[1 + d], src_s.at[1 + d], src_r.at[1 + d], (x, y + d))
        else:
            c = remote(res.at[1 + d], rbuf.at[1 + d], res_s.at[1 + d], res_r.at[1 + d], (x + d, y))
        c.wait_recv()

    def column(src, buf, send, recv):
        for k in range(1, n_gy):
            to = lax.rem(y + k, n_gy)
            remote(src, buf.at[y], send.at[k], recv.at[y], (x, to)).start()
        buf[y] = src[...]

    def column_wait(src, buf, send, recv):
        for k in range(1, n_gy):
            peer = lax.rem(y + k, n_gy)
            remote(src, buf.at[peer], send.at[k], recv.at[peer], (x, peer)).wait_recv()

    row_at = lax.broadcasted_iota(jnp.int32, (8, panels), 0)
    quarter = 4 * (y // 4)
    half = rhs
    base = 4 * (x // 4)
    spot = lax.rem(x, 4)

    own = geo[...].astype(F32)
    own = jnp.concatenate([own, jnp.zeros((leaf_dev, 4, panels), F32)], axis=1)
    own = own.reshape(8 * leaf_dev, panels)
    gbuf[1] = own.astype(BF16)
    gf[1] = own
    lists[1] = jnp.full(lists.shape[1:], -1, jnp.int32)
    lists[1, :, 0:slots] = near[...]

    def source_features(place):
        shift = lax.convert_element_type(place - 1, F32)

        def leaf(k, carry):
            q = gf[place, pl.ds(pl.multiple_of(8 * k, 8), 8), :]
            q = jnp.where(row_at == 1, q + shift, q)
            area = q[3:4]
            factor = FOUR_PI / area
            factor = factor * factor
            square = q[0:1] * q[0:1] + q[1:2] * q[1:2] + q[2:3] * q[2:3] + area
            one = jnp.where(row_at == 4, 1.0, 0.0)
            v = jnp.where(row_at < 3, q, jnp.where(row_at == 3, square, one)) * factor
            a, b, c = pieces(v)
            wide = jnp.concatenate([a, b, c, a, b, a], axis=0)
            sfeat[place * leaf_dev + k] = wide.T.astype(BF16)
            return carry

        lax.fori_loop(0, leaf_dev, leaf, 0)

    def target_features(side, at):
        def leaf(l, carry):
            p = gf[at, pl.ds(pl.multiple_of(8 * l, 8), 8), :]
            p = jnp.where(row_at == 0, p + float(side), p)
            for dz in (-1, 0, 1):
                t = jnp.where(row_at == 2, p - float(dz), p)
                square = t[0:1] * t[0:1] + t[1:2] * t[1:2] + t[2:3] * t[2:3]
                last = jnp.where(row_at == 4, square, 0.0)
                v = jnp.where(row_at < 3, -2.0 * t, jnp.where(row_at == 3, 1.0, last))
                a, b, c = pieces(v)
                wide = jnp.concatenate([a, a, a, b, b, c], axis=0)
                tfeat[((side + 1) * leaf_dev + l) * 3 + dz + 1] = wide.astype(BF16)
            return carry

        lax.fori_loop(0, leaf_dev, leaf, 0)

    def weights(side):
        mine = lists[side + 1]
        leaf = lax.broadcasted_iota(jnp.int32, mine.shape, 0)
        for s in range(3):
            for dz in (-1, 0, 1):
                n = (x * n_gy + y + s - 1) * leaf_dev + dz + leaf
                hits = jnp.where(mine == n, 1.0, 0.0)
                count = jnp.sum(hits, axis=1, keepdims=True)
                weight[((side + 1) * 3 + s) * 3 + dz + 1] = jnp.broadcast_to(
                    count, (leaf_dev, panels)
                )

    def transposed(source, take):
        wide = source[...].astype(F32)
        for h in range(panels // 128):
            flat[h] = wide[:, 128 * h : 128 * (h + 1)]
        for k in range(leaf_dev):
            take(
                k,
                jnp.concatenate(
                    [
                        flat[h, pl.ds(k, 128, stride=leaf_dev), :]
                        for h in range(panels // 128)
                    ],
                    axis=1,
                ).astype(BF16),
            )

    loads[0].wait()
    loads[1].wait()
    parts = []
    transposed(base_in, lambda k, b: parts.append(dot(b, hsrc[1, k], 1, 1)))
    projection = total(parts)
    proj[:, 0:half] = projection[0:64]
    proj[:, half:] = projection[64:128]

    pl.semaphore_wait(barrier, n_gx - 1 + n_gy - 1)
    column(proj, col_buf, p1_s, p1_r)
    for d in sides:
        @pl.when(has(d, x, n_gx))
        def _():
            geo_x(d).start()
            list_x(d).start()

        @pl.when(has(d, y, n_gy))
        def _():
            geo_y(d).start()
            src_y(d).start()

    source_features(1)
    target_features(0, 1)
    weights(0)
    acc[...] = jnp.zeros_like(acc)
    for d in sides:
        @pl.when(jnp.logical_not(has(d, x, n_gx)))
        def _():
            rbuf[1 + d] = jnp.zeros(rbuf.shape[1:], BF16)

    def coupled(level):
        c = coup[level]
        c_high = c.astype(BF16)
        c_low = (c - c_high.astype(F32)).astype(BF16)
        g = gath[...]
        g_high = g.astype(BF16)
        g_low = (g - g_high.astype(F32)).astype(BF16)
        return dot(c_high, g_high) + (dot(c_low, g_high) + dot(c_high, g_low))

    def after_first():
        column_wait(proj, col_buf, p1_s, p1_r)
        row_src[0:32, 0:half] = total([col_buf[quarter + g, 32:64, 0:half] for g in range(4)])
        coarse = total([col_buf[g, :, half:] for g in range(n_gy)])
        row_src[0:32, half:] = coarse[0:32]
        row_src[32:48, 0:half] = coarse[32:48]
        row_src[32:48, half:] = coarse[48:64]
        for k in range(1, n_gx):
            to = lax.rem(x + k, n_gx)
            remote(row_src, row_buf.at[x], p2_s.at[k], p2_r.at[x], (to, y)).start()
        row_buf[x] = row_src[...]
        loads[2].wait()
        for m in range(16):
            gath[pl.ds(m * 32, 32), :] = col_buf[far[0, m], 0:32, 0:half]
        target[0:32, :] = coupled(0)

    def after_second():
        for k in range(1, n_gx):
            peer = lax.rem(x + k, n_gx)
            remote(row_src, row_buf.at[peer], p2_s.at[k], p2_r.at[peer], (peer, y)).wait_recv()
        for c in range(n_gx // 4):
            coarse = total([row_buf[4 * c + g, 32:48, :] for g in range(4)])
            tab3[c, 0:16, :] = coarse[:, 0:half]
            tab3[c, 16:32, :] = coarse[:, half:]
        for level in (1, 2, 3):
            for m in range(16):
                s = far[level, m]
                if level == 3:
                    gath[pl.ds(m * 32, 32), :] = tab3[s]
                elif level == 1:
                    gath[pl.ds(m * 32, 32), :] = row_buf[s, 0:32, 0:half]
                else:
                    gath[pl.ds(m * 32, 32), :] = row_buf[s, 0:32, half:]
            term = coupled(level)
            if level == 1:
                int_src[0:32, 0:half] = term
            elif level == 2:
                int_src[0:32, half:] = term
            else:
                int_src[32:48, 0:half] = term[0:16]
                int_src[32:48, half:] = term[16:32]
        column(int_src, int_buf, p3_s, p3_r)

    def after_third():
        column_wait(int_src, int_buf, p3_s, p3_r)
        c3_src[...] = total([int_buf[g, 32:48, :] for g in range(n_gy)])
        for k in range(1, 4):
            to = base + lax.rem(spot + k, 4)
            remote(c3_src, c3_buf.at[spot], p4_s.at[k], p4_r.at[spot], (to, y)).start()
        c3_buf[spot] = c3_src[...]
        target[32:64, :] = total([int_buf[quarter + g, 0:32, 0:half] for g in range(4)])
        target[64:96, :] = total([int_buf[g, 0:32, half:] for g in range(n_gy)])

    def after_fourth():
        for k in range(1, 4):
            peer = lax.rem(spot + k, 4)
            remote(
                c3_src, c3_buf.at[peer], p4_s.at[k], p4_r.at[peer], (base + peer, y)
            ).wait_recv()
        coarse = total([c3_buf[g] for g in range(4)])
        target[96:112, :] = coarse[:, 0:half]
        target[112:128, :] = coarse[:, half:]
        loads[3].wait()

        def take(k, b):
            by_leaf[k] = b

        transposed(base_out, take)

    def from_row():
        for d in sides:
            @pl.when(has(d, x, n_gx))
            def _():
                arrived(geo_x, d)
                arrived(list_x, d)
                gf[4 + d] = gbuf[4 + d].astype(F32)
                target_features(d, 4 + d)
                weights(d)

    def from_column():
        for d in sides:
            @pl.when(has(d, y, n_gy))
            def _():
                arrived(geo_y, d)
                gf[1 + d] = gbuf[1 + d].astype(F32)
                source_features(1 + d)
                arrived(src_y, d)

    def give(d):
        @pl.when(has(d, x, n_gx))
        def _():
            res[1 + d] = acc[1 + d].astype(BF16)
            res_x(d).start()

    def chunk(s, t):
        for l in range(leaf_dev):
            ks = [k for k in (l - 1, l, l + 1) if 0 <= k < leaf_dev]
            mats = []
            for k in ks:
                dz = k - l
                squared = dot(sfeat[s * leaf_dev + k], tfeat[(t * leaf_dev + l) * 3 + dz + 1])
                w = weight[(t * 3 + s) * 3 + dz + 1, l : l + 1, :]
                mats.append((lax.rsqrt(squared) * w).astype(BF16))
            wide = jnp.concatenate([hsrc[s, k] for k in ks], axis=1)
            acc[t, l] += dot(wide, jnp.concatenate(mats, axis=0))

    def step(c, carry):
        stages = {
            1: [from_row],
            2: [after_first],
            3: [from_column, after_second],
            5: [lambda: give(1), after_third],
            7: [lambda: give(-1), after_fourth],
        }
        for at, work in stages.items():
            @pl.when(c == at)
            def _():
                for one in work:
                    one()

        s = jnp.where(c < 3, 1, 2 * lax.rem(c, 2))
        late = jnp.where(c < 5, 2, jnp.where(c < 7, 0, 1))
        t = jnp.where(c == 0, 1, jnp.where(c == 2, 0, late))
        at_x, at_y = x + t - 1, y + s - 1
        inside = jnp.logical_and(
            jnp.logical_and(at_x >= 0, at_x < n_gx), jnp.logical_and(at_y >= 0, at_y < n_gy)
        )

        @pl.when(inside)
        def _():
            chunk(s, t)

        return carry

    lax.fori_loop(0, 9, step, 0)

    turned = target[...].T.astype(BF16)
    for d in sides:
        @pl.when(has(d, x, n_gx))
        def _():
            arrived(res_x, d)
    for k in range(leaf_dev):
        near_field = acc[1, k] + (rbuf[0, k].astype(F32) + rbuf[2, k].astype(F32))
        out[k] = near_field + dot(turned, by_leaf[k])

    for d in sides:
        @pl.when(has(d, x, n_gx))
        def _():
            geo_x(d).wait_send()
            list_x(d).wait_send()
            res_x(d).wait_send()

        @pl.when(has(d, y, n_gy))
        def _():
            geo_y(d).wait_send()
            src_y(d).wait_send()
    for k in range(1, n_gy):
        to = lax.rem(y + k, n_gy)
        remote(proj, col_buf.at[y], p1_s.at[k], p1_r.at[y], (x, to)).wait_send()
        remote(int_src, int_buf.at[y], p3_s.at[k], p3_r.at[y], (x, to)).wait_send()
    for k in range(1, n_gx):
        to = lax.rem(x + k, n_gx)
        remote(row_src, row_buf.at[x], p2_s.at[k], p2_r.at[x], (to, y)).wait_send()
    for k in range(1, 4):
        to = base + lax.rem(spot + k, 4)
        remote(c3_src, c3_buf.at[spot], p4_s.at[k], p4_r.at[spot], (to, y)).wait_send()


def body(sources, geometry, near_lists, far_lists, bases_in, bases_out, couplings):
    leaf_dev, rhs, panels = sources.shape[2:]
    n_gx, n_gy = lax.axis_size("gx"), lax.axis_size("gy")
    vmem = pl.BlockSpec(memory_space=pltpu.VMEM)
    anywhere = pl.BlockSpec(memory_space=pl.ANY)
    sems = pltpu.SemaphoreType.DMA
    flat_rows = bases_in.shape[2] * bases_in.shape[3] * leaf_dev
    potential = pl.pallas_call(
        functools.partial(kernel, n_gx, n_gy),
        out_shape=jax.ShapeDtypeStruct((leaf_dev, rhs, panels), F32),
        in_specs=[
            anywhere, vmem, vmem, pl.BlockSpec(memory_space=pltpu.SMEM),
            anywhere, anywhere, anywhere,
        ],
        out_specs=vmem,
        scratch_shapes=[
            pltpu.VMEM((3, leaf_dev, rhs, panels), BF16),
            pltpu.VMEM((6, 8 * leaf_dev, panels), BF16),
            pltpu.VMEM((6, 8 * leaf_dev, panels), F32),
            pltpu.VMEM((3, leaf_dev, 128), jnp.int32),
            pltpu.VMEM((27, leaf_dev, panels), F32),
            pltpu.VMEM((3 * leaf_dev, panels, FEATURES), BF16),
            pltpu.VMEM((9 * leaf_dev, FEATURES, panels), BF16),
            pltpu.VMEM((3, leaf_dev, rhs, panels), F32),
            pltpu.VMEM((3, leaf_dev, rhs, panels), BF16),
            pltpu.VMEM((3, leaf_dev, rhs, panels), BF16),
            pltpu.VMEM((flat_rows, panels), BF16),
            pltpu.VMEM((flat_rows, panels), BF16),
            pltpu.VMEM((panels // 128, flat_rows, 128), F32),
            pltpu.VMEM((leaf_dev, 128, panels), BF16),
            pltpu.VMEM(couplings.shape[2:], F32),
            pltpu.VMEM((64, 2 * rhs), F32),
            pltpu.VMEM((n_gy, 64, 2 * rhs), F32),
            pltpu.VMEM((48, 2 * rhs), F32),
            pltpu.VMEM((n_gx, 48, 2 * rhs), F32),
            pltpu.VMEM((n_gx // 4, 32, rhs), F32),
            pltpu.VMEM((512, rhs), F32),
            pltpu.VMEM((48, 2 * rhs), F32),
            pltpu.VMEM((n_gy, 48, 2 * rhs), F32),
            pltpu.VMEM((16, 2 * rhs), F32),
            pltpu.VMEM((4, 16, 2 * rhs), F32),
            pltpu.VMEM((128, rhs), F32),
            sems((4,)),
            sems((6,)), sems((6,)), sems((3,)), sems((3,)),
            sems((3,)), sems((3,)), sems((3,)), sems((3,)),
            sems((n_gy,)), sems((n_gy,)),
            sems((n_gx,)), sems((n_gx,)),
            sems((n_gy,)), sems((n_gy,)),
            sems((4,)), sems((4,)),
        ],
        compiler_params=pltpu.CompilerParams(
            collective_id=0, has_side_effects=True, vmem_limit_bytes=40 * 1024 * 1024
        ),
    )(
        sources[0, 0], geometry[0, 0], near_lists[0, 0], far_lists[0, 0],
        bases_in.reshape(flat_rows, panels), bases_out.reshape(flat_rows, panels),
        couplings[0, 0],
    )
    return potential.reshape(sources.shape)


def solution(mesh):
    in_specs = (
        P("gx", "gy", None, None, None),
        P("gx", "gy", None, None, None),
        P("gx", "gy", None, None),
        P("gx", "gy", None, None),
        P("gx", "gy", None, None, None, None),
        P("gx", "gy", None, None, None, None),
        P("gx", "gy", None, None, None),
    )
    out_specs = P("gx", "gy", None, None, None)
    return jax.shard_map(body, mesh=mesh, in_specs=in_specs, out_specs=out_specs, check_vma=False)
```

```python
import functools
import math

import jax
import jax.numpy as jnp
from jax import lax
from jax.experimental import pallas as pl
from jax.experimental.pallas import tpu as pltpu
from jax.sharding import PartitionSpec as P

FOUR_PI = 4.0 * math.pi
MESH = pl.DeviceIdType.MESH
BF16 = jnp.bfloat16
F32 = jnp.float32
FEATURES = 48


def dot(a, b, da=1, db=0):
    return lax.dot_general(a, b, (((da,), (db,)), ((), ())), preferred_element_type=F32)


def rounded(v):
    return v.astype(BF16).astype(F32)


def pieces(v):
    high = rounded(v)
    mid = rounded(v - high)
    return high, mid, rounded(v - high - mid)


def total(terms):
    return functools.reduce(jnp.add, terms)


def kernel(
    n_gx, n_gy, src_in, geo_in, near_in, far, in_in, out_in, coup_in, out,
    geo, near, hsrc, gbuf, gf, lists, weight, sfeat, tfeat, acc, res, rbuf,
    base_in, base_out, flat, by_leaf, coup,
    mats, proj, col_buf, row_src, row_buf, tab3, gath, int_src, int_buf, c3_src, c3_buf, target,
    load, geo_s, geo_r, list_s, list_r, src_s, src_r, res_s, res_r,
    p1_s, p1_r, p2_s, p2_r, p3_s, p3_r, p4_s, p4_r,
):
    x = lax.axis_index("gx")
    y = lax.axis_index("gy")
    leaf_dev, rhs, panels = out.shape
    slots = near.shape[1]
    middle = leaf_dev // 2
    first = middle + 1
    barrier = pltpu.get_barrier_semaphore()
    for k in range(1, n_gx):
        pl.semaphore_signal(
            barrier, inc=1, device_id=(lax.rem(x + k, n_gx), y), device_id_type=MESH
        )
    for k in range(1, n_gy):
        pl.semaphore_signal(
            barrier, inc=1, device_id=(x, lax.rem(y + k, n_gy)), device_id_type=MESH
        )

    loads = [
        pltpu.make_async_copy(a, b, load.at[i])
        for i, (a, b) in enumerate(
            [(src_in, hsrc.at[1]), (in_in, base_in), (coup_in, coup), (out_in, base_out), (geo_in, geo), (near_in, near)]
        )
    ]
    for one in loads:
        one.start()

    def remote(src, dst, send, recv, where):
        return pltpu.make_async_remote_copy(
            src_ref=src, dst_ref=dst, send_sem=send, recv_sem=recv,
            device_id=where, device_id_type=MESH,
        )

    def has(d, at, n):
        return at > 0 if d < 0 else at < n - 1

    sides = (-1, 1)

    def geo_y(d):
        return remote(gbuf.at[1], gbuf.at[1 - d], geo_s.at[1 + d], geo_r.at[1 - d], (x, y + d))

    def geo_x(d):
        return remote(
            gbuf.at[1], gbuf.at[4 - d], geo_s.at[4 + d], geo_r.at[4 - d], (x + d, y)
        )

    def list_x(d):
        return remote(lists.at[1], lists.at[1 - d], list_s.at[1 + d], list_r.at[1 - d], (x + d, y))

    def src_y(d, h):
        part = pl.ds(first * h, first if h == 0 else leaf_dev - first)
        return remote(
            hsrc.at[1, part], hsrc.at[1 - d, part],
            src_s.at[1 + d, h], src_r.at[1 - d, h], (x, y + d),
        )

    def res_x(d, h):
        part = pl.ds(middle * h, middle)
        return remote(
            res.at[1 + d, part], rbuf.at[1 - d, part],
            res_s.at[1 + d, h], res_r.at[1 - d, h], (x + d, y),
        )

    def arrived(make, d, h=0):
        if make is geo_y:
            c = remote(gbuf.at[1], gbuf.at[1 + d], geo_s.at[1 + d], geo_r.at[1 + d], (x, y + d))
        elif make is geo_x:
            c = remote(gbuf.at[1], gbuf.at[4 + d], geo_s.at[4 + d], geo_r.at[4 + d], (x + d, y))
        elif make is list_x:
            c = remote(
                lists.at[1], lists.at[1 + d], list_s.at[1 + d], list_r.at[1 + d], (x + d, y)
            )
        elif make is src_y:
            part = pl.ds(first * h, first if h == 0 else leaf_dev - first)
            c = remote(
                hsrc.at[1, part], hsrc.at[1 + d, part],
                src_s.at[1 + d, h], src_r.at[1 + d, h], (x, y + d),
            )
        else:
            part = pl.ds(middle * h, middle)
            c = remote(
                res.at[1 + d, part], rbuf.at[1 + d, part],
                res_s.at[1 + d, h], res_r.at[1 + d, h], (x + d, y),
            )
        c.wait_recv()

    def column(src, buf, send, recv):
        for k in range(1, n_gy):
            to = lax.rem(y + k, n_gy)
            remote(src, buf.at[y], send.at[k], recv.at[y], (x, to)).start()
        buf[y] = src[...]

    def column_wait(src, buf, send, recv):
        for k in range(1, n_gy):
            peer = lax.rem(y + k, n_gy)
            remote(src, buf.at[peer], send.at[k], recv.at[peer], (x, peer)).wait_recv()

    row_at = lax.broadcasted_iota(jnp.int32, (8, panels), 0)
    quarter = 4 * (y // 4)
    half = rhs
    base = 4 * (x // 4)
    spot = lax.rem(x, 4)

    loads[4].wait()
    loads[5].wait()
    own = geo[...].astype(F32)
    own = jnp.concatenate([own, jnp.zeros((leaf_dev, 4, panels), F32)], axis=1)
    own = own.reshape(8 * leaf_dev, panels)
    gbuf[1] = own.astype(BF16)
    gf[1] = own
    lists[1] = jnp.full(lists.shape[1:], -1, jnp.int32)
    lists[1, :, 0:slots] = near[...]

    def source_features(place):
        shift = lax.convert_element_type(place - 1, F32)

        def leaf(k, carry):
            q = gf[place, pl.ds(pl.multiple_of(8 * k, 8), 8), :]
            q = jnp.where(row_at == 1, q + shift, q)
            area = q[3:4]
            factor = FOUR_PI / area
            factor = factor * factor
            square = q[0:1] * q[0:1] + q[1:2] * q[1:2] + q[2:3] * q[2:3] + area
            one = jnp.where(row_at == 4, 1.0, 0.0)
            v = jnp.where(row_at < 3, q, jnp.where(row_at == 3, square, one)) * factor
            a, b, c = pieces(v)
            wide = jnp.concatenate([a, b, c, a, b, a], axis=0)
            sfeat[place * leaf_dev + k] = wide.T.astype(BF16)
            return carry

        lax.fori_loop(0, leaf_dev, leaf, 0, unroll=4)

    def target_features(side, at):
        def leaf(l, carry):
            p = gf[at, pl.ds(pl.multiple_of(8 * l, 8), 8), :]
            p = jnp.where(row_at == 0, p + float(side), p)
            for dz in (-1, 0, 1):
                t = jnp.where(row_at == 2, p - float(dz), p)
                square = t[0:1] * t[0:1] + t[1:2] * t[1:2] + t[2:3] * t[2:3]
                last = jnp.where(row_at == 4, square, 0.0)
                v = jnp.where(row_at < 3, -2.0 * t, jnp.where(row_at == 3, 1.0, last))
                a, b, c = pieces(v)
                wide = jnp.concatenate([a, a, a, b, b, c], axis=0)
                tfeat[((side + 1) * leaf_dev + l) * 3 + dz + 1] = wide.astype(BF16)
            return carry

        lax.fori_loop(0, leaf_dev, leaf, 0, unroll=4)

    def weights(side):
        mine = lists[side + 1]
        leaf = lax.broadcasted_iota(jnp.int32, mine.shape, 0)
        for s in range(3):
            for dz in (-1, 0, 1):
                n = (x * n_gy + y + s - 1) * leaf_dev + dz + leaf
                there = jnp.logical_and(y + s >= 1, y + s <= n_gy)
                hits = jnp.where(jnp.logical_and(mine == n, there), 1.0, 0.0)
                count = jnp.sum(hits, axis=1, keepdims=True)
                weight[((side + 1) * 3 + s) * 3 + dz + 1] = jnp.broadcast_to(
                    count, (leaf_dev, panels)
                )

    def transposed(source, take):
        wide = source[...].astype(F32)
        for h in range(panels // 128):
            flat[h] = wide[:, 128 * h : 128 * (h + 1)]
        for k in range(leaf_dev):
            take(
                k,
                jnp.concatenate(
                    [
                        flat[h, pl.ds(k, 128, stride=leaf_dev), :]
                        for h in range(panels // 128)
                    ],
                    axis=1,
                ).astype(BF16),
            )

    source_features(1)
    target_features(0, 1)
    weights(0)
    acc[...] = jnp.zeros_like(acc)

    loads[0].wait()
    loads[1].wait()
    parts = []
    transposed(base_in, lambda k, b: parts.append(dot(b, hsrc[1, k], 1, 1)))
    projection = total(parts)
    proj[:, 0:half] = projection[0:64]
    proj[:, half:] = projection[64:128]

    pl.semaphore_wait(barrier, n_gx - 1 + n_gy - 1)
    column(proj, col_buf, p1_s, p1_r)
    for d in sides:
        @pl.when(has(d, x, n_gx))
        def _():
            geo_x(d).start()
            list_x(d).start()

        @pl.when(has(d, y, n_gy))
        def _():
            geo_y(d).start()
            src_y(d, 0).start()
            src_y(d, 1).start()

    lane = lax.broadcasted_iota(jnp.int32, (panels, FEATURES), 1)
    away = jnp.where(lane == 3, 1.0, 0.0).astype(BF16)
    for d in sides:
        @pl.when(jnp.logical_not(has(d, x, n_gx)))
        def _():
            rbuf[1 + d] = jnp.zeros(rbuf.shape[1:], BF16)

        @pl.when(jnp.logical_not(has(d, y, n_gy)))
        def _():
            hsrc[1 + d] = jnp.zeros(hsrc.shape[1:], BF16)
            for k in range(leaf_dev):
                sfeat[(1 + d) * leaf_dev + k] = away

    def coupled(level):
        c = coup[level]
        c_high = c.astype(BF16)
        c_low = (c - c_high.astype(F32)).astype(BF16)
        g = gath[...]
        g_high = g.astype(BF16)
        g_low = (g - g_high.astype(F32)).astype(BF16)
        return dot(c_high, g_high) + (dot(c_low, g_high) + dot(c_high, g_low))

    def after_first():
        column_wait(proj, col_buf, p1_s, p1_r)
        row_src[0:32, 0:half] = total([col_buf[quarter + g, 32:64, 0:half] for g in range(4)])
        coarse = total([col_buf[g, :, half:] for g in range(n_gy)])
        row_src[0:32, half:] = coarse[0:32]
        row_src[32:48, 0:half] = coarse[32:48]
        row_src[32:48, half:] = coarse[48:64]
        for k in range(1, n_gx):
            to = lax.rem(x + k, n_gx)
            remote(row_src, row_buf.at[x], p2_s.at[k], p2_r.at[x], (to, y)).start()
        row_buf[x] = row_src[...]
        loads[2].wait()
        for m in range(16):
            gath[pl.ds(m * 32, 32), :] = col_buf[far[0, m], 0:32, 0:half]
        target[0:32, :] = coupled(0)

    def after_second():
        for k in range(1, n_gx):
            peer = lax.rem(x + k, n_gx)
            remote(row_src, row_buf.at[peer], p2_s.at[k], p2_r.at[peer], (peer, y)).wait_recv()
        for c in range(n_gx // 4):
            coarse = total([row_buf[4 * c + g, 32:48, :] for g in range(4)])
            tab3[c, 0:16, :] = coarse[:, 0:half]
            tab3[c, 16:32, :] = coarse[:, half:]
        for level in (1, 2, 3):
            for m in range(16):
                s = far[level, m]
                if level == 3:
                    gath[pl.ds(m * 32, 32), :] = tab3[s]
                elif level == 1:
                    gath[pl.ds(m * 32, 32), :] = row_buf[s, 0:32, 0:half]
                else:
                    gath[pl.ds(m * 32, 32), :] = row_buf[s, 0:32, half:]
            term = coupled(level)
            if level == 1:
                int_src[0:32, 0:half] = term
            elif level == 2:
                int_src[0:32, half:] = term
            else:
                int_src[32:48, 0:half] = term[0:16]
                int_src[32:48, half:] = term[16:32]
        column(int_src, int_buf, p3_s, p3_r)

    def after_third():
        column_wait(int_src, int_buf, p3_s, p3_r)
        c3_src[...] = total([int_buf[g, 32:48, :] for g in range(n_gy)])
        for k in range(1, 4):
            to = base + lax.rem(spot + k, 4)
            remote(c3_src, c3_buf.at[spot], p4_s.at[k], p4_r.at[spot], (to, y)).start()
        c3_buf[spot] = c3_src[...]
        target[32:64, :] = total([int_buf[quarter + g, 0:32, 0:half] for g in range(4)])
        target[64:96, :] = total([int_buf[g, 0:32, half:] for g in range(n_gy)])

    def after_fourth():
        for k in range(1, 4):
            peer = lax.rem(spot + k, 4)
            remote(
                c3_src, c3_buf.at[peer], p4_s.at[k], p4_r.at[peer], (base + peer, y)
            ).wait_recv()
        coarse = total([c3_buf[g] for g in range(4)])
        target[96:112, :] = coarse[:, 0:half]
        target[112:128, :] = coarse[:, half:]
    def turn_bases():
        loads[3].wait()

        def take(k, b):
            by_leaf[k] = b

        transposed(base_out, take)

    def from_row():
        for d in sides:
            @pl.when(has(d, x, n_gx))
            def _():
                arrived(geo_x, d)
                arrived(list_x, d)
                gf[4 + d] = gbuf[4 + d].astype(F32)
                target_features(d, 4 + d)
                weights(d)

    def from_column():
        for d in sides:
            @pl.when(has(d, y, n_gy))
            def _():
                arrived(geo_y, d)
                gf[1 + d] = gbuf[1 + d].astype(F32)
                source_features(1 + d)
                arrived(src_y, d, 0)

    def rest_of_column():
        for d in sides:
            @pl.when(has(d, y, n_gy))
            def _():
                arrived(src_y, d, 1)

    def give(h):
        for d in sides:
            @pl.when(has(d, x, n_gx))
            def _():
                part = slice(middle * h, middle * h + middle)
                res[1 + d, part] = acc[1 + d, part].astype(BF16)
                res_x(d, h).start()

    def chunk(t, halves):
        work = [(s, h, i) for s, h in halves for i in range(middle)]

        def leaves(h, i):
            sign = 1 - 2 * h
            l = (leaf_dev - 1) * h + sign * i
            return l, [(l + sign * e, sign * e) for e in (-1, 0, 1) if i + e >= 0]

        def fill(n):
            s, h, i = work[n]
            l, ks = leaves(h, i)
            for at, (k, dz) in enumerate(ks):
                squared = dot(sfeat[s * leaf_dev + k], tfeat[(t * leaf_dev + l) * 3 + dz + 1])
                w = weight[(t * 3 + s) * 3 + dz + 1, pl.ds(l, 1), :]
                mats[n % 2, panels * at : panels * (at + 1), :] = (
                    lax.rsqrt(squared) * w
                ).astype(BF16)

        def apply(n):
            s, h, i = work[n]
            l, ks = leaves(h, i)
            wide = jnp.concatenate([hsrc[s, k] for k, _ in ks], axis=1)
            acc[t, l] += dot(wide, mats[n % 2, 0 : panels * len(ks), :])

        fill(0)
        for n in range(len(work)):
            if n + 1 < len(work):
                fill(n + 1)
            apply(n)

    def step(c, carry):
        stages = {
            1: [from_row],
            2: [after_first],
            3: [from_column],
            4: [after_second],
            5: [lambda: give(0), rest_of_column],
            7: [lambda: give(1), after_third],
            8: [turn_bases],
        }
        for at, work in stages.items():
            @pl.when(c == at)
            def _():
                for one in work:
                    one()

        own_turn = c < 3
        t = jnp.where(jnp.logical_or(c == 0, c > 6), 1, 2 * lax.rem(c, 2))
        half_turn = jnp.where(c < 7, (c - 3) // 2, c - 7)
        a = (jnp.where(own_turn, 1, 2), jnp.where(own_turn, 0, half_turn))
        b = (jnp.where(own_turn, 1, 0), jnp.where(own_turn, 1, half_turn))
        at_x = x + t - 1

        @pl.when(jnp.logical_and(at_x >= 0, at_x < n_gx))
        def _():
            chunk(t, [a, b])

        return carry

    lax.fori_loop(0, 9, step, 0)

    after_fourth()
    turned = target[...].T.astype(BF16)
    for d in sides:
        @pl.when(has(d, x, n_gx))
        def _():
            arrived(res_x, d, 0)
            arrived(res_x, d, 1)
    for k in range(leaf_dev):
        near_field = acc[1, k] + (rbuf[0, k].astype(F32) + rbuf[2, k].astype(F32))
        out[k] = near_field + dot(turned, by_leaf[k])

    for d in sides:
        @pl.when(has(d, x, n_gx))
        def _():
            geo_x(d).wait_send()
            list_x(d).wait_send()
            res_x(d, 0).wait_send()
            res_x(d, 1).wait_send()

        @pl.when(has(d, y, n_gy))
        def _():
            geo_y(d).wait_send()
            src_y(d, 0).wait_send()
            src_y(d, 1).wait_send()
    for k in range(1, n_gy):
        to = lax.rem(y + k, n_gy)
        remote(proj, col_buf.at[y], p1_s.at[k], p1_r.at[y], (x, to)).wait_send()
        remote(int_src, int_buf.at[y], p3_s.at[k], p3_r.at[y], (x, to)).wait_send()
    for k in range(1, n_gx):
        to = lax.rem(x + k, n_gx)
        remote(row_src, row_buf.at[x], p2_s.at[k], p2_r.at[x], (to, y)).wait_send()
    for k in range(1, 4):
        to = base + lax.rem(spot + k, 4)
        remote(c3_src, c3_buf.at[spot], p4_s.at[k], p4_r.at[spot], (to, y)).wait_send()


def body(sources, geometry, near_lists, far_lists, bases_in, bases_out, couplings):
    leaf_dev, rhs, panels = sources.shape[2:]
    n_gx, n_gy = lax.axis_size("gx"), lax.axis_size("gy")
    vmem = pl.BlockSpec(memory_space=pltpu.VMEM)
    anywhere = pl.BlockSpec(memory_space=pl.ANY)
    sems = pltpu.SemaphoreType.DMA
    flat_rows = bases_in.shape[2] * bases_in.shape[3] * leaf_dev
    potential = pl.pallas_call(
        functools.partial(kernel, n_gx, n_gy),
        out_shape=jax.ShapeDtypeStruct((leaf_dev, rhs, panels), F32),
        in_specs=[
            anywhere, anywhere, anywhere, pl.BlockSpec(memory_space=pltpu.SMEM),
            anywhere, anywhere, anywhere,
        ],
        out_specs=vmem,
        scratch_shapes=[
            pltpu.VMEM(geometry.shape[2:], BF16),
            pltpu.VMEM(near_lists.shape[2:], jnp.int32),
            pltpu.VMEM((3, leaf_dev, rhs, panels), BF16),
            pltpu.VMEM((6, 8 * leaf_dev, panels), BF16),
            pltpu.VMEM((6, 8 * leaf_dev, panels), F32),
            pltpu.VMEM((3, leaf_dev, 128), jnp.int32),
            pltpu.VMEM((27, leaf_dev, panels), F32),
            pltpu.VMEM((3 * leaf_dev, panels, FEATURES), BF16),
            pltpu.VMEM((9 * leaf_dev, FEATURES, panels), BF16),
            pltpu.VMEM((3, leaf_dev, rhs, panels), F32),
            pltpu.VMEM((3, leaf_dev, rhs, panels), BF16),
            pltpu.VMEM((3, leaf_dev, rhs, panels), BF16),
            pltpu.VMEM((flat_rows, panels), BF16),
            pltpu.VMEM((flat_rows, panels), BF16),
            pltpu.VMEM((panels // 128, flat_rows, 128), F32),
            pltpu.VMEM((leaf_dev, 128, panels), BF16),
            pltpu.VMEM(couplings.shape[2:], F32),
            pltpu.VMEM((2, 3 * panels, panels), BF16),
            pltpu.VMEM((64, 2 * rhs), F32),
            pltpu.VMEM((n_gy, 64, 2 * rhs), F32),
            pltpu.VMEM((48, 2 * rhs), F32),
            pltpu.VMEM((n_gx, 48, 2 * rhs), F32),
            pltpu.VMEM((n_gx // 4, 32, rhs), F32),
            pltpu.VMEM((512, rhs), F32),
            pltpu.VMEM((48, 2 * rhs), F32),
            pltpu.VMEM((n_gy, 48, 2 * rhs), F32),
            pltpu.VMEM((16, 2 * rhs), F32),
            pltpu.VMEM((4, 16, 2 * rhs), F32),
            pltpu.VMEM((128, rhs), F32),
            sems((6,)),
            sems((6,)), sems((6,)), sems((3,)), sems((3,)),
            sems((3, 2)), sems((3, 2)), sems((3, 2)), sems((3, 2)),
            sems((n_gy,)), sems((n_gy,)),
            sems((n_gx,)), sems((n_gx,)),
            sems((n_gy,)), sems((n_gy,)),
            sems((4,)), sems((4,)),
        ],
        compiler_params=pltpu.CompilerParams(
            collective_id=0, has_side_effects=True, vmem_limit_bytes=60 * 1024 * 1024
        ),
    )(
        sources[0, 0], geometry[0, 0], near_lists[0, 0], far_lists[0, 0],
        bases_in.reshape(flat_rows, panels), bases_out.reshape(flat_rows, panels),
        couplings[0, 0],
    )
    return potential.reshape(sources.shape)


def solution(mesh):
    in_specs = (
        P("gx", "gy", None, None, None),
        P("gx", "gy", None, None, None),
        P("gx", "gy", None, None),
        P("gx", "gy", None, None),
        P("gx", "gy", None, None, None, None),
        P("gx", "gy", None, None, None, None),
        P("gx", "gy", None, None, None),
    )
    out_specs = P("gx", "gy", None, None, None)
    return jax.shard_map(body, mesh=mesh, in_specs=in_specs, out_specs=out_specs, check_vma=False)
```

```python
import functools
import math

import jax
import jax.numpy as jnp
from jax import lax
from jax.experimental import pallas as pl
from jax.experimental.pallas import tpu as pltpu
from jax.sharding import PartitionSpec as P

FOUR_PI = 4.0 * math.pi
MESH = pl.DeviceIdType.MESH
BF16 = jnp.bfloat16
F32 = jnp.float32
FEATURES = 48


def dot(a, b, da=1, db=0):
    return lax.dot_general(a, b, (((da,), (db,)), ((), ())), preferred_element_type=F32)


def rounded(v):
    return v.astype(BF16).astype(F32)


def pieces(v):
    high = rounded(v)
    mid = rounded(v - high)
    return high, mid, rounded(v - high - mid)


def total(terms):
    return functools.reduce(jnp.add, terms)


def kernel(
    n_gx, n_gy, src_in, geo_in, near_in, far, in_in, out_in, coup_in, out, rbuf,
    geo, near, hsrc, gbuf, gf, lists, weight, sfeat, tfeat, acc, res, zeros,
    base_in, base_out, flat, by_leaf, target, coup, level0, level12, blocks, block_buf, group_src, group_buf,
    mats, proj, col_buf, row_src, row_buf, tab3, int_src, int_buf,
    load, out_s, fill_s, geo_s, geo_r, list_s, list_r, src_s, src_r, res_s, res_r,
    p1_s, p1_r, p2_s, p2_r, p3_s, p3_r,
    block_s, block_r, group_s, group_r,
):
    x = lax.axis_index("gx")
    y = lax.axis_index("gy")
    leaf_dev, rhs, panels = out.shape
    slots = near.shape[1]
    middle = leaf_dev // 2
    first = middle + 1
    barrier = pltpu.get_barrier_semaphore()
    for k in range(1, n_gx):
        pl.semaphore_signal(
            barrier, inc=1, device_id=(lax.rem(x + k, n_gx), y), device_id_type=MESH
        )
    for k in range(1, n_gy):
        pl.semaphore_signal(
            barrier, inc=1, device_id=(x, lax.rem(y + k, n_gy)), device_id_type=MESH
        )

    loads = [
        pltpu.make_async_copy(a, b, load.at[i])
        for i, (a, b) in enumerate(
            [
                (src_in, hsrc.at[1]), (in_in, base_in), (coup_in, coup), (geo_in, geo), (near_in, near),
                (out_in, base_out),
            ]
        )
    ]
    for one in loads:
        one.start()

    def remote(src, dst, send, recv, where):
        return pltpu.make_async_remote_copy(
            src_ref=src, dst_ref=dst, send_sem=send, recv_sem=recv,
            device_id=where, device_id_type=MESH,
        )

    def has(d, at, n):
        return at > 0 if d < 0 else at < n - 1

    sides = (-1, 1)

    def geo_y(d):
        return remote(gbuf.at[1], gbuf.at[1 - d], geo_s.at[1 + d], geo_r.at[1 - d], (x, y + d))

    def geo_x(d):
        return remote(
            gbuf.at[1], gbuf.at[4 - d], geo_s.at[4 + d], geo_r.at[4 - d], (x + d, y)
        )

    def list_x(d):
        return remote(lists.at[1], lists.at[1 - d], list_s.at[1 + d], list_r.at[1 - d], (x + d, y))

    def src_y(d, h):
        part = pl.ds(first * h, first if h == 0 else leaf_dev - first)
        return remote(
            hsrc.at[1, part], hsrc.at[1 - d, part],
            src_s.at[1 + d, h], src_r.at[1 - d, h], (x, y + d),
        )

    def res_x(d, h):
        part = pl.ds(middle * h, middle)
        return remote(
            res.at[1 + d, part], rbuf.at[(1 - d) // 2, part],
            res_s.at[1 + d, h], res_r.at[1 - d, h], (x + d, y),
        )

    def absent(d):
        return pltpu.make_async_copy(zeros, rbuf.at[(1 + d) // 2], fill_s.at[(1 + d) // 2])

    def store(k):
        return pltpu.make_async_copy(acc.at[1, k], out.at[k], out_s.at[k])

    def arrived(make, d, h=0):
        if make is geo_y:
            c = remote(gbuf.at[1], gbuf.at[1 + d], geo_s.at[1 + d], geo_r.at[1 + d], (x, y + d))
        elif make is geo_x:
            c = remote(gbuf.at[1], gbuf.at[4 + d], geo_s.at[4 + d], geo_r.at[4 + d], (x + d, y))
        elif make is list_x:
            c = remote(
                lists.at[1], lists.at[1 + d], list_s.at[1 + d], list_r.at[1 + d], (x + d, y)
            )
        elif make is src_y:
            part = pl.ds(first * h, first if h == 0 else leaf_dev - first)
            c = remote(
                hsrc.at[1, part], hsrc.at[1 + d, part],
                src_s.at[1 + d, h], src_r.at[1 + d, h], (x, y + d),
            )
        else:
            part = pl.ds(middle * h, middle)
            c = remote(
                res.at[1 + d, part], rbuf.at[(1 + d) // 2, part],
                res_s.at[1 + d, h], res_r.at[1 + d, h], (x + d, y),
            )
        c.wait_recv()

    def column(src, buf, send, recv):
        for k in range(1, n_gy):
            to = lax.rem(y + k, n_gy)
            remote(src, buf.at[y], send.at[k], recv.at[y], (x, to)).start()
        buf[y] = src[...]

    def column_wait(src, buf, send, recv):
        for k in range(1, n_gy):
            peer = lax.rem(y + k, n_gy)
            remote(src, buf.at[peer], send.at[k], recv.at[peer], (x, peer)).wait_recv()

    row_at = lax.broadcasted_iota(jnp.int32, (8, panels), 0)
    quarter = 4 * (y // 4)
    half = rhs
    base = 4 * (x // 4)
    spot = lax.rem(x, 4)
    mine = lax.rem(y, 4)
    wide3 = 32 * (n_gx // 4)

    loads[3].wait()
    loads[4].wait()
    def product(a, b):
        a_high, b_high = a.astype(BF16), b.astype(BF16)
        a_low = (a - a_high.astype(F32)).astype(BF16)
        b_low = (b - b_high.astype(F32)).astype(BF16)
        return dot(a_high, b_high) + (dot(a_low, b_high) + dot(a_high, b_low))

    def by_cluster(level, clusters):
        shape = (32, 32 * clusters)
        lane = lax.broadcasted_iota(jnp.int32, shape, 1)
        place = lane >> 5
        same = (lane & 31) == lax.broadcasted_iota(jnp.int32, shape, 0)
        pick = [
            jnp.where(jnp.logical_and(same, place == far[level, m]), 1.0, 0.0).astype(BF16)
            for m in range(16)
        ]
        split = jnp.concatenate(pieces(coup[level]), axis=0).astype(BF16)
        v = dot(split, jnp.concatenate(pick, axis=0))
        return (v[0:32] + v[32:64]) + v[64:96]

    def block_copy(k):
        to = lax.rem(y + k, n_gy)
        return remote(
            blocks.at[lax.rem(to, 4)], block_buf.at[y], block_s.at[k], block_r.at[y], (x, to)
        )

    def group_copy(k):
        to = base + lax.rem(spot + k, 4)
        return remote(group_src, group_buf.at[spot], group_s.at[k], group_r.at[spot], (to, y))

    def gather_couplings():
        v = by_cluster(3, n_gx // 4)
        for b in range(4):
            blocks[b, :, 0 : v.shape[1]] = v[8 * b : 8 * b + 8]

    def give_couplings():
        for k in range(1, n_gy):
            block_copy(k).start()
        block_buf[y] = blocks[mine]

    def own_couplings():
        level0[...] = by_cluster(0, n_gy)
        level12[0:32, :] = by_cluster(1, n_gx)
        level12[32:64, :] = by_cluster(2, n_gx)

    own = geo[...].astype(F32)
    own = jnp.concatenate([own, jnp.zeros((leaf_dev, 4, panels), F32)], axis=1)
    own = own.reshape(8 * leaf_dev, panels)
    gbuf[1] = own.astype(BF16)
    gf[1] = own
    lists[1] = jnp.full(lists.shape[1:], -1, jnp.int32)
    lists[1, :, 0:slots] = near[...]

    def source_features(place):
        shift = lax.convert_element_type(place - 1, F32)

        def leaf(k, carry):
            q = gf[place, pl.ds(pl.multiple_of(8 * k, 8), 8), :]
            q = jnp.where(row_at == 1, q + shift, q)
            area = q[3:4]
            factor = FOUR_PI / area
            factor = factor * factor
            square = q[0:1] * q[0:1] + q[1:2] * q[1:2] + q[2:3] * q[2:3] + area
            one = jnp.where(row_at == 4, 1.0, 0.0)
            v = jnp.where(row_at < 3, q, jnp.where(row_at == 3, square, one)) * factor
            a, b, c = pieces(v)
            wide = jnp.concatenate([a, b, c, a, b, a], axis=0)
            sfeat[place * leaf_dev + k] = wide.T.astype(BF16)
            return carry

        lax.fori_loop(0, leaf_dev, leaf, 0, unroll=4)

    def target_features(side, at):
        def leaf(l, carry):
            p = gf[at, pl.ds(pl.multiple_of(8 * l, 8), 8), :]
            p = jnp.where(row_at == 0, p + float(side), p)
            for dz in (-1, 0, 1):
                t = jnp.where(row_at == 2, p - float(dz), p)
                square = t[0:1] * t[0:1] + t[1:2] * t[1:2] + t[2:3] * t[2:3]
                last = jnp.where(row_at == 4, square, 0.0)
                v = jnp.where(row_at < 3, -2.0 * t, jnp.where(row_at == 3, 1.0, last))
                a, b, c = pieces(v)
                wide = jnp.concatenate([a, a, a, b, b, c], axis=0)
                tfeat[((side + 1) * leaf_dev + l) * 3 + dz + 1] = wide.astype(BF16)
            return carry

        lax.fori_loop(0, leaf_dev, leaf, 0, unroll=4)

    def weights(side):
        mine = lists[side + 1]
        leaf = lax.broadcasted_iota(jnp.int32, mine.shape, 0)
        for s in range(3):
            for dz in (-1, 0, 1):
                n = (x * n_gy + y + s - 1) * leaf_dev + dz + leaf
                there = jnp.logical_and(y + s >= 1, y + s <= n_gy)
                hits = jnp.where(jnp.logical_and(mine == n, there), 1.0, 0.0)
                count = jnp.sum(hits, axis=1, keepdims=True)
                weight[((side + 1) * 3 + s) * 3 + dz + 1] = jnp.broadcast_to(
                    count, (leaf_dev, panels)
                )

    def transposed(source, take):
        wide = source[...].astype(F32)
        for h in range(panels // 128):
            flat[h] = wide[:, 128 * h : 128 * (h + 1)]
        for k in range(leaf_dev):
            take(
                k,
                jnp.concatenate(
                    [
                        flat[h, pl.ds(k, 128, stride=leaf_dev), :]
                        for h in range(panels // 128)
                    ],
                    axis=1,
                ).astype(BF16),
            )

    source_features(1)
    target_features(0, 1)
    weights(0)
    acc[...] = jnp.zeros_like(acc)

    loads[0].wait()
    loads[1].wait()
    parts = []
    transposed(base_in, lambda k, b: parts.append(dot(b, hsrc[1, k], 1, 1)))
    projection = total(parts)
    proj[:, 0:half] = projection[0:64]
    proj[:, half:] = projection[64:128]

    loads[2].wait()
    gather_couplings()
    pl.semaphore_wait(barrier, n_gx - 1 + n_gy - 1)
    column(proj, col_buf, p1_s, p1_r)
    give_couplings()
    for d in sides:
        @pl.when(has(d, x, n_gx))
        def _():
            geo_x(d).start()
            list_x(d).start()

        @pl.when(has(d, y, n_gy))
        def _():
            geo_y(d).start()
            src_y(d, 0).start()
            src_y(d, 1).start()

    lane = lax.broadcasted_iota(jnp.int32, (panels, FEATURES), 1)
    away = jnp.where(lane == 3, 1.0, 0.0).astype(BF16)
    for d in sides:
        @pl.when(jnp.logical_not(has(d, x, n_gx)))
        def _():
            zeros[...] = jnp.zeros(zeros.shape, BF16)
            absent(d).start()

        @pl.when(jnp.logical_not(has(d, y, n_gy)))
        def _():
            hsrc[1 + d] = jnp.zeros(hsrc.shape[1:], BF16)
            for k in range(leaf_dev):
                sfeat[(1 + d) * leaf_dev + k] = away

    def after_first():
        column_wait(proj, col_buf, p1_s, p1_r)
        row_src[0:32, 0:half] = total([col_buf[quarter + g, 32:64, 0:half] for g in range(4)])
        coarse = total([col_buf[g, :, half:] for g in range(n_gy)])
        row_src[0:32, half:] = coarse[0:32]
        row_src[32:48, 0:half] = coarse[32:48]
        row_src[32:48, half:] = coarse[48:64]
        for k in range(1, n_gx):
            to = lax.rem(x + k, n_gx)
            remote(row_src, row_buf.at[x], p2_s.at[k], p2_r.at[x], (to, y)).start()
        row_buf[x] = row_src[...]
        for k in range(1, n_gy):
            peer = lax.rem(y + k, n_gy)
            remote(
                blocks.at[0], block_buf.at[peer], block_s.at[k], block_r.at[peer], (x, peer)
            ).wait_recv()
        group_src[:, 0:wide3] = total([block_buf[g, :, 0:wide3] for g in range(n_gy)])
        for k in range(1, 4):
            group_copy(k).start()
        group_buf[spot] = group_src[...]
        zero = jnp.concatenate([col_buf[g, 0:32, 0:half] for g in range(n_gy)], axis=0)
        target[0:32, :] = product(level0[...], zero).astype(BF16)

    def after_second():
        for k in range(1, n_gx):
            peer = lax.rem(x + k, n_gx)
            remote(row_src, row_buf.at[peer], p2_s.at[k], p2_r.at[peer], (peer, y)).wait_recv()
        for k in range(1, 4):
            peer = lax.rem(spot + k, 4)
            remote(
                group_src, group_buf.at[peer], group_s.at[k], group_r.at[peer], (base + peer, y)
            ).wait_recv()
        fine = jnp.concatenate([row_buf[g, 0:32] for g in range(n_gx)], axis=0)
        both = product(level12[...], fine)
        int_src[0:32, 0:half] = both[0:32, 0:half]
        int_src[0:32, half:] = both[32:64, half:]
        for c in range(n_gx // 4):
            coarse = total([row_buf[4 * c + g, 32:48, :] for g in range(4)])
            tab3[32 * c : 32 * c + 16, :] = coarse[:, 0:half]
            tab3[32 * c + 16 : 32 * c + 32, :] = coarse[:, half:]
        third = total([group_buf[g, :, 0:wide3] for g in range(4)])
        int_src[32:40, 0:half] = product(third, tab3[...])
        int_src[32:40, half:] = jnp.zeros((8, half), F32)
        column(int_src, int_buf, p3_s, p3_r)

    def after_third():
        column_wait(int_src, int_buf, p3_s, p3_r)
        target[32:64, :] = total([int_buf[quarter + g, 0:32, 0:half] for g in range(4)]).astype(BF16)
        target[64:96, :] = total([int_buf[g, 0:32, half:] for g in range(n_gy)]).astype(BF16)
        third = [int_buf[quarter + b, 32:40, 0:half] for b in range(4)]
        target[96:128, :] = jnp.concatenate(third, axis=0).astype(BF16)

    def turn_bases():
        loads[5].wait()

        def take(k, b):
            by_leaf[k] = b

        transposed(base_out, take)

    def from_row():
        for d in sides:
            @pl.when(has(d, x, n_gx))
            def _():
                arrived(geo_x, d)
                arrived(list_x, d)
                gf[4 + d] = gbuf[4 + d].astype(F32)
                target_features(d, 4 + d)
                weights(d)

    def from_column():
        for d in sides:
            @pl.when(has(d, y, n_gy))
            def _():
                arrived(geo_y, d)
                gf[1 + d] = gbuf[1 + d].astype(F32)
                source_features(1 + d)
                arrived(src_y, d, 0)

    def rest_of_column():
        for d in sides:
            @pl.when(has(d, y, n_gy))
            def _():
                arrived(src_y, d, 1)

    def give(h):
        for d in sides:
            @pl.when(has(d, x, n_gx))
            def _():
                part = slice(middle * h, middle * h + middle)
                res[1 + d, part] = acc[1 + d, part].astype(BF16)
                res_x(d, h).start()

    def chunk(t, halves):
        work = [(s, h, i) for s, h in halves for i in range(middle)]

        def leaves(h, i):
            sign = 1 - 2 * h
            l = (leaf_dev - 1) * h + sign * i
            return l, [(l + sign * e, sign * e) for e in (-1, 0, 1) if i + e >= 0]

        def fill(n):
            s, h, i = work[n]
            l, ks = leaves(h, i)
            for at, (k, dz) in enumerate(ks):
                squared = dot(sfeat[s * leaf_dev + k], tfeat[(t * leaf_dev + l) * 3 + dz + 1])
                w = weight[(t * 3 + s) * 3 + dz + 1, pl.ds(l, 1), :]
                mats[n % 2, panels * at : panels * (at + 1), :] = (
                    lax.rsqrt(squared) * w
                ).astype(BF16)

        def apply(n):
            s, h, i = work[n]
            l, ks = leaves(h, i)
            wide = jnp.concatenate([hsrc[s, k] for k, _ in ks], axis=1)
            acc[t, l] += dot(wide, mats[n % 2, 0 : panels * len(ks), :])

        fill(0)
        for n in range(len(work)):
            if n + 1 < len(work):
                fill(n + 1)
            apply(n)

    own_couplings()

    def step(c, carry):
        stages = {
            1: [from_row],
            2: [after_first],
            3: [from_column],
            4: [after_second],
            5: [lambda: give(0), rest_of_column],
            7: [lambda: give(1), after_third],
            8: [turn_bases],
        }
        for at, work in stages.items():
            @pl.when(c == at)
            def _():
                for one in work:
                    one()

        own_turn = c < 3
        t = jnp.where(jnp.logical_or(c == 0, c > 6), 1, 2 * lax.rem(c, 2))
        half_turn = jnp.where(c < 7, (c - 3) // 2, c - 7)
        a = (jnp.where(own_turn, 1, 2), jnp.where(own_turn, 0, half_turn))
        b = (jnp.where(own_turn, 1, 0), jnp.where(own_turn, 1, half_turn))
        at_x = x + t - 1

        @pl.when(jnp.logical_and(at_x >= 0, at_x < n_gx))
        def _():
            chunk(t, [a, b])

        return carry

    lax.fori_loop(0, 9, step, 0)

    turned = target[...].astype(F32).T.astype(BF16)
    for k in range(leaf_dev):
        acc[1, k] += dot(turned, by_leaf[k])
        store(k).start()
    for d in sides:
        @pl.when(has(d, x, n_gx))
        def _():
            arrived(res_x, d, 0)
            arrived(res_x, d, 1)

        @pl.when(jnp.logical_not(has(d, x, n_gx)))
        def _():
            absent(d).wait()
    for k in range(leaf_dev):
        store(k).wait()

    for d in sides:
        @pl.when(has(d, x, n_gx))
        def _():
            geo_x(d).wait_send()
            list_x(d).wait_send()
            res_x(d, 0).wait_send()
            res_x(d, 1).wait_send()

        @pl.when(has(d, y, n_gy))
        def _():
            geo_y(d).wait_send()
            src_y(d, 0).wait_send()
            src_y(d, 1).wait_send()
    for k in range(1, n_gy):
        to = lax.rem(y + k, n_gy)
        remote(proj, col_buf.at[y], p1_s.at[k], p1_r.at[y], (x, to)).wait_send()
        remote(int_src, int_buf.at[y], p3_s.at[k], p3_r.at[y], (x, to)).wait_send()
        block_copy(k).wait_send()
    for k in range(1, 4):
        group_copy(k).wait_send()
    for k in range(1, n_gx):
        to = lax.rem(x + k, n_gx)
        remote(row_src, row_buf.at[x], p2_s.at[k], p2_r.at[x], (to, y)).wait_send()


def body(sources, geometry, near_lists, far_lists, bases_in, bases_out, couplings):
    leaf_dev, rhs, panels = sources.shape[2:]
    n_gx, n_gy = lax.axis_size("gx"), lax.axis_size("gy")
    anywhere = pl.BlockSpec(memory_space=pltpu.HBM)
    sems = pltpu.SemaphoreType.DMA
    flat_rows = bases_in.shape[2] * bases_in.shape[3] * leaf_dev
    own, given = pl.pallas_call(
        functools.partial(kernel, n_gx, n_gy),
        out_shape=(
            jax.ShapeDtypeStruct((leaf_dev, rhs, panels), F32),
            jax.ShapeDtypeStruct((2, leaf_dev, rhs, panels), BF16),
        ),
        in_specs=[
            anywhere, anywhere, anywhere, pl.BlockSpec(memory_space=pltpu.SMEM),
            anywhere, anywhere, anywhere,
        ],
        out_specs=(anywhere, anywhere),
        scratch_shapes=[
            pltpu.VMEM(geometry.shape[2:], BF16),
            pltpu.VMEM(near_lists.shape[2:], jnp.int32),
            pltpu.VMEM((3, leaf_dev, rhs, panels), BF16),
            pltpu.VMEM((6, 8 * leaf_dev, panels), BF16),
            pltpu.VMEM((6, 8 * leaf_dev, panels), F32),
            pltpu.VMEM((3, leaf_dev, 128), jnp.int32),
            pltpu.VMEM((27, leaf_dev, panels), F32),
            pltpu.VMEM((3 * leaf_dev, panels, FEATURES), BF16),
            pltpu.VMEM((9 * leaf_dev, FEATURES, panels), BF16),
            pltpu.VMEM((3, leaf_dev, rhs, panels), F32),
            pltpu.VMEM((3, leaf_dev, rhs, panels), BF16),
            pltpu.VMEM((leaf_dev, rhs, panels), BF16),
            pltpu.VMEM((flat_rows, panels), BF16),
            pltpu.VMEM((flat_rows, panels), BF16),
            pltpu.VMEM((panels // 128, flat_rows, 128), F32),
            pltpu.VMEM((leaf_dev, 128, panels), BF16),
            pltpu.VMEM((128, rhs), BF16),
            pltpu.VMEM(couplings.shape[2:], F32),
            pltpu.VMEM((32, 32 * n_gy), F32),
            pltpu.VMEM((64, 32 * n_gx), F32),
            pltpu.VMEM((4, 8, max(128, 8 * n_gx)), F32),
            pltpu.VMEM((n_gy, 8, max(128, 8 * n_gx)), F32),
            pltpu.VMEM((8, max(128, 8 * n_gx)), F32),
            pltpu.VMEM((4, 8, max(128, 8 * n_gx)), F32),
            pltpu.VMEM((2, 3 * panels, panels), BF16),
            pltpu.VMEM((64, 2 * rhs), F32),
            pltpu.VMEM((n_gy, 64, 2 * rhs), F32),
            pltpu.VMEM((48, 2 * rhs), F32),
            pltpu.VMEM((n_gx, 48, 2 * rhs), F32),
            pltpu.VMEM((8 * n_gx, rhs), F32),
            pltpu.VMEM((40, 2 * rhs), F32),
            pltpu.VMEM((n_gy, 40, 2 * rhs), F32),
            sems((6,)), sems((leaf_dev,)), sems((2,)),
            sems((6,)), sems((6,)), sems((3,)), sems((3,)),
            sems((3, 2)), sems((3, 2)), sems((3, 2)), sems((3, 2)),
            sems((n_gy,)), sems((n_gy,)),
            sems((n_gx,)), sems((n_gx,)),
            sems((n_gy,)), sems((n_gy,)),
            sems((n_gy,)), sems((n_gy,)),
            sems((4,)), sems((4,)),
        ],
        compiler_params=pltpu.CompilerParams(
            collective_id=0, has_side_effects=True, vmem_limit_bytes=61440 * 1024
        ),
    )(
        sources[0, 0], geometry[0, 0], near_lists[0, 0], far_lists[0, 0],
        bases_in.reshape(flat_rows, panels), bases_out.reshape(flat_rows, panels),
        couplings[0, 0],
    )
    potential = own + (given[0].astype(F32) + given[1].astype(F32))
    return potential.reshape(sources.shape)


def solution(mesh):
    in_specs = (
        P("gx", "gy", None, None, None),
        P("gx", "gy", None, None, None),
        P("gx", "gy", None, None),
        P("gx", "gy", None, None),
        P("gx", "gy", None, None, None, None),
        P("gx", "gy", None, None, None, None),
        P("gx", "gy", None, None, None),
    )
    out_specs = P("gx", "gy", None, None, None)
    return jax.shard_map(body, mesh=mesh, in_specs=in_specs, out_specs=out_specs, check_vma=False)
```

```python
import functools
import math

import jax
import jax.numpy as jnp
from jax import lax
from jax.experimental import pallas as pl
from jax.experimental.pallas import tpu as pltpu
from jax.sharding import PartitionSpec as P

FOUR_PI = 4.0 * math.pi
MESH = pl.DeviceIdType.MESH
BF16 = jnp.bfloat16
F32 = jnp.float32
FEATURES = 48


def dot(a, b, da=1, db=0):
    return lax.dot_general(a, b, (((da,), (db,)), ((), ())), preferred_element_type=F32)


def rounded(v):
    return v.astype(BF16).astype(F32)


def pieces(v):
    high = rounded(v)
    mid = rounded(v - high)
    return high, mid, rounded(v - high - mid)


def total(terms):
    return functools.reduce(jnp.add, terms)


def kernel(
    n_gx, n_gy, src_in, geo_in, near_in, far, in_in, out_in, coup_in, out, rbuf,
    hsrc, gbuf, gf, lists, weight, sfeat, tfeat, acc, res, zeros,
    base_in, base_out, flat, by_leaf, target, coup, level0, level12, blocks, block_buf, group_src, group_buf,
    mats, proj, col_buf, row_src, row_buf, tab3, int_src, int_buf,
    load, out_s, fill_s, geo_s, geo_r, list_s, list_r, src_s, src_r, res_s, res_r,
    p1_s, p1_r, p2_s, p2_r, p3_s, p3_r,
    block_s, block_r, group_s, group_r,
):
    x = lax.axis_index("gx")
    y = lax.axis_index("gy")
    leaf_dev, rhs, panels = out.shape
    middle = leaf_dev // 2
    first = middle + 1
    barrier = pltpu.get_barrier_semaphore()
    for k in range(1, n_gx):
        pl.semaphore_signal(
            barrier, inc=1, device_id=(lax.rem(x + k, n_gx), y), device_id_type=MESH
        )
    for k in range(1, n_gy):
        pl.semaphore_signal(
            barrier, inc=1, device_id=(x, lax.rem(y + k, n_gy)), device_id_type=MESH
        )

    loads = [
        pltpu.make_async_copy(a, b, load.at[i])
        for i, (a, b) in enumerate(
            [
                (src_in, hsrc.at[1]), (in_in, base_in), (coup_in, coup), (geo_in, gbuf.at[1]), (near_in, lists.at[1]),
                (out_in, base_out),
            ]
        )
    ]
    for one in loads:
        one.start()

    def remote(src, dst, send, recv, where):
        return pltpu.make_async_remote_copy(
            src_ref=src, dst_ref=dst, send_sem=send, recv_sem=recv,
            device_id=where, device_id_type=MESH,
        )

    def has(d, at, n):
        return at > 0 if d < 0 else at < n - 1

    sides = (-1, 1)

    def geo_y(d):
        return remote(geo_in, gbuf.at[1 - d], geo_s.at[1 + d], geo_r.at[1 - d], (x, y + d))

    def geo_x(d):
        return remote(
            geo_in, gbuf.at[4 - d], geo_s.at[4 + d], geo_r.at[4 - d], (x + d, y)
        )

    def list_x(d):
        return remote(near_in, lists.at[1 - d], list_s.at[1 + d], list_r.at[1 - d], (x + d, y))

    def src_y(d, h):
        part = pl.ds(first * h, first if h == 0 else leaf_dev - first)
        return remote(
            src_in.at[part], hsrc.at[1 - d, part],
            src_s.at[1 + d, h], src_r.at[1 - d, h], (x, y + d),
        )

    def res_x(d, h):
        part = pl.ds(middle * h, middle)
        return remote(
            res.at[1 + d, part], rbuf.at[(1 - d) // 2, part],
            res_s.at[1 + d, h], res_r.at[1 - d, h], (x + d, y),
        )

    def absent(d):
        return pltpu.make_async_copy(zeros, rbuf.at[(1 + d) // 2], fill_s.at[(1 + d) // 2])

    def store(k):
        return pltpu.make_async_copy(acc.at[1, k], out.at[k], out_s.at[k])

    def arrived(make, d, h=0):
        if make is geo_y:
            c = remote(gbuf.at[1], gbuf.at[1 + d], geo_s.at[1 + d], geo_r.at[1 + d], (x, y + d))
        elif make is geo_x:
            c = remote(gbuf.at[1], gbuf.at[4 + d], geo_s.at[4 + d], geo_r.at[4 + d], (x + d, y))
        elif make is list_x:
            c = remote(
                lists.at[1], lists.at[1 + d], list_s.at[1 + d], list_r.at[1 + d], (x + d, y)
            )
        elif make is src_y:
            part = pl.ds(first * h, first if h == 0 else leaf_dev - first)
            c = remote(
                hsrc.at[1, part], hsrc.at[1 + d, part],
                src_s.at[1 + d, h], src_r.at[1 + d, h], (x, y + d),
            )
        else:
            part = pl.ds(middle * h, middle)
            c = remote(
                res.at[1 + d, part], rbuf.at[(1 + d) // 2, part],
                res_s.at[1 + d, h], res_r.at[1 + d, h], (x + d, y),
            )
        c.wait_recv()

    def column(src, buf, send, recv):
        for k in range(1, n_gy):
            to = lax.rem(y + k, n_gy)
            remote(src, buf.at[y], send.at[k], recv.at[y], (x, to)).start()
        buf[y] = src[...]

    def column_wait(src, buf, send, recv):
        for k in range(1, n_gy):
            peer = lax.rem(y + k, n_gy)
            remote(src, buf.at[peer], send.at[k], recv.at[peer], (x, peer)).wait_recv()

    row_at = lax.broadcasted_iota(jnp.int32, (8, panels), 0)
    quarter = 4 * (y // 4)
    half = rhs
    base = 4 * (x // 4)
    spot = lax.rem(x, 4)
    mine = lax.rem(y, 4)
    wide3 = 32 * (n_gx // 4)

    def product(a, b):
        a_high, b_high = a.astype(BF16), b.astype(BF16)
        a_low = (a - a_high.astype(F32)).astype(BF16)
        b_low = (b - b_high.astype(F32)).astype(BF16)
        return dot(a_high, b_high) + (dot(a_low, b_high) + dot(a_high, b_low))

    def by_cluster(level, clusters):
        shape = (32, 32 * clusters)
        lane = lax.broadcasted_iota(jnp.int32, shape, 1)
        place = lane >> 5
        same = (lane & 31) == lax.broadcasted_iota(jnp.int32, shape, 0)
        pick = [
            jnp.where(jnp.logical_and(same, place == far[level, m]), 1.0, 0.0).astype(BF16)
            for m in range(16)
        ]
        split = jnp.concatenate(pieces(coup[level]), axis=0).astype(BF16)
        v = dot(split, jnp.concatenate(pick, axis=0))
        return (v[0:32] + v[32:64]) + v[64:96]

    def block_copy(k):
        to = lax.rem(y + k, n_gy)
        return remote(
            blocks.at[lax.rem(to, 4)], block_buf.at[y], block_s.at[k], block_r.at[y], (x, to)
        )

    def group_copy(k):
        to = base + lax.rem(spot + k, 4)
        return remote(group_src, group_buf.at[spot], group_s.at[k], group_r.at[spot], (to, y))

    def gather_couplings():
        v = by_cluster(3, n_gx // 4)
        for b in range(4):
            blocks[b, :, 0 : v.shape[1]] = v[8 * b : 8 * b + 8]

    def give_couplings():
        for k in range(1, n_gy):
            block_copy(k).start()
        block_buf[y] = blocks[mine]

    def own_couplings():
        level0[...] = by_cluster(0, n_gy)
        level12[0:32, :] = by_cluster(1, n_gx)
        level12[32:64, :] = by_cluster(2, n_gx)

    def spread(at):
        raw = gbuf[at].astype(F32)
        raw = jnp.concatenate([raw, jnp.zeros((leaf_dev, 4, panels), F32)], axis=1)
        gf[at] = raw.reshape(8 * leaf_dev, panels)

    def source_features(place):
        shift = lax.convert_element_type(place - 1, F32)

        def leaf(k, carry):
            q = gf[place, pl.ds(pl.multiple_of(8 * k, 8), 8), :]
            q = jnp.where(row_at == 1, q + shift, q)
            area = q[3:4]
            factor = FOUR_PI / area
            factor = factor * factor
            square = q[0:1] * q[0:1] + q[1:2] * q[1:2] + q[2:3] * q[2:3] + area
            one = jnp.where(row_at == 4, 1.0, 0.0)
            v = jnp.where(row_at < 3, q, jnp.where(row_at == 3, square, one)) * factor
            a, b, c = pieces(v)
            wide = jnp.concatenate([a, b, c, a, b, a], axis=0)
            sfeat[place * leaf_dev + k] = wide.T.astype(BF16)
            return carry

        lax.fori_loop(0, leaf_dev, leaf, 0, unroll=4)

    def target_features(side, at):
        def leaf(l, carry):
            p = gf[at, pl.ds(pl.multiple_of(8 * l, 8), 8), :]
            p = jnp.where(row_at == 0, p + float(side), p)
            for dz in (-1, 0, 1):
                t = jnp.where(row_at == 2, p - float(dz), p)
                square = t[0:1] * t[0:1] + t[1:2] * t[1:2] + t[2:3] * t[2:3]
                last = jnp.where(row_at == 4, square, 0.0)
                v = jnp.where(row_at < 3, -2.0 * t, jnp.where(row_at == 3, 1.0, last))
                a, b, c = pieces(v)
                wide = jnp.concatenate([a, a, a, b, b, c], axis=0)
                tfeat[((side + 1) * leaf_dev + l) * 3 + dz + 1] = wide.astype(BF16)
            return carry

        lax.fori_loop(0, leaf_dev, leaf, 0, unroll=4)

    def weights(side):
        mine = lists[side + 1]
        leaf = lax.broadcasted_iota(jnp.int32, mine.shape, 0)
        for s in range(3):
            for dz in (-1, 0, 1):
                n = (x * n_gy + y + s - 1) * leaf_dev + dz + leaf
                there = jnp.logical_and(y + s >= 1, y + s <= n_gy)
                hits = jnp.where(jnp.logical_and(mine == n, there), 1.0, 0.0)
                count = jnp.sum(hits, axis=1, keepdims=True)
                weight[((side + 1) * 3 + s) * 3 + dz + 1] = jnp.broadcast_to(
                    count, (leaf_dev, panels)
                )

    def transposed(source, take):
        wide = source[...].astype(F32)
        for h in range(panels // 128):
            flat[h] = wide[:, 128 * h : 128 * (h + 1)]
        for k in range(leaf_dev):
            take(
                k,
                jnp.concatenate(
                    [
                        flat[h, pl.ds(k, 128, stride=leaf_dev), :]
                        for h in range(panels // 128)
                    ],
                    axis=1,
                ).astype(BF16),
            )

    def projections():
        loads[0].wait()
        loads[1].wait()
        parts = []
        transposed(base_in, lambda k, b: parts.append(dot(b, hsrc[1, k], 1, 1)))
        projection = total(parts)
        proj[:, 0:half] = projection[0:64]
        proj[:, half:] = projection[64:128]

    def own_features():
        loads[3].wait()
        loads[4].wait()
        spread(1)
        source_features(1)
        target_features(0, 1)
        weights(0)
        acc[...] = jnp.zeros_like(acc)

    def couplings():
        loads[2].wait()
        gather_couplings()

    def enter():
        pl.semaphore_wait(barrier, n_gx - 1 + n_gy - 1)

    def send_geometry():
        for d in sides:
            @pl.when(has(d, x, n_gx))
            def _():
                geo_x(d).start()
                list_x(d).start()

            @pl.when(has(d, y, n_gy))
            def _():
                geo_y(d).start()

    def send_sources():
        for d in sides:
            @pl.when(has(d, y, n_gy))
            def _():
                src_y(d, 0).start()
                src_y(d, 1).start()

    def send_projections():
        column(proj, col_buf, p1_s, p1_r)

    projections()
    enter()
    send_geometry()
    send_projections()
    couplings()
    give_couplings()
    send_sources()
    own_features()
    lane = lax.broadcasted_iota(jnp.int32, (panels, FEATURES), 1)
    away = jnp.where(lane == 3, 1.0, 0.0).astype(BF16)
    for d in sides:
        @pl.when(jnp.logical_not(has(d, x, n_gx)))
        def _():
            zeros[...] = jnp.zeros(zeros.shape, BF16)
            absent(d).start()

        @pl.when(jnp.logical_not(has(d, y, n_gy)))
        def _():
            hsrc[1 + d] = jnp.zeros(hsrc.shape[1:], BF16)
            for k in range(leaf_dev):
                sfeat[(1 + d) * leaf_dev + k] = away

    def after_first():
        column_wait(proj, col_buf, p1_s, p1_r)
        row_src[0:32, 0:half] = total([col_buf[quarter + g, 32:64, 0:half] for g in range(4)])
        coarse = total([col_buf[g, :, half:] for g in range(n_gy)])
        row_src[0:32, half:] = coarse[0:32]
        row_src[32:48, 0:half] = coarse[32:48]
        row_src[32:48, half:] = coarse[48:64]
        for k in range(1, n_gx):
            to = lax.rem(x + k, n_gx)
            remote(row_src, row_buf.at[x], p2_s.at[k], p2_r.at[x], (to, y)).start()
        row_buf[x] = row_src[...]
        for k in range(1, n_gy):
            peer = lax.rem(y + k, n_gy)
            remote(
                blocks.at[0], block_buf.at[peer], block_s.at[k], block_r.at[peer], (x, peer)
            ).wait_recv()
        group_src[:, 0:wide3] = total([block_buf[g, :, 0:wide3] for g in range(n_gy)])
        for k in range(1, 4):
            group_copy(k).start()
        group_buf[spot] = group_src[...]
        zero = jnp.concatenate([col_buf[g, 0:32, 0:half] for g in range(n_gy)], axis=0)
        target[0:32, :] = product(level0[...], zero).astype(BF16)

    def after_second():
        for k in range(1, n_gx):
            peer = lax.rem(x + k, n_gx)
            remote(row_src, row_buf.at[peer], p2_s.at[k], p2_r.at[peer], (peer, y)).wait_recv()
        for k in range(1, 4):
            peer = lax.rem(spot + k, 4)
            remote(
                group_src, group_buf.at[peer], group_s.at[k], group_r.at[peer], (base + peer, y)
            ).wait_recv()
        fine = jnp.concatenate([row_buf[g, 0:32] for g in range(n_gx)], axis=0)
        both = product(level12[...], fine)
        int_src[0:32, 0:half] = both[0:32, 0:half]
        int_src[0:32, half:] = both[32:64, half:]
        for c in range(n_gx // 4):
            coarse = total([row_buf[4 * c + g, 32:48, :] for g in range(4)])
            tab3[32 * c : 32 * c + 16, :] = coarse[:, 0:half]
            tab3[32 * c + 16 : 32 * c + 32, :] = coarse[:, half:]
        third = total([group_buf[g, :, 0:wide3] for g in range(4)])
        int_src[32:40, 0:half] = product(third, tab3[...])
        int_src[32:40, half:] = jnp.zeros((8, half), F32)
        column(int_src, int_buf, p3_s, p3_r)

    def after_third():
        column_wait(int_src, int_buf, p3_s, p3_r)
        target[32:64, :] = total([int_buf[quarter + g, 0:32, 0:half] for g in range(4)]).astype(BF16)
        target[64:96, :] = total([int_buf[g, 0:32, half:] for g in range(n_gy)]).astype(BF16)
        third = [int_buf[quarter + b, 32:40, 0:half] for b in range(4)]
        target[96:128, :] = jnp.concatenate(third, axis=0).astype(BF16)

    def turn_bases():
        loads[5].wait()

        def take(k, b):
            by_leaf[k] = b

        transposed(base_out, take)

    def from_row():
        for d in sides:
            @pl.when(has(d, x, n_gx))
            def _():
                arrived(geo_x, d)
                arrived(list_x, d)
                spread(4 + d)
                target_features(d, 4 + d)
                weights(d)

    def from_column():
        for d in sides:
            @pl.when(has(d, y, n_gy))
            def _():
                arrived(geo_y, d)
                spread(1 + d)
                source_features(1 + d)
                arrived(src_y, d, 0)

    def rest_of_column():
        for d in sides:
            @pl.when(has(d, y, n_gy))
            def _():
                arrived(src_y, d, 1)

    outer = 2 * lax.rem(x, 2)

    def give(t, h):
        @pl.when(jnp.logical_and(x + t >= 1, x + t <= n_gx))
        def _():
            part = pl.ds(middle * h, middle)
            res[t, part] = acc[t, part].astype(BF16)
            res_x(t - 1, h).start()

    def chunk(t, halves):
        work = [(s, h, i) for s, h in halves for i in range(middle)]

        def leaves(h, i):
            sign = 1 - 2 * h
            l = (leaf_dev - 1) * h + sign * i
            return l, [(l + sign * e, sign * e) for e in (-1, 0, 1) if i + e >= 0]

        def fill(n):
            s, h, i = work[n]
            l, ks = leaves(h, i)
            for at, (k, dz) in enumerate(ks):
                squared = dot(sfeat[s * leaf_dev + k], tfeat[(t * leaf_dev + l) * 3 + dz + 1])
                w = weight[(t * 3 + s) * 3 + dz + 1, pl.ds(l, 1), :]
                mats[n % 2, panels * at : panels * (at + 1), :] = (
                    lax.rsqrt(squared) * w
                ).astype(BF16)

        def apply(n):
            s, h, i = work[n]
            l, ks = leaves(h, i)
            wide = jnp.concatenate([hsrc[s, k] for k, _ in ks], axis=1)
            acc[t, l] += dot(wide, mats[n % 2, 0 : panels * len(ks), :])

        fill(0)
        for n in range(len(work)):
            if n + 1 < len(work):
                fill(n + 1)
            apply(n)

    own_couplings()

    def step(c, carry):
        stages = {
            1: [from_row],
            2: [after_first],
            3: [turn_bases, from_column],
            4: [lambda: give(outer, 0), after_second, rest_of_column],
            5: [lambda: give(outer, 1)],
            6: [lambda: give(2 - outer, 0)],
            7: [lambda: give(2 - outer, 1)],

        }
        for at, work in stages.items():
            @pl.when(c == at)
            def _():
                for one in work:
                    one()

        own_turn = c < 3
        other = jnp.where(jnp.logical_or(c == 1, jnp.logical_or(c == 3, c == 4)), outer, 2 - outer)
        t = jnp.where(jnp.logical_or(c == 0, c > 6), 1, other)
        half_turn = lax.rem(c + 1, 2)
        a = (jnp.where(own_turn, 1, 2), jnp.where(own_turn, 0, half_turn))
        b = (jnp.where(own_turn, 1, 0), jnp.where(own_turn, 1, half_turn))
        at_x = x + t - 1

        @pl.when(jnp.logical_and(at_x >= 0, at_x < n_gx))
        def _():
            chunk(t, [a, b])

        return carry

    lax.fori_loop(0, 9, step, 0)

    after_third()
    turned = target[...].astype(F32).T.astype(BF16)
    for k in range(leaf_dev):
        acc[1, k] += dot(turned, by_leaf[k])
        store(k).start()
    for d in sides:
        @pl.when(has(d, x, n_gx))
        def _():
            arrived(res_x, d, 0)
            arrived(res_x, d, 1)

        @pl.when(jnp.logical_not(has(d, x, n_gx)))
        def _():
            absent(d).wait()
    for k in range(leaf_dev):
        store(k).wait()

    for d in sides:
        @pl.when(has(d, x, n_gx))
        def _():
            geo_x(d).wait_send()
            list_x(d).wait_send()
            res_x(d, 0).wait_send()
            res_x(d, 1).wait_send()

        @pl.when(has(d, y, n_gy))
        def _():
            geo_y(d).wait_send()
            src_y(d, 0).wait_send()
            src_y(d, 1).wait_send()
    for k in range(1, n_gy):
        to = lax.rem(y + k, n_gy)
        remote(proj, col_buf.at[y], p1_s.at[k], p1_r.at[y], (x, to)).wait_send()
        remote(int_src, int_buf.at[y], p3_s.at[k], p3_r.at[y], (x, to)).wait_send()
        block_copy(k).wait_send()
    for k in range(1, 4):
        group_copy(k).wait_send()
    for k in range(1, n_gx):
        to = lax.rem(x + k, n_gx)
        remote(row_src, row_buf.at[x], p2_s.at[k], p2_r.at[x], (to, y)).wait_send()


def body(sources, geometry, near_lists, far_lists, bases_in, bases_out, couplings):
    leaf_dev, rhs, panels = sources.shape[2:]
    n_gx, n_gy = lax.axis_size("gx"), lax.axis_size("gy")
    anywhere = pl.BlockSpec(memory_space=pltpu.HBM)
    sems = pltpu.SemaphoreType.DMA
    flat_rows = bases_in.shape[2] * bases_in.shape[3] * leaf_dev
    own, given = pl.pallas_call(
        functools.partial(kernel, n_gx, n_gy),
        out_shape=(
            jax.ShapeDtypeStruct((leaf_dev, rhs, panels), F32),
            jax.ShapeDtypeStruct((2, leaf_dev, rhs, panels), BF16),
        ),
        in_specs=[
            anywhere, anywhere, anywhere, pl.BlockSpec(memory_space=pltpu.SMEM),
            anywhere, anywhere, anywhere,
        ],
        out_specs=(anywhere, anywhere),
        scratch_shapes=[
            pltpu.VMEM((3, leaf_dev, rhs, panels), BF16),
            pltpu.VMEM((6,) + geometry.shape[2:], BF16),
            pltpu.VMEM((6, 8 * leaf_dev, panels), F32),
            pltpu.VMEM((3,) + near_lists.shape[2:], jnp.int32),
            pltpu.VMEM((27, leaf_dev, panels), F32),
            pltpu.VMEM((3 * leaf_dev, panels, FEATURES), BF16),
            pltpu.VMEM((9 * leaf_dev, FEATURES, panels), BF16),
            pltpu.VMEM((3, leaf_dev, rhs, panels), F32),
            pltpu.VMEM((3, leaf_dev, rhs, panels), BF16),
            pltpu.VMEM((leaf_dev, rhs, panels), BF16),
            pltpu.VMEM((flat_rows, panels), BF16),
            pltpu.VMEM((flat_rows, panels), BF16),
            pltpu.VMEM((panels // 128, flat_rows, 128), F32),
            pltpu.VMEM((leaf_dev, 128, panels), BF16),
            pltpu.VMEM((128, rhs), BF16),
            pltpu.VMEM(couplings.shape[2:], F32),
            pltpu.VMEM((32, 32 * n_gy), F32),
            pltpu.VMEM((64, 32 * n_gx), F32),
            pltpu.VMEM((4, 8, max(128, 8 * n_gx)), F32),
            pltpu.VMEM((n_gy, 8, max(128, 8 * n_gx)), F32),
            pltpu.VMEM((8, max(128, 8 * n_gx)), F32),
            pltpu.VMEM((4, 8, max(128, 8 * n_gx)), F32),
            pltpu.VMEM((2, 3 * panels, panels), BF16),
            pltpu.VMEM((64, 2 * rhs), F32),
            pltpu.VMEM((n_gy, 64, 2 * rhs), F32),
            pltpu.VMEM((48, 2 * rhs), F32),
            pltpu.VMEM((n_gx, 48, 2 * rhs), F32),
            pltpu.VMEM((8 * n_gx, rhs), F32),
            pltpu.VMEM((40, 2 * rhs), F32),
            pltpu.VMEM((n_gy, 40, 2 * rhs), F32),
            sems((6,)), sems((leaf_dev,)), sems((2,)),
            sems((6,)), sems((6,)), sems((3,)), sems((3,)),
            sems((3, 2)), sems((3, 2)), sems((3, 2)), sems((3, 2)),
            sems((n_gy,)), sems((n_gy,)),
            sems((n_gx,)), sems((n_gx,)),
            sems((n_gy,)), sems((n_gy,)),
            sems((n_gy,)), sems((n_gy,)),
            sems((4,)), sems((4,)),
        ],
        compiler_params=pltpu.CompilerParams(
            collective_id=0, has_side_effects=True, vmem_limit_bytes=61440 * 1024
        ),
    )(
        sources[0, 0], geometry[0, 0], near_lists[0, 0], far_lists[0, 0],
        bases_in.reshape(flat_rows, panels), bases_out.reshape(flat_rows, panels),
        couplings[0, 0],
    )
    potential = own + (given[0].astype(F32) + given[1].astype(F32))
    return potential.reshape(sources.shape)


def solution(mesh):
    in_specs = (
        P("gx", "gy", None, None, None),
        P("gx", "gy", None, None, None),
        P("gx", "gy", None, None),
        P("gx", "gy", None, None),
        P("gx", "gy", None, None, None, None),
        P("gx", "gy", None, None, None, None),
        P("gx", "gy", None, None, None),
    )
    out_specs = P("gx", "gy", None, None, None)
    return jax.shard_map(body, mesh=mesh, in_specs=in_specs, out_specs=out_specs, check_vma=False)
```

```python
import functools
import math

import jax
import jax.numpy as jnp
from jax import lax
from jax.experimental import pallas as pl
from jax.experimental.pallas import tpu as pltpu
from jax.sharding import PartitionSpec as P

FOUR_PI = 4.0 * math.pi
MESH = pl.DeviceIdType.MESH
BF16 = jnp.bfloat16
F32 = jnp.float32
FEATURES = 48


def dot(a, b, da=1, db=0):
    return lax.dot_general(a, b, (((da,), (db,)), ((), ())), preferred_element_type=F32)


def rounded(v):
    return v.astype(BF16).astype(F32)


def pieces(v):
    high = rounded(v)
    mid = rounded(v - high)
    return high, mid, rounded(v - high - mid)


def total(terms):
    return functools.reduce(jnp.add, terms)


def kernel(
    n_gx, n_gy, src_in, geo_in, near_in, far, in_in, out_in, coup_in, out, rbuf,
    hsrc, gbuf, gf, lists, weight, sfeat, tfeat, acc, res, zeros,
    base_in, base_out, flat, by_leaf, target, coup, level0, level12, blocks, block_buf, group_src, group_buf,
    mats, proj, col_buf, row_src, row_buf, tab3, int_src, int_buf,
    load, out_s, fill_s, geo_s, geo_r, list_s, list_r, src_s, src_r, res_s, res_r,
    p1_s, p1_r, p2_s, p2_r, p3_s, p3_r,
    block_s, block_r, group_s, group_r,
):
    x = lax.axis_index("gx")
    y = lax.axis_index("gy")
    leaf_dev, rhs, panels = out.shape
    middle = leaf_dev // 2
    first = middle + 1
    barrier = pltpu.get_barrier_semaphore()
    for k in range(1, n_gx):
        pl.semaphore_signal(
            barrier, inc=1, device_id=(lax.rem(x + k, n_gx), y), device_id_type=MESH
        )
    for k in range(1, n_gy):
        pl.semaphore_signal(
            barrier, inc=1, device_id=(x, lax.rem(y + k, n_gy)), device_id_type=MESH
        )

    loads = [
        pltpu.make_async_copy(a, b, load.at[i])
        for i, (a, b) in enumerate(
            [
                (src_in, hsrc.at[1]), (in_in, base_in), (coup_in, coup), (geo_in, gbuf.at[1]), (near_in, lists.at[1]),
                (out_in, base_out),
            ]
        )
    ]
    for one in loads:
        one.start()
    acc[...] = jnp.zeros_like(acc)

    def remote(src, dst, send, recv, where):
        return pltpu.make_async_remote_copy(
            src_ref=src, dst_ref=dst, send_sem=send, recv_sem=recv,
            device_id=where, device_id_type=MESH,
        )

    def has(d, at, n):
        return at > 0 if d < 0 else at < n - 1

    sides = (-1, 1)

    def geo_y(d):
        return remote(geo_in, gbuf.at[1 - d], geo_s.at[1 + d], geo_r.at[1 - d], (x, y + d))

    def geo_x(d):
        return remote(
            geo_in, gbuf.at[4 - d], geo_s.at[4 + d], geo_r.at[4 - d], (x + d, y)
        )

    def list_x(d):
        return remote(near_in, lists.at[1 - d], list_s.at[1 + d], list_r.at[1 - d], (x + d, y))

    def src_y(d, h):
        part = pl.ds(first * h, first if h == 0 else leaf_dev - first)
        return remote(
            src_in.at[part], hsrc.at[1 - d, part],
            src_s.at[1 + d, h], src_r.at[1 - d, h], (x, y + d),
        )

    def res_x(d, h):
        part = pl.ds(middle * h, middle)
        return remote(
            res.at[1 + d, part], rbuf.at[(1 - d) // 2, part],
            res_s.at[1 + d, h], res_r.at[1 - d, h], (x + d, y),
        )

    def absent(d):
        return pltpu.make_async_copy(zeros, rbuf.at[(1 + d) // 2], fill_s.at[(1 + d) // 2])

    def store(k):
        return pltpu.make_async_copy(acc.at[1, k], out.at[k], out_s.at[k])

    def arrived(make, d, h=0):
        if make is geo_y:
            c = remote(gbuf.at[1], gbuf.at[1 + d], geo_s.at[1 + d], geo_r.at[1 + d], (x, y + d))
        elif make is geo_x:
            c = remote(gbuf.at[1], gbuf.at[4 + d], geo_s.at[4 + d], geo_r.at[4 + d], (x + d, y))
        elif make is list_x:
            c = remote(
                lists.at[1], lists.at[1 + d], list_s.at[1 + d], list_r.at[1 + d], (x + d, y)
            )
        elif make is src_y:
            part = pl.ds(first * h, first if h == 0 else leaf_dev - first)
            c = remote(
                hsrc.at[1, part], hsrc.at[1 + d, part],
                src_s.at[1 + d, h], src_r.at[1 + d, h], (x, y + d),
            )
        else:
            part = pl.ds(middle * h, middle)
            c = remote(
                res.at[1 + d, part], rbuf.at[(1 + d) // 2, part],
                res_s.at[1 + d, h], res_r.at[1 + d, h], (x + d, y),
            )
        c.wait_recv()

    def column(src, buf, send, recv):
        for k in range(1, n_gy):
            to = lax.rem(y + k, n_gy)
            remote(src, buf.at[y], send.at[k], recv.at[y], (x, to)).start()
        buf[y] = src[...]

    def column_wait(src, buf, send, recv):
        for k in range(1, n_gy):
            peer = lax.rem(y + k, n_gy)
            remote(src, buf.at[peer], send.at[k], recv.at[peer], (x, peer)).wait_recv()

    row_at = lax.broadcasted_iota(jnp.int32, (8, panels), 0)
    quarter = 4 * (y // 4)
    half = rhs
    base = 4 * (x // 4)
    spot = lax.rem(x, 4)
    mine = lax.rem(y, 4)
    wide3 = 32 * (n_gx // 4)

    def product(a, b):
        a_high, b_high = a.astype(BF16), b.astype(BF16)
        a_low = (a - a_high.astype(F32)).astype(BF16)
        b_low = (b - b_high.astype(F32)).astype(BF16)
        return dot(a_high, b_high) + (dot(a_low, b_high) + dot(a_high, b_low))

    def by_cluster(level, clusters):
        shape = (32, 32 * clusters)
        lane = lax.broadcasted_iota(jnp.int32, shape, 1)
        place = lane >> 5
        same = (lane & 31) == lax.broadcasted_iota(jnp.int32, shape, 0)
        pick = [
            jnp.where(jnp.logical_and(same, place == far[level, m]), 1.0, 0.0).astype(BF16)
            for m in range(16)
        ]
        split = jnp.concatenate(pieces(coup[level]), axis=0).astype(BF16)
        v = dot(split, jnp.concatenate(pick, axis=0))
        return (v[0:32] + v[32:64]) + v[64:96]

    def block_copy(k):
        to = lax.rem(y + k, n_gy)
        return remote(
            blocks.at[lax.rem(to, 4)], block_buf.at[y], block_s.at[k], block_r.at[y], (x, to)
        )

    def group_copy(k):
        to = base + lax.rem(spot + k, 4)
        return remote(group_src, group_buf.at[spot], group_s.at[k], group_r.at[spot], (to, y))

    def gather_couplings():
        v = by_cluster(3, n_gx // 4)
        for b in range(4):
            blocks[b, :, 0 : v.shape[1]] = v[8 * b : 8 * b + 8]

    def give_couplings():
        for k in range(1, n_gy):
            block_copy(k).start()
        block_buf[y] = blocks[mine]

    def own_couplings():
        level0[...] = by_cluster(0, n_gy)
        level12[0:32, :] = by_cluster(1, n_gx)
        level12[32:64, :] = by_cluster(2, n_gx)

    def spread(at):
        raw = gbuf[at].astype(F32)
        raw = jnp.concatenate([raw, jnp.zeros((leaf_dev, 4, panels), F32)], axis=1)
        gf[at] = raw.reshape(8 * leaf_dev, panels)

    def source_features(place):
        shift = lax.convert_element_type(place - 1, F32)

        def leaf(k, carry):
            q = gf[place, pl.ds(pl.multiple_of(8 * k, 8), 8), :]
            q = jnp.where(row_at == 1, q + shift, q)
            area = q[3:4]
            factor = FOUR_PI / area
            factor = factor * factor
            square = q[0:1] * q[0:1] + q[1:2] * q[1:2] + q[2:3] * q[2:3] + area
            one = jnp.where(row_at == 4, 1.0, 0.0)
            v = jnp.where(row_at < 3, q, jnp.where(row_at == 3, square, one)) * factor
            a, b, c = pieces(v)
            wide = jnp.concatenate([a, b, c, a, b, a], axis=0)
            sfeat[place * leaf_dev + k] = wide.T.astype(BF16)
            return carry

        lax.fori_loop(0, leaf_dev, leaf, 0, unroll=8)

    def target_features(side, at):
        def leaf(l, carry):
            p = gf[at, pl.ds(pl.multiple_of(8 * l, 8), 8), :]
            p = jnp.where(row_at == 0, p + float(side), p)
            for dz in (-1, 0, 1):
                t = jnp.where(row_at == 2, p - float(dz), p)
                square = t[0:1] * t[0:1] + t[1:2] * t[1:2] + t[2:3] * t[2:3]
                last = jnp.where(row_at == 4, square, 0.0)
                v = jnp.where(row_at < 3, -2.0 * t, jnp.where(row_at == 3, 1.0, last))
                a, b, c = pieces(v)
                wide = jnp.concatenate([a, a, a, b, b, c], axis=0)
                tfeat[((side + 1) * leaf_dev + l) * 3 + dz + 1] = wide.astype(BF16)
            return carry

        lax.fori_loop(0, leaf_dev, leaf, 0, unroll=8)

    def weights(side):
        mine = lists[side + 1]
        leaf = lax.broadcasted_iota(jnp.int32, mine.shape, 0)
        for s in range(3):
            for dz in (-1, 0, 1):
                n = (x * n_gy + y + s - 1) * leaf_dev + dz + leaf
                there = jnp.logical_and(y + s >= 1, y + s <= n_gy)
                hits = jnp.where(jnp.logical_and(mine == n, there), 1.0, 0.0)
                count = jnp.sum(hits, axis=1, keepdims=True)
                weight[((side + 1) * 3 + s) * 3 + dz + 1] = jnp.broadcast_to(
                    count, (leaf_dev, panels)
                )

    def transposed(source, take):
        wide = source[...].astype(F32)
        for h in range(panels // 128):
            flat[h] = wide[:, 128 * h : 128 * (h + 1)]
        for k in range(leaf_dev):
            take(
                k,
                jnp.concatenate(
                    [
                        flat[h, pl.ds(k, 128, stride=leaf_dev), :]
                        for h in range(panels // 128)
                    ],
                    axis=1,
                ).astype(BF16),
            )

    def projections():
        loads[0].wait()
        loads[1].wait()
        parts = []
        transposed(base_in, lambda k, b: parts.append(dot(b, hsrc[1, k], 1, 1)))
        projection = total(parts)
        proj[:, 0:half] = projection[0:64]
        proj[:, half:] = projection[64:128]

    def own_features():
        loads[3].wait()
        loads[4].wait()
        spread(1)
        source_features(1)
        target_features(0, 1)
        weights(0)

    def couplings():
        loads[2].wait()
        gather_couplings()

    def enter():
        pl.semaphore_wait(barrier, n_gx - 1 + n_gy - 1)

    def send_geometry():
        for d in sides:
            @pl.when(has(d, x, n_gx))
            def _():
                geo_x(d).start()
                list_x(d).start()

            @pl.when(has(d, y, n_gy))
            def _():
                geo_y(d).start()

    def send_sources():
        for d in sides:
            @pl.when(has(d, y, n_gy))
            def _():
                src_y(d, 0).start()
                src_y(d, 1).start()

    def send_projections():
        column(proj, col_buf, p1_s, p1_r)

    projections()
    enter()
    send_geometry()
    send_projections()
    couplings()
    give_couplings()
    send_sources()
    own_features()
    lane = lax.broadcasted_iota(jnp.int32, (panels, FEATURES), 1)
    away = jnp.where(lane == 3, 1.0, 0.0).astype(BF16)
    for d in sides:
        @pl.when(jnp.logical_not(has(d, x, n_gx)))
        def _():
            zeros[...] = jnp.zeros(zeros.shape, BF16)
            absent(d).start()

        @pl.when(jnp.logical_not(has(d, y, n_gy)))
        def _():
            hsrc[1 + d] = jnp.zeros(hsrc.shape[1:], BF16)
            for k in range(leaf_dev):
                sfeat[(1 + d) * leaf_dev + k] = away

    def after_first():
        column_wait(proj, col_buf, p1_s, p1_r)
        row_src[0:32, 0:half] = total([col_buf[quarter + g, 32:64, 0:half] for g in range(4)])
        coarse = total([col_buf[g, :, half:] for g in range(n_gy)])
        row_src[0:32, half:] = coarse[0:32]
        row_src[32:48, 0:half] = coarse[32:48]
        row_src[32:48, half:] = coarse[48:64]
        for k in range(1, n_gx):
            to = lax.rem(x + k, n_gx)
            remote(row_src, row_buf.at[x], p2_s.at[k], p2_r.at[x], (to, y)).start()
        row_buf[x] = row_src[...]
        for k in range(1, n_gy):
            peer = lax.rem(y + k, n_gy)
            remote(
                blocks.at[0], block_buf.at[peer], block_s.at[k], block_r.at[peer], (x, peer)
            ).wait_recv()
        group_src[:, 0:wide3] = total([block_buf[g, :, 0:wide3] for g in range(n_gy)])
        for k in range(1, 4):
            group_copy(k).start()
        group_buf[spot] = group_src[...]
        zero = jnp.concatenate([col_buf[g, 0:32, 0:half] for g in range(n_gy)], axis=0)
        target[0:32, :] = product(level0[...], zero).astype(BF16)

    def after_second():
        for k in range(1, n_gx):
            peer = lax.rem(x + k, n_gx)
            remote(row_src, row_buf.at[peer], p2_s.at[k], p2_r.at[peer], (peer, y)).wait_recv()
        for k in range(1, 4):
            peer = lax.rem(spot + k, 4)
            remote(
                group_src, group_buf.at[peer], group_s.at[k], group_r.at[peer], (base + peer, y)
            ).wait_recv()
        fine = jnp.concatenate([row_buf[g, 0:32] for g in range(n_gx)], axis=0)
        both = product(level12[...], fine)
        int_src[0:32, 0:half] = both[0:32, 0:half]
        int_src[0:32, half:] = both[32:64, half:]
        for c in range(n_gx // 4):
            coarse = total([row_buf[4 * c + g, 32:48, :] for g in range(4)])
            tab3[32 * c : 32 * c + 16, :] = coarse[:, 0:half]
            tab3[32 * c + 16 : 32 * c + 32, :] = coarse[:, half:]
        third = total([group_buf[g, :, 0:wide3] for g in range(4)])
        int_src[32:40, 0:half] = product(third, tab3[...])
        int_src[32:40, half:] = jnp.zeros((8, half), F32)
        column(int_src, int_buf, p3_s, p3_r)

    def after_third():
        column_wait(int_src, int_buf, p3_s, p3_r)
        target[32:64, :] = total([int_buf[quarter + g, 0:32, 0:half] for g in range(4)]).astype(BF16)
        target[64:96, :] = total([int_buf[g, 0:32, half:] for g in range(n_gy)]).astype(BF16)
        third = [int_buf[quarter + b, 32:40, 0:half] for b in range(4)]
        target[96:128, :] = jnp.concatenate(third, axis=0).astype(BF16)

    def turn_bases():
        loads[5].wait()

        def take(k, b):
            by_leaf[k] = b

        transposed(base_out, take)

    def from_row():
        for d in sides:
            @pl.when(has(d, x, n_gx))
            def _():
                arrived(geo_x, d)
                arrived(list_x, d)
                spread(4 + d)
                target_features(d, 4 + d)
                weights(d)

    def from_column():
        for d in sides:
            @pl.when(has(d, y, n_gy))
            def _():
                arrived(geo_y, d)
                spread(1 + d)
                source_features(1 + d)
                arrived(src_y, d, 0)

    def rest_of_column():
        for d in sides:
            @pl.when(has(d, y, n_gy))
            def _():
                arrived(src_y, d, 1)

    outer = 2 * lax.rem(x, 2)

    def give(t, h):
        @pl.when(jnp.logical_and(x + t >= 1, x + t <= n_gx))
        def _():
            part = pl.ds(middle * h, middle)
            res[t, part] = acc[t, part].astype(BF16)
            res_x(t - 1, h).start()

    def chunk(t, halves):
        work = [(s, h, i) for s, h in halves for i in range(middle)]

        def leaves(h, i):
            sign = 1 - 2 * h
            l = (leaf_dev - 1) * h + sign * i
            return l, [(l + sign * e, sign * e) for e in (-1, 0, 1) if i + e >= 0]

        def fill(n):
            s, h, i = work[n]
            l, ks = leaves(h, i)
            for at, (k, dz) in enumerate(ks):
                squared = dot(sfeat[s * leaf_dev + k], tfeat[(t * leaf_dev + l) * 3 + dz + 1])
                w = weight[(t * 3 + s) * 3 + dz + 1, pl.ds(l, 1), :]
                mats[n % 2, panels * at : panels * (at + 1), :] = (
                    lax.rsqrt(squared) * w
                ).astype(BF16)

        def apply(n):
            s, h, i = work[n]
            l, ks = leaves(h, i)
            wide = jnp.concatenate([hsrc[s, k] for k, _ in ks], axis=1)
            acc[t, l] += dot(wide, mats[n % 2, 0 : panels * len(ks), :])

        fill(0)
        for n in range(len(work)):
            if n + 1 < len(work):
                fill(n + 1)
            apply(n)

    own_couplings()

    def step(c, carry):
        stages = {
            1: [from_row],
            2: [after_first],
            3: [turn_bases, from_column],
            4: [lambda: give(outer, 0)],
            5: [lambda: give(2 - outer, 0), rest_of_column, after_second],
            6: [lambda: give(outer, 1)],
            7: [lambda: give(2 - outer, 1)],

        }
        for at, work in stages.items():
            @pl.when(c == at)
            def _():
                for one in work:
                    one()

        own_turn = c < 3
        other = jnp.where(lax.rem(c, 2) == 1, outer, 2 - outer)
        t = jnp.where(jnp.logical_or(c == 0, c > 6), 1, other)
        half_turn = jnp.where(c < 7, (c - 3) // 2, c - 7)
        a = (jnp.where(own_turn, 1, 2), jnp.where(own_turn, 0, half_turn))
        b = (jnp.where(own_turn, 1, 0), jnp.where(own_turn, 1, half_turn))
        at_x = x + t - 1

        @pl.when(jnp.logical_and(at_x >= 0, at_x < n_gx))
        def _():
            chunk(t, [a, b])

        return carry

    lax.fori_loop(0, 9, step, 0)

    after_third()
    turned = target[...].astype(F32).T.astype(BF16)
    for k in range(leaf_dev):
        acc[1, k] += dot(turned, by_leaf[k])
        store(k).start()
    for d in sides:
        @pl.when(has(d, x, n_gx))
        def _():
            arrived(res_x, d, 0)
            arrived(res_x, d, 1)

        @pl.when(jnp.logical_not(has(d, x, n_gx)))
        def _():
            absent(d).wait()
    for k in range(leaf_dev):
        store(k).wait()

    for d in sides:
        @pl.when(has(d, x, n_gx))
        def _():
            geo_x(d).wait_send()
            list_x(d).wait_send()
            res_x(d, 0).wait_send()
            res_x(d, 1).wait_send()

        @pl.when(has(d, y, n_gy))
        def _():
            geo_y(d).wait_send()
            src_y(d, 0).wait_send()
            src_y(d, 1).wait_send()
    for k in range(1, n_gy):
        to = lax.rem(y + k, n_gy)
        remote(proj, col_buf.at[y], p1_s.at[k], p1_r.at[y], (x, to)).wait_send()
        remote(int_src, int_buf.at[y], p3_s.at[k], p3_r.at[y], (x, to)).wait_send()
        block_copy(k).wait_send()
    for k in range(1, 4):
        group_copy(k).wait_send()
    for k in range(1, n_gx):
        to = lax.rem(x + k, n_gx)
        remote(row_src, row_buf.at[x], p2_s.at[k], p2_r.at[x], (to, y)).wait_send()


def body(sources, geometry, near_lists, far_lists, bases_in, bases_out, couplings):
    leaf_dev, rhs, panels = sources.shape[2:]
    n_gx, n_gy = lax.axis_size("gx"), lax.axis_size("gy")
    anywhere = pl.BlockSpec(memory_space=pltpu.HBM)
    sems = pltpu.SemaphoreType.DMA
    flat_rows = bases_in.shape[2] * bases_in.shape[3] * leaf_dev
    own, given = pl.pallas_call(
        functools.partial(kernel, n_gx, n_gy),
        out_shape=(
            jax.ShapeDtypeStruct((leaf_dev, rhs, panels), F32),
            jax.ShapeDtypeStruct((2, leaf_dev, rhs, panels), BF16),
        ),
        in_specs=[
            anywhere, anywhere, anywhere, pl.BlockSpec(memory_space=pltpu.SMEM),
            anywhere, anywhere, anywhere,
        ],
        out_specs=(anywhere, anywhere),
        scratch_shapes=[
            pltpu.VMEM((3, leaf_dev, rhs, panels), BF16),
            pltpu.VMEM((6,) + geometry.shape[2:], BF16),
            pltpu.VMEM((6, 8 * leaf_dev, panels), F32),
            pltpu.VMEM((3,) + near_lists.shape[2:], jnp.int32),
            pltpu.VMEM((27, leaf_dev, panels), F32),
            pltpu.VMEM((3 * leaf_dev, panels, FEATURES), BF16),
            pltpu.VMEM((9 * leaf_dev, FEATURES, panels), BF16),
            pltpu.VMEM((3, leaf_dev, rhs, panels), F32),
            pltpu.VMEM((3, leaf_dev, rhs, panels), BF16),
            pltpu.VMEM((leaf_dev, rhs, panels), BF16),
            pltpu.VMEM((flat_rows, panels), BF16),
            pltpu.VMEM((flat_rows, panels), BF16),
            pltpu.VMEM((panels // 128, flat_rows, 128), F32),
            pltpu.VMEM((leaf_dev, 128, panels), BF16),
            pltpu.VMEM((128, rhs), BF16),
            pltpu.VMEM(couplings.shape[2:], F32),
            pltpu.VMEM((32, 32 * n_gy), F32),
            pltpu.VMEM((64, 32 * n_gx), F32),
            pltpu.VMEM((4, 8, max(128, 8 * n_gx)), F32),
            pltpu.VMEM((n_gy, 8, max(128, 8 * n_gx)), F32),
            pltpu.VMEM((8, max(128, 8 * n_gx)), F32),
            pltpu.VMEM((4, 8, max(128, 8 * n_gx)), F32),
            pltpu.VMEM((2, 3 * panels, panels), BF16),
            pltpu.VMEM((64, 2 * rhs), F32),
            pltpu.VMEM((n_gy, 64, 2 * rhs), F32),
            pltpu.VMEM((48, 2 * rhs), F32),
            pltpu.VMEM((n_gx, 48, 2 * rhs), F32),
            pltpu.VMEM((8 * n_gx, rhs), F32),
            pltpu.VMEM((40, 2 * rhs), F32),
            pltpu.VMEM((n_gy, 40, 2 * rhs), F32),
            sems((6,)), sems((leaf_dev,)), sems((2,)),
            sems((6,)), sems((6,)), sems((3,)), sems((3,)),
            sems((3, 2)), sems((3, 2)), sems((3, 2)), sems((3, 2)),
            sems((n_gy,)), sems((n_gy,)),
            sems((n_gx,)), sems((n_gx,)),
            sems((n_gy,)), sems((n_gy,)),
            sems((n_gy,)), sems((n_gy,)),
            sems((4,)), sems((4,)),
        ],
        compiler_params=pltpu.CompilerParams(
            collective_id=0, has_side_effects=True, vmem_limit_bytes=61440 * 1024
        ),
    )(
        sources[0, 0], geometry[0, 0], near_lists[0, 0], far_lists[0, 0],
        bases_in.reshape(flat_rows, panels), bases_out.reshape(flat_rows, panels),
        couplings[0, 0],
    )
    potential = own + (given[0].astype(F32) + given[1].astype(F32))
    return potential.reshape(sources.shape)


def solution(mesh):
    in_specs = (
        P("gx", "gy", None, None, None),
        P("gx", "gy", None, None, None),
        P("gx", "gy", None, None),
        P("gx", "gy", None, None),
        P("gx", "gy", None, None, None, None),
        P("gx", "gy", None, None, None, None),
        P("gx", "gy", None, None, None),
    )
    out_specs = P("gx", "gy", None, None, None)
    return jax.shard_map(body, mesh=mesh, in_specs=in_specs, out_specs=out_specs, check_vma=False)
```

```python
import functools
import math

import jax
import jax.numpy as jnp
from jax import lax
from jax.experimental import pallas as pl
from jax.experimental.pallas import tpu as pltpu
from jax.sharding import PartitionSpec as P

FOUR_PI = 4.0 * math.pi
MESH = pl.DeviceIdType.MESH
BF16 = jnp.bfloat16
F32 = jnp.float32
FEATURES = 48


def dot(a, b, da=1, db=0):
    return lax.dot_general(a, b, (((da,), (db,)), ((), ())), preferred_element_type=F32)


def rounded(v):
    return v.astype(BF16).astype(F32)


def pieces(v):
    high = rounded(v)
    mid = rounded(v - high)
    return high, mid, rounded(v - high - mid)


def total(terms):
    return functools.reduce(jnp.add, terms)


def kernel(
    n_gx, n_gy, src_in, geo_in, near_in, far, in_in, out_in, coup_in, out, rbuf,
    hsrc, gbuf, gf, lists, weight, sfeat, tfeat, acc, res, zeros,
    base_in, base_out, flat, by_leaf, target, coup, level0, level12, blocks, block_buf, group_src, group_buf,
    mats, proj, col_buf, row_src, row_buf, tab3, int_src, int_buf,
    load, out_s, fill_s, geo_s, geo_r, list_s, list_r, src_s, src_r, res_s, res_r,
    p1_s, p1_r, p2_s, p2_r, p3_s, p3_r,
    block_s, block_r, group_s, group_r,
):
    x = lax.axis_index("gx")
    y = lax.axis_index("gy")
    leaf_dev, rhs, panels = out.shape
    middle = leaf_dev // 2
    first = middle + 1
    barrier = pltpu.get_barrier_semaphore()
    for k in range(1, n_gx):
        pl.semaphore_signal(
            barrier, inc=1, device_id=(lax.rem(x + k, n_gx), y), device_id_type=MESH
        )
    for k in range(1, n_gy):
        pl.semaphore_signal(
            barrier, inc=1, device_id=(x, lax.rem(y + k, n_gy)), device_id_type=MESH
        )

    loads = [
        pltpu.make_async_copy(a, b, load.at[i])
        for i, (a, b) in enumerate(
            [
                (src_in, hsrc.at[1]), (in_in, base_in), (coup_in, coup), (geo_in, gbuf.at[1]), (near_in, lists.at[1]),
                (out_in, base_out),
            ]
        )
    ]
    for one in loads:
        one.start()
    acc[...] = jnp.zeros_like(acc)

    def remote(src, dst, send, recv, where):
        return pltpu.make_async_remote_copy(
            src_ref=src, dst_ref=dst, send_sem=send, recv_sem=recv,
            device_id=where, device_id_type=MESH,
        )

    def has(d, at, n):
        return at > 0 if d < 0 else at < n - 1

    sides = (-1, 1)

    def geo_y(d):
        return remote(geo_in, gbuf.at[1 - d], geo_s.at[1 + d], geo_r.at[1 - d], (x, y + d))

    def geo_x(d):
        return remote(
            geo_in, gbuf.at[4 - d], geo_s.at[4 + d], geo_r.at[4 - d], (x + d, y)
        )

    def list_x(d):
        return remote(near_in, lists.at[1 - d], list_s.at[1 + d], list_r.at[1 - d], (x + d, y))

    def src_y(d, h):
        part = pl.ds(first * h, first if h == 0 else leaf_dev - first)
        return remote(
            src_in.at[part], hsrc.at[1 - d, part],
            src_s.at[1 + d, h], src_r.at[1 - d, h], (x, y + d),
        )

    def res_x(d, h):
        part = pl.ds(middle * h, middle)
        return remote(
            res.at[1 + d, part], rbuf.at[(1 - d) // 2, part],
            res_s.at[1 + d, h], res_r.at[1 - d, h], (x + d, y),
        )

    def absent(d):
        return pltpu.make_async_copy(zeros, rbuf.at[(1 + d) // 2], fill_s.at[(1 + d) // 2])

    def store(k):
        return pltpu.make_async_copy(acc.at[1, k], out.at[k], out_s.at[k])

    def arrived(make, d, h=0):
        if make is geo_y:
            c = remote(gbuf.at[1], gbuf.at[1 + d], geo_s.at[1 + d], geo_r.at[1 + d], (x, y + d))
        elif make is geo_x:
            c = remote(gbuf.at[1], gbuf.at[4 + d], geo_s.at[4 + d], geo_r.at[4 + d], (x + d, y))
        elif make is list_x:
            c = remote(
                lists.at[1], lists.at[1 + d], list_s.at[1 + d], list_r.at[1 + d], (x + d, y)
            )
        elif make is src_y:
            part = pl.ds(first * h, first if h == 0 else leaf_dev - first)
            c = remote(
                hsrc.at[1, part], hsrc.at[1 + d, part],
                src_s.at[1 + d, h], src_r.at[1 + d, h], (x, y + d),
            )
        else:
            part = pl.ds(middle * h, middle)
            c = remote(
                res.at[1 + d, part], rbuf.at[(1 + d) // 2, part],
                res_s.at[1 + d, h], res_r.at[1 + d, h], (x + d, y),
            )
        c.wait_recv()

    def column(src, buf, send, recv):
        for k in range(1, n_gy):
            to = lax.rem(y + k, n_gy)
            remote(src, buf.at[y], send.at[k], recv.at[y], (x, to)).start()
        buf[y] = src[...]

    def column_wait(src, buf, send, recv):
        for k in range(1, n_gy):
            peer = lax.rem(y + k, n_gy)
            remote(src, buf.at[peer], send.at[k], recv.at[peer], (x, peer)).wait_recv()

    row_at = lax.broadcasted_iota(jnp.int32, (8, panels), 0)
    quarter = 4 * (y // 4)
    half = rhs
    base = 4 * (x // 4)
    spot = lax.rem(x, 4)
    mine = lax.rem(y, 4)
    wide3 = 32 * (n_gx // 4)

    def product(a, b):
        a_high, b_high = a.astype(BF16), b.astype(BF16)
        a_low = (a - a_high.astype(F32)).astype(BF16)
        b_low = (b - b_high.astype(F32)).astype(BF16)
        return dot(a_high, b_high) + (dot(a_low, b_high) + dot(a_high, b_low))

    def by_cluster(level, clusters):
        shape = (32, 32 * clusters)
        lane = lax.broadcasted_iota(jnp.int32, shape, 1)
        place = lane >> 5
        same = (lane & 31) == lax.broadcasted_iota(jnp.int32, shape, 0)
        pick = [
            jnp.where(jnp.logical_and(same, place == far[level, m]), 1.0, 0.0).astype(BF16)
            for m in range(16)
        ]
        split = jnp.concatenate(pieces(coup[level]), axis=0).astype(BF16)
        v = dot(split, jnp.concatenate(pick, axis=0))
        return (v[0:32] + v[32:64]) + v[64:96]

    def block_copy(k):
        to = lax.rem(y + k, n_gy)
        return remote(
            blocks.at[lax.rem(to, 4)], block_buf.at[y], block_s.at[k], block_r.at[y], (x, to)
        )

    def group_copy(k):
        to = base + lax.rem(spot + k, 4)
        return remote(group_src, group_buf.at[spot], group_s.at[k], group_r.at[spot], (to, y))

    def gather_couplings():
        v = by_cluster(3, n_gx // 4)
        for b in range(4):
            blocks[b, :, 0 : v.shape[1]] = v[8 * b : 8 * b + 8]

    def give_couplings():
        for k in range(1, n_gy):
            block_copy(k).start()
        block_buf[y] = blocks[mine]

    def own_couplings():
        level0[...] = by_cluster(0, n_gy)
        level12[0:32, :] = by_cluster(1, n_gx)
        level12[32:64, :] = by_cluster(2, n_gx)

    def spread(at):
        raw = gbuf[at].astype(F32)
        raw = jnp.concatenate([raw, jnp.zeros((leaf_dev, 4, panels), F32)], axis=1)
        gf[at] = raw.reshape(8 * leaf_dev, panels)

    def source_features(place):
        shift = lax.convert_element_type(place - 1, F32)

        def leaf(k, carry):
            q = gf[place, pl.ds(pl.multiple_of(8 * k, 8), 8), :]
            q = jnp.where(row_at == 1, q + shift, q)
            area = q[3:4]
            factor = FOUR_PI / area
            factor = factor * factor
            square = q[0:1] * q[0:1] + q[1:2] * q[1:2] + q[2:3] * q[2:3] + area
            one = jnp.where(row_at == 4, 1.0, 0.0)
            v = jnp.where(row_at < 3, q, jnp.where(row_at == 3, square, one)) * factor
            a, b, c = pieces(v)
            wide = jnp.concatenate([a, b, c, a, b, a], axis=0)
            sfeat[place * leaf_dev + k] = wide.T.astype(BF16)
            return carry

        lax.fori_loop(0, leaf_dev, leaf, 0, unroll=8)

    def target_features(side, at):
        def leaf(l, carry):
            p = gf[at, pl.ds(pl.multiple_of(8 * l, 8), 8), :]
            p = jnp.where(row_at == 0, p + float(side), p)
            for dz in (-1, 0, 1):
                t = jnp.where(row_at == 2, p - float(dz), p)
                square = t[0:1] * t[0:1] + t[1:2] * t[1:2] + t[2:3] * t[2:3]
                last = jnp.where(row_at == 4, square, 0.0)
                v = jnp.where(row_at < 3, -2.0 * t, jnp.where(row_at == 3, 1.0, last))
                a, b, c = pieces(v)
                wide = jnp.concatenate([a, a, a, b, b, c], axis=0)
                tfeat[((side + 1) * leaf_dev + l) * 3 + dz + 1] = wide.astype(BF16)
            return carry

        lax.fori_loop(0, leaf_dev, leaf, 0, unroll=8)

    def weights(side):
        mine = lists[side + 1]
        leaf = lax.broadcasted_iota(jnp.int32, mine.shape, 0)
        for s in range(3):
            for dz in (-1, 0, 1):
                n = (x * n_gy + y + s - 1) * leaf_dev + dz + leaf
                there = jnp.logical_and(y + s >= 1, y + s <= n_gy)
                hits = jnp.where(jnp.logical_and(mine == n, there), 1.0, 0.0)
                count = jnp.sum(hits, axis=1, keepdims=True)
                weight[((side + 1) * 3 + s) * 3 + dz + 1] = jnp.broadcast_to(
                    count, (leaf_dev, panels)
                )

    def transposed(source, take):
        wide = source[...].astype(F32)
        for h in range(panels // 128):
            flat[h] = wide[:, 128 * h : 128 * (h + 1)]
        for k in range(leaf_dev):
            take(
                k,
                jnp.concatenate(
                    [
                        flat[h, pl.ds(k, 128, stride=leaf_dev), :]
                        for h in range(panels // 128)
                    ],
                    axis=1,
                ).astype(BF16),
            )

    def projections():
        loads[0].wait()
        loads[1].wait()
        parts = []
        transposed(base_in, lambda k, b: parts.append(dot(b, hsrc[1, k], 1, 1)))
        projection = total(parts)
        proj[:, 0:half] = projection[0:64]
        proj[:, half:] = projection[64:128]

    def own_features():
        loads[3].wait()
        loads[4].wait()
        spread(1)
        source_features(1)
        target_features(0, 1)
        weights(0)

    def couplings():
        loads[2].wait()
        gather_couplings()

    def enter():
        pl.semaphore_wait(barrier, n_gx - 1 + n_gy - 1)

    def send_geometry():
        for d in sides:
            @pl.when(has(d, x, n_gx))
            def _():
                geo_x(d).start()
                list_x(d).start()

            @pl.when(has(d, y, n_gy))
            def _():
                geo_y(d).start()

    def send_sources():
        for d in sides:
            @pl.when(has(d, y, n_gy))
            def _():
                src_y(d, 0).start()
                src_y(d, 1).start()

    def send_projections():
        column(proj, col_buf, p1_s, p1_r)

    projections()
    enter()
    send_geometry()
    send_projections()
    couplings()
    give_couplings()
    send_sources()
    own_features()
    lane = lax.broadcasted_iota(jnp.int32, (panels, FEATURES), 1)
    away = jnp.where(lane == 3, 1.0, 0.0).astype(BF16)
    for d in sides:
        @pl.when(jnp.logical_not(has(d, x, n_gx)))
        def _():
            zeros[...] = jnp.zeros(zeros.shape, BF16)
            absent(d).start()

        @pl.when(jnp.logical_not(has(d, y, n_gy)))
        def _():
            hsrc[1 + d] = jnp.zeros(hsrc.shape[1:], BF16)
            for k in range(leaf_dev):
                sfeat[(1 + d) * leaf_dev + k] = away

    def after_first():
        column_wait(proj, col_buf, p1_s, p1_r)
        row_src[0:32, 0:half] = total([col_buf[quarter + g, 32:64, 0:half] for g in range(4)])
        coarse = total([col_buf[g, :, half:] for g in range(n_gy)])
        row_src[0:32, half:] = coarse[0:32]
        row_src[32:48, 0:half] = coarse[32:48]
        row_src[32:48, half:] = coarse[48:64]
        for k in range(1, n_gx):
            to = lax.rem(x + k, n_gx)
            remote(row_src, row_buf.at[x], p2_s.at[k], p2_r.at[x], (to, y)).start()
        row_buf[x] = row_src[...]
        for k in range(1, n_gy):
            peer = lax.rem(y + k, n_gy)
            remote(
                blocks.at[0], block_buf.at[peer], block_s.at[k], block_r.at[peer], (x, peer)
            ).wait_recv()
        group_src[:, 0:wide3] = total([block_buf[g, :, 0:wide3] for g in range(n_gy)])
        for k in range(1, 4):
            group_copy(k).start()
        group_buf[spot] = group_src[...]
        zero = jnp.concatenate([col_buf[g, 0:32, 0:half] for g in range(n_gy)], axis=0)
        target[0:32, :] = product(level0[...], zero).astype(BF16)

    def after_second():
        for k in range(1, n_gx):
            peer = lax.rem(x + k, n_gx)
            remote(row_src, row_buf.at[peer], p2_s.at[k], p2_r.at[peer], (peer, y)).wait_recv()
        for k in range(1, 4):
            peer = lax.rem(spot + k, 4)
            remote(
                group_src, group_buf.at[peer], group_s.at[k], group_r.at[peer], (base + peer, y)
            ).wait_recv()
        fine = jnp.concatenate([row_buf[g, 0:32] for g in range(n_gx)], axis=0)
        both = product(level12[...], fine)
        int_src[0:32, 0:half] = both[0:32, 0:half]
        int_src[0:32, half:] = both[32:64, half:]
        for c in range(n_gx // 4):
            coarse = total([row_buf[4 * c + g, 32:48, :] for g in range(4)])
            tab3[32 * c : 32 * c + 16, :] = coarse[:, 0:half]
            tab3[32 * c + 16 : 32 * c + 32, :] = coarse[:, half:]
        third = total([group_buf[g, :, 0:wide3] for g in range(4)])
        int_src[32:40, 0:half] = product(third, tab3[...])
        int_src[32:40, half:] = jnp.zeros((8, half), F32)
        column(int_src, int_buf, p3_s, p3_r)

    def after_third():
        column_wait(int_src, int_buf, p3_s, p3_r)
        target[32:64, :] = total([int_buf[quarter + g, 0:32, 0:half] for g in range(4)]).astype(BF16)
        target[64:96, :] = total([int_buf[g, 0:32, half:] for g in range(n_gy)]).astype(BF16)
        third = [int_buf[quarter + b, 32:40, 0:half] for b in range(4)]
        target[96:128, :] = jnp.concatenate(third, axis=0).astype(BF16)

    def turn_bases():
        loads[5].wait()

        def take(k, b):
            by_leaf[k] = b

        transposed(base_out, take)

    def from_row():
        for d in sides:
            @pl.when(has(d, x, n_gx))
            def _():
                arrived(geo_x, d)
                arrived(list_x, d)
                spread(4 + d)
                target_features(d, 4 + d)
                weights(d)

    def from_column():
        for d in sides:
            @pl.when(has(d, y, n_gy))
            def _():
                arrived(geo_y, d)
                spread(1 + d)
                source_features(1 + d)
                arrived(src_y, d, 0)

    def rest_of_column():
        for d in sides:
            @pl.when(has(d, y, n_gy))
            def _():
                arrived(src_y, d, 1)

    outer = 2 * lax.rem(x, 2)

    def give(t, h):
        @pl.when(jnp.logical_and(x + t >= 1, x + t <= n_gx))
        def _():
            part = pl.ds(middle * h, middle)
            res[t, part] = acc[t, part].astype(BF16)
            res_x(t - 1, h).start()

    def chunk(t, halves):
        work = [(s, h, i) for s, h in halves for i in range(middle)]

        def leaves(h, i):
            sign = 1 - 2 * h
            l = (leaf_dev - 1) * h + sign * i
            return l, [(l + sign * e, sign * e) for e in (-1, 0, 1) if i + e >= 0]

        def fill(n):
            s, h, i = work[n]
            l, ks = leaves(h, i)
            for at, (k, dz) in enumerate(ks):
                squared = dot(sfeat[s * leaf_dev + k], tfeat[(t * leaf_dev + l) * 3 + dz + 1])
                w = weight[(t * 3 + s) * 3 + dz + 1, pl.ds(l, 1), :]
                mats[n % 2, panels * at : panels * (at + 1), :] = (
                    lax.rsqrt(squared) * w
                ).astype(BF16)

        def apply(n):
            s, h, i = work[n]
            l, ks = leaves(h, i)
            wide = jnp.concatenate([hsrc[s, k] for k, _ in ks], axis=1)
            acc[t, l] += dot(wide, mats[n % 2, 0 : panels * len(ks), :])

        fill(0)
        for n in range(len(work)):
            if n + 1 < len(work):
                fill(n + 1)
            apply(n)

    own_couplings()

    def step(c, carry):
        stages = {
            1: [from_row],
            2: [after_first],
            3: [turn_bases, from_column],
            4: [lambda: give(outer, 0)],
            5: [lambda: give(2 - outer, 0), rest_of_column],
            6: [after_second, lambda: give(outer, 1)],
            7: [lambda: give(2 - outer, 1)],

        }
        for at, work in stages.items():
            @pl.when(c == at)
            def _():
                for one in work:
                    one()

        own_turn = c < 3
        other = jnp.where(lax.rem(c, 2) == 1, outer, 2 - outer)
        t = jnp.where(jnp.logical_or(c == 0, c > 6), 1, other)
        half_turn = jnp.where(c < 7, (c - 3) // 2, c - 7)
        a = (jnp.where(own_turn, 1, 2), jnp.where(own_turn, 0, half_turn))
        b = (jnp.where(own_turn, 1, 0), jnp.where(own_turn, 1, half_turn))
        at_x = x + t - 1

        @pl.when(jnp.logical_and(at_x >= 0, at_x < n_gx))
        def _():
            chunk(t, [a, b])

        return carry

    lax.fori_loop(0, 9, step, 0)

    after_third()
    turned = target[...].astype(F32).T.astype(BF16)
    for k in range(leaf_dev):
        acc[1, k] += dot(turned, by_leaf[k])
        store(k).start()
    for d in sides:
        @pl.when(has(d, x, n_gx))
        def _():
            arrived(res_x, d, 0)
            arrived(res_x, d, 1)

        @pl.when(jnp.logical_not(has(d, x, n_gx)))
        def _():
            absent(d).wait()
    for k in range(leaf_dev):
        store(k).wait()

    for d in sides:
        @pl.when(has(d, x, n_gx))
        def _():
            geo_x(d).wait_send()
            list_x(d).wait_send()
            res_x(d, 0).wait_send()
            res_x(d, 1).wait_send()

        @pl.when(has(d, y, n_gy))
        def _():
            geo_y(d).wait_send()
            src_y(d, 0).wait_send()
            src_y(d, 1).wait_send()
    for k in range(1, n_gy):
        to = lax.rem(y + k, n_gy)
        remote(proj, col_buf.at[y], p1_s.at[k], p1_r.at[y], (x, to)).wait_send()
        remote(int_src, int_buf.at[y], p3_s.at[k], p3_r.at[y], (x, to)).wait_send()
        block_copy(k).wait_send()
    for k in range(1, 4):
        group_copy(k).wait_send()
    for k in range(1, n_gx):
        to = lax.rem(x + k, n_gx)
        remote(row_src, row_buf.at[x], p2_s.at[k], p2_r.at[x], (to, y)).wait_send()


def body(sources, geometry, near_lists, far_lists, bases_in, bases_out, couplings):
    leaf_dev, rhs, panels = sources.shape[2:]
    n_gx, n_gy = lax.axis_size("gx"), lax.axis_size("gy")
    anywhere = pl.BlockSpec(memory_space=pltpu.HBM)
    sems = pltpu.SemaphoreType.DMA
    flat_rows = bases_in.shape[2] * bases_in.shape[3] * leaf_dev
    own, given = pl.pallas_call(
        functools.partial(kernel, n_gx, n_gy),
        out_shape=(
            jax.ShapeDtypeStruct((leaf_dev, rhs, panels), F32),
            jax.ShapeDtypeStruct((2, leaf_dev, rhs, panels), BF16),
        ),
        in_specs=[
            anywhere, anywhere, anywhere, pl.BlockSpec(memory_space=pltpu.SMEM),
            anywhere, anywhere, anywhere,
        ],
        out_specs=(anywhere, anywhere),
        scratch_shapes=[
            pltpu.VMEM((3, leaf_dev, rhs, panels), BF16),
            pltpu.VMEM((6,) + geometry.shape[2:], BF16),
            pltpu.VMEM((6, 8 * leaf_dev, panels), F32),
            pltpu.VMEM((3,) + near_lists.shape[2:], jnp.int32),
            pltpu.VMEM((27, leaf_dev, panels), F32),
            pltpu.VMEM((3 * leaf_dev, panels, FEATURES), BF16),
            pltpu.VMEM((9 * leaf_dev, FEATURES, panels), BF16),
            pltpu.VMEM((3, leaf_dev, rhs, panels), F32),
            pltpu.VMEM((3, leaf_dev, rhs, panels), BF16),
            pltpu.VMEM((leaf_dev, rhs, panels), BF16),
            pltpu.VMEM((flat_rows, panels), BF16),
            pltpu.VMEM((flat_rows, panels), BF16),
            pltpu.VMEM((panels // 128, flat_rows, 128), F32),
            pltpu.VMEM((leaf_dev, 128, panels), BF16),
            pltpu.VMEM((128, rhs), BF16),
            pltpu.VMEM(couplings.shape[2:], F32),
            pltpu.VMEM((32, 32 * n_gy), F32),
            pltpu.VMEM((64, 32 * n_gx), F32),
            pltpu.VMEM((4, 8, max(128, 8 * n_gx)), F32),
            pltpu.VMEM((n_gy, 8, max(128, 8 * n_gx)), F32),
            pltpu.VMEM((8, max(128, 8 * n_gx)), F32),
            pltpu.VMEM((4, 8, max(128, 8 * n_gx)), F32),
            pltpu.VMEM((2, 3 * panels, panels), BF16),
            pltpu.VMEM((64, 2 * rhs), F32),
            pltpu.VMEM((n_gy, 64, 2 * rhs), F32),
            pltpu.VMEM((48, 2 * rhs), F32),
            pltpu.VMEM((n_gx, 48, 2 * rhs), F32),
            pltpu.VMEM((8 * n_gx, rhs), F32),
            pltpu.VMEM((40, 2 * rhs), F32),
            pltpu.VMEM((n_gy, 40, 2 * rhs), F32),
            sems((6,)), sems((leaf_dev,)), sems((2,)),
            sems((6,)), sems((6,)), sems((3,)), sems((3,)),
            sems((3, 2)), sems((3, 2)), sems((3, 2)), sems((3, 2)),
            sems((n_gy,)), sems((n_gy,)),
            sems((n_gx,)), sems((n_gx,)),
            sems((n_gy,)), sems((n_gy,)),
            sems((n_gy,)), sems((n_gy,)),
            sems((4,)), sems((4,)),
        ],
        compiler_params=pltpu.CompilerParams(
            collective_id=0, has_side_effects=True, vmem_limit_bytes=61440 * 1024
        ),
    )(
        sources[0, 0], geometry[0, 0], near_lists[0, 0], far_lists[0, 0],
        bases_in.reshape(flat_rows, panels), bases_out.reshape(flat_rows, panels),
        couplings[0, 0],
    )
    potential = own + (given[0].astype(F32) + given[1].astype(F32))
    return potential.reshape(sources.shape)


def solution(mesh):
    in_specs = (
        P("gx", "gy", None, None, None),
        P("gx", "gy", None, None, None),
        P("gx", "gy", None, None),
        P("gx", "gy", None, None),
        P("gx", "gy", None, None, None, None),
        P("gx", "gy", None, None, None, None),
        P("gx", "gy", None, None, None),
    )
    out_specs = P("gx", "gy", None, None, None)
    return jax.shard_map(body, mesh=mesh, in_specs=in_specs, out_specs=out_specs, check_vma=False)
```

```python
import functools
import math

import jax
import jax.numpy as jnp
from jax import lax
from jax.experimental import pallas as pl
from jax.experimental.pallas import tpu as pltpu
from jax.sharding import PartitionSpec as P

FOUR_PI = 4.0 * math.pi
MESH = pl.DeviceIdType.MESH
BF16 = jnp.bfloat16
F32 = jnp.float32
FEATURES = 48


def dot(a, b, da=1, db=0):
    return lax.dot_general(a, b, (((da,), (db,)), ((), ())), preferred_element_type=F32)


def rounded(v):
    return v.astype(BF16).astype(F32)


def pieces(v):
    high = rounded(v)
    mid = rounded(v - high)
    return high, mid, rounded(v - high - mid)


def total(terms):
    return functools.reduce(jnp.add, terms)


def kernel(
    n_gx, n_gy, src_in, geo_in, near_in, far, in_in, out_in, coup_in, out, rbuf,
    hsrc, gbuf, gf, lists, weight, sfeat, tfeat, acc, res, zeros,
    base_in, base_out, flat, by_leaf, target, coup, level0, level12, blocks, block_buf, group_src, group_buf,
    mats, proj, col_buf, row_src, row_buf, tab3, int_src, int_buf,
    load, out_s, fill_s, geo_s, geo_r, list_s, list_r, src_s, src_r, res_s, res_r,
    p1_s, p1_r, p2_s, p2_r, p3_s, p3_r,
    block_s, block_r, group_s, group_r,
):
    x = lax.axis_index("gx")
    y = lax.axis_index("gy")
    leaf_dev, rhs, panels = out.shape
    middle = leaf_dev // 2
    first = middle + 1
    barrier = pltpu.get_barrier_semaphore()
    for k in range(1, n_gx):
        pl.semaphore_signal(
            barrier, inc=1, device_id=(lax.rem(x + k, n_gx), y), device_id_type=MESH
        )
    for k in range(1, n_gy):
        pl.semaphore_signal(
            barrier, inc=1, device_id=(x, lax.rem(y + k, n_gy)), device_id_type=MESH
        )

    loads = [
        pltpu.make_async_copy(a, b, load.at[i])
        for i, (a, b) in enumerate(
            [
                (src_in, hsrc.at[1]), (in_in, base_in), (coup_in, coup), (geo_in, gbuf.at[1]), (near_in, lists.at[1]),
                (out_in, base_out),
            ]
        )
    ]
    for one in loads:
        one.start()
    acc[...] = jnp.zeros_like(acc)

    def remote(src, dst, send, recv, where):
        return pltpu.make_async_remote_copy(
            src_ref=src, dst_ref=dst, send_sem=send, recv_sem=recv,
            device_id=where, device_id_type=MESH,
        )

    def has(d, at, n):
        return at > 0 if d < 0 else at < n - 1

    sides = (-1, 1)

    def geo_y(d):
        return remote(geo_in, gbuf.at[1 - d], geo_s.at[1 + d], geo_r.at[1 - d], (x, y + d))

    def geo_x(d):
        return remote(
            geo_in, gbuf.at[4 - d], geo_s.at[4 + d], geo_r.at[4 - d], (x + d, y)
        )

    def list_x(d):
        return remote(near_in, lists.at[1 - d], list_s.at[1 + d], list_r.at[1 - d], (x + d, y))

    def src_y(d, h):
        part = pl.ds(first * h, first if h == 0 else leaf_dev - first)
        return remote(
            src_in.at[part], hsrc.at[1 - d, part],
            src_s.at[1 + d, h], src_r.at[1 - d, h], (x, y + d),
        )

    def res_x(d, h):
        part = pl.ds(middle * h, middle)
        return remote(
            res.at[1 + d, part], rbuf.at[(1 - d) // 2, part],
            res_s.at[1 + d, h], res_r.at[1 - d, h], (x + d, y),
        )

    def absent(d):
        return pltpu.make_async_copy(zeros, rbuf.at[(1 + d) // 2], fill_s.at[(1 + d) // 2])

    def store(k):
        return pltpu.make_async_copy(acc.at[1, k], out.at[k], out_s.at[k])

    def arrived(make, d, h=0):
        if make is geo_y:
            c = remote(gbuf.at[1], gbuf.at[1 + d], geo_s.at[1 + d], geo_r.at[1 + d], (x, y + d))
        elif make is geo_x:
            c = remote(gbuf.at[1], gbuf.at[4 + d], geo_s.at[4 + d], geo_r.at[4 + d], (x + d, y))
        elif make is list_x:
            c = remote(
                lists.at[1], lists.at[1 + d], list_s.at[1 + d], list_r.at[1 + d], (x + d, y)
            )
        elif make is src_y:
            part = pl.ds(first * h, first if h == 0 else leaf_dev - first)
            c = remote(
                hsrc.at[1, part], hsrc.at[1 + d, part],
                src_s.at[1 + d, h], src_r.at[1 + d, h], (x, y + d),
            )
        else:
            part = pl.ds(middle * h, middle)
            c = remote(
                res.at[1 + d, part], rbuf.at[(1 + d) // 2, part],
                res_s.at[1 + d, h], res_r.at[1 + d, h], (x + d, y),
            )
        c.wait_recv()

    def column(src, buf, send, recv):
        for k in range(1, n_gy):
            to = lax.rem(y + k, n_gy)
            remote(src, buf.at[y], send.at[k], recv.at[y], (x, to)).start()
        buf[y] = src[...]

    def column_wait(src, buf, send, recv):
        for k in range(1, n_gy):
            peer = lax.rem(y + k, n_gy)
            remote(src, buf.at[peer], send.at[k], recv.at[peer], (x, peer)).wait_recv()

    row_at = lax.broadcasted_iota(jnp.int32, (8, panels), 0)
    quarter = 4 * (y // 4)
    half = rhs
    base = 4 * (x // 4)
    spot = lax.rem(x, 4)
    mine = lax.rem(y, 4)
    wide3 = 32 * (n_gx // 4)

    def product(a, b):
        a_high, b_high = a.astype(BF16), b.astype(BF16)
        a_low = (a - a_high.astype(F32)).astype(BF16)
        b_low = (b - b_high.astype(F32)).astype(BF16)
        return dot(a_high, b_high) + (dot(a_low, b_high) + dot(a_high, b_low))

    def by_cluster(level, clusters):
        shape = (32, 32 * clusters)
        lane = lax.broadcasted_iota(jnp.int32, shape, 1)
        place = lane >> 5
        same = (lane & 31) == lax.broadcasted_iota(jnp.int32, shape, 0)
        pick = [
            jnp.where(jnp.logical_and(same, place == far[level, m]), 1.0, 0.0).astype(BF16)
            for m in range(16)
        ]
        split = jnp.concatenate(pieces(coup[level]), axis=0).astype(BF16)
        v = dot(split, jnp.concatenate(pick, axis=0))
        return (v[0:32] + v[32:64]) + v[64:96]

    def block_copy(k):
        to = lax.rem(y + k, n_gy)
        return remote(
            blocks.at[lax.rem(to, 4)], block_buf.at[y], block_s.at[k], block_r.at[y], (x, to)
        )

    def group_copy(k):
        to = base + lax.rem(spot + k, 4)
        return remote(group_src, group_buf.at[spot], group_s.at[k], group_r.at[spot], (to, y))

    def gather_couplings():
        v = by_cluster(3, n_gx // 4)
        for b in range(4):
            blocks[b, :, 0 : v.shape[1]] = v[8 * b : 8 * b + 8]

    def give_couplings():
        for k in range(1, n_gy):
            block_copy(k).start()
        block_buf[y] = blocks[mine]

    def own_couplings():
        level0[...] = by_cluster(0, n_gy)
        level12[0:32, :] = by_cluster(1, n_gx)
        level12[32:64, :] = by_cluster(2, n_gx)

    def spread(at):
        raw = gbuf[at].astype(F32)
        raw = jnp.concatenate([raw, jnp.zeros((leaf_dev, 4, panels), F32)], axis=1)
        gf[at] = raw.reshape(8 * leaf_dev, panels)

    def source_features(place):
        shift = lax.convert_element_type(place - 1, F32)

        def leaf(k, carry):
            q = gf[place, pl.ds(pl.multiple_of(8 * k, 8), 8), :]
            q = jnp.where(row_at == 1, q + shift, q)
            area = q[3:4]
            factor = FOUR_PI / area
            factor = factor * factor
            square = q[0:1] * q[0:1] + q[1:2] * q[1:2] + q[2:3] * q[2:3] + area
            one = jnp.where(row_at == 4, 1.0, 0.0)
            v = jnp.where(row_at < 3, q, jnp.where(row_at == 3, square, one)) * factor
            a, b, c = pieces(v)
            wide = jnp.concatenate([a, b, c, a, b, a], axis=0)
            sfeat[place * leaf_dev + k] = wide.T.astype(BF16)
            return carry

        lax.fori_loop(0, leaf_dev, leaf, 0, unroll=8)

    def target_features(side, at):
        def leaf(l, carry):
            p = gf[at, pl.ds(pl.multiple_of(8 * l, 8), 8), :]
            p = jnp.where(row_at == 0, p + float(side), p)
            for dz in (-1, 0, 1):
                t = jnp.where(row_at == 2, p - float(dz), p)
                square = t[0:1] * t[0:1] + t[1:2] * t[1:2] + t[2:3] * t[2:3]
                last = jnp.where(row_at == 4, square, 0.0)
                v = jnp.where(row_at < 3, -2.0 * t, jnp.where(row_at == 3, 1.0, last))
                a, b, c = pieces(v)
                wide = jnp.concatenate([a, a, a, b, b, c], axis=0)
                tfeat[((side + 1) * leaf_dev + l) * 3 + dz + 1] = wide.astype(BF16)
            return carry

        lax.fori_loop(0, leaf_dev, leaf, 0, unroll=8)

    def weights(side):
        mine = lists[side + 1]
        leaf = lax.broadcasted_iota(jnp.int32, mine.shape, 0)
        for s in range(3):
            for dz in (-1, 0, 1):
                n = (x * n_gy + y + s - 1) * leaf_dev + dz + leaf
                there = jnp.logical_and(y + s >= 1, y + s <= n_gy)
                hits = jnp.where(jnp.logical_and(mine == n, there), 1.0, 0.0)
                count = jnp.sum(hits, axis=1, keepdims=True)
                weight[((side + 1) * 3 + s) * 3 + dz + 1] = jnp.broadcast_to(
                    count, (leaf_dev, panels)
                )

    def transposed(source, take):
        wide = source[...].astype(F32)
        for h in range(panels // 128):
            flat[h] = wide[:, 128 * h : 128 * (h + 1)]
        for k in range(leaf_dev):
            take(
                k,
                jnp.concatenate(
                    [
                        flat[h, pl.ds(k, 128, stride=leaf_dev), :]
                        for h in range(panels // 128)
                    ],
                    axis=1,
                ).astype(BF16),
            )

    def projections():
        loads[0].wait()
        loads[1].wait()
        parts = []
        transposed(base_in, lambda k, b: parts.append(dot(b, hsrc[1, k], 1, 1)))
        projection = total(parts)
        proj[:, 0:half] = projection[0:64]
        proj[:, half:] = projection[64:128]

    def own_features():
        loads[3].wait()
        loads[4].wait()
        spread(1)
        source_features(1)
        target_features(0, 1)
        weights(0)

    def couplings():
        loads[2].wait()
        gather_couplings()

    def enter():
        pl.semaphore_wait(barrier, n_gx - 1 + n_gy - 1)

    def send_geometry():
        for d in sides:
            @pl.when(has(d, x, n_gx))
            def _():
                geo_x(d).start()
                list_x(d).start()

            @pl.when(has(d, y, n_gy))
            def _():
                geo_y(d).start()

    def send_sources(h):
        for d in sides:
            @pl.when(has(d, y, n_gy))
            def _():
                src_y(d, h).start()

    def send_projections():
        column(proj, col_buf, p1_s, p1_r)

    projections()
    enter()
    send_geometry()
    send_projections()
    couplings()
    give_couplings()
    send_sources(0)
    own_features()
    lane = lax.broadcasted_iota(jnp.int32, (panels, FEATURES), 1)
    away = jnp.where(lane == 3, 1.0, 0.0).astype(BF16)
    for d in sides:
        @pl.when(jnp.logical_not(has(d, x, n_gx)))
        def _():
            zeros[...] = jnp.zeros(zeros.shape, BF16)
            absent(d).start()

        @pl.when(jnp.logical_not(has(d, y, n_gy)))
        def _():
            hsrc[1 + d] = jnp.zeros(hsrc.shape[1:], BF16)
            for k in range(leaf_dev):
                sfeat[(1 + d) * leaf_dev + k] = away

    def after_first():
        column_wait(proj, col_buf, p1_s, p1_r)
        row_src[0:32, 0:half] = total([col_buf[quarter + g, 32:64, 0:half] for g in range(4)])
        coarse = total([col_buf[g, :, half:] for g in range(n_gy)])
        row_src[0:32, half:] = coarse[0:32]
        row_src[32:48, 0:half] = coarse[32:48]
        row_src[32:48, half:] = coarse[48:64]
        for k in range(1, n_gx):
            to = lax.rem(x + k, n_gx)
            remote(row_src, row_buf.at[x], p2_s.at[k], p2_r.at[x], (to, y)).start()
        row_buf[x] = row_src[...]
        for k in range(1, n_gy):
            peer = lax.rem(y + k, n_gy)
            remote(
                blocks.at[0], block_buf.at[peer], block_s.at[k], block_r.at[peer], (x, peer)
            ).wait_recv()
        group_src[:, 0:wide3] = total([block_buf[g, :, 0:wide3] for g in range(n_gy)])
        for k in range(1, 4):
            group_copy(k).start()
        group_buf[spot] = group_src[...]
        zero = jnp.concatenate([col_buf[g, 0:32, 0:half] for g in range(n_gy)], axis=0)
        target[0:32, :] = product(level0[...], zero).astype(BF16)

    def after_second():
        for k in range(1, n_gx):
            peer = lax.rem(x + k, n_gx)
            remote(row_src, row_buf.at[peer], p2_s.at[k], p2_r.at[peer], (peer, y)).wait_recv()
        for k in range(1, 4):
            peer = lax.rem(spot + k, 4)
            remote(
                group_src, group_buf.at[peer], group_s.at[k], group_r.at[peer], (base + peer, y)
            ).wait_recv()
        fine = jnp.concatenate([row_buf[g, 0:32] for g in range(n_gx)], axis=0)
        both = product(level12[...], fine)
        int_src[0:32, 0:half] = both[0:32, 0:half]
        int_src[0:32, half:] = both[32:64, half:]
        for c in range(n_gx // 4):
            coarse = total([row_buf[4 * c + g, 32:48, :] for g in range(4)])
            tab3[32 * c : 32 * c + 16, :] = coarse[:, 0:half]
            tab3[32 * c + 16 : 32 * c + 32, :] = coarse[:, half:]
        third = total([group_buf[g, :, 0:wide3] for g in range(4)])
        int_src[32:40, 0:half] = product(third, tab3[...])
        int_src[32:40, half:] = jnp.zeros((8, half), F32)
        column(int_src, int_buf, p3_s, p3_r)

    def after_third():
        column_wait(int_src, int_buf, p3_s, p3_r)
        target[32:64, :] = total([int_buf[quarter + g, 0:32, 0:half] for g in range(4)]).astype(BF16)
        target[64:96, :] = total([int_buf[g, 0:32, half:] for g in range(n_gy)]).astype(BF16)
        third = [int_buf[quarter + b, 32:40, 0:half] for b in range(4)]
        target[96:128, :] = jnp.concatenate(third, axis=0).astype(BF16)

    def turn_bases():
        loads[5].wait()

        def take(k, b):
            by_leaf[k] = b

        transposed(base_out, take)

    def from_row():
        for d in sides:
            @pl.when(has(d, x, n_gx))
            def _():
                arrived(geo_x, d)
                arrived(list_x, d)
                spread(4 + d)
                target_features(d, 4 + d)
                weights(d)

    def from_column():
        for d in sides:
            @pl.when(has(d, y, n_gy))
            def _():
                arrived(geo_y, d)
                spread(1 + d)
                source_features(1 + d)
                arrived(src_y, d, 0)

    def rest_of_column():
        for d in sides:
            @pl.when(has(d, y, n_gy))
            def _():
                arrived(src_y, d, 1)

    outer = 2 * lax.rem(x, 2)

    def give(t, h):
        @pl.when(jnp.logical_and(x + t >= 1, x + t <= n_gx))
        def _():
            part = pl.ds(middle * h, middle)
            res[t, part] = acc[t, part].astype(BF16)
            res_x(t - 1, h).start()

    def chunk(t, halves):
        work = [(s, h, i) for s, h in halves for i in range(middle)]

        def leaves(h, i):
            sign = 1 - 2 * h
            l = (leaf_dev - 1) * h + sign * i
            return l, [(l + sign * e, sign * e) for e in (-1, 0, 1) if i + e >= 0]

        def fill(n):
            s, h, i = work[n]
            l, ks = leaves(h, i)
            for at, (k, dz) in enumerate(ks):
                squared = dot(sfeat[s * leaf_dev + k], tfeat[(t * leaf_dev + l) * 3 + dz + 1])
                w = weight[(t * 3 + s) * 3 + dz + 1, pl.ds(l, 1), :]
                mats[n % 2, panels * at : panels * (at + 1), :] = (
                    lax.rsqrt(squared) * w
                ).astype(BF16)

        def apply(n):
            s, h, i = work[n]
            l, ks = leaves(h, i)
            wide = jnp.concatenate([hsrc[s, k] for k, _ in ks], axis=1)
            acc[t, l] += dot(wide, mats[n % 2, 0 : panels * len(ks), :])

        fill(0)
        for n in range(len(work)):
            if n + 1 < len(work):
                fill(n + 1)
            apply(n)

    own_couplings()

    def step(c, carry):
        stages = {
            1: [from_row],
            2: [after_first, lambda: send_sources(1)],
            3: [turn_bases, from_column],
            4: [lambda: give(outer, 0)],
            5: [lambda: give(2 - outer, 0), rest_of_column, after_second],
            6: [lambda: give(outer, 1)],
            7: [lambda: give(2 - outer, 1)],

        }
        for at, work in stages.items():
            @pl.when(c == at)
            def _():
                for one in work:
                    one()

        own_turn = c < 3
        other = jnp.where(lax.rem(c, 2) == 1, outer, 2 - outer)
        t = jnp.where(jnp.logical_or(c == 0, c > 6), 1, other)
        half_turn = jnp.where(c < 7, (c - 3) // 2, c - 7)
        a = (jnp.where(own_turn, 1, 2), jnp.where(own_turn, 0, half_turn))
        b = (jnp.where(own_turn, 1, 0), jnp.where(own_turn, 1, half_turn))
        at_x = x + t - 1

        @pl.when(jnp.logical_and(at_x >= 0, at_x < n_gx))
        def _():
            chunk(t, [a, b])

        return carry

    lax.fori_loop(0, 9, step, 0)

    after_third()
    turned = target[...].astype(F32).T.astype(BF16)
    for k in range(leaf_dev):
        acc[1, k] += dot(turned, by_leaf[k])
        store(k).start()
    for d in sides:
        @pl.when(has(d, x, n_gx))
        def _():
            arrived(res_x, d, 0)
            arrived(res_x, d, 1)

        @pl.when(jnp.logical_not(has(d, x, n_gx)))
        def _():
            absent(d).wait()
    for k in range(leaf_dev):
        store(k).wait()

    for d in sides:
        @pl.when(has(d, x, n_gx))
        def _():
            geo_x(d).wait_send()
            list_x(d).wait_send()
            res_x(d, 0).wait_send()
            res_x(d, 1).wait_send()

        @pl.when(has(d, y, n_gy))
        def _():
            geo_y(d).wait_send()
            src_y(d, 0).wait_send()
            src_y(d, 1).wait_send()
    for k in range(1, n_gy):
        to = lax.rem(y + k, n_gy)
        remote(proj, col_buf.at[y], p1_s.at[k], p1_r.at[y], (x, to)).wait_send()
        remote(int_src, int_buf.at[y], p3_s.at[k], p3_r.at[y], (x, to)).wait_send()
        block_copy(k).wait_send()
    for k in range(1, 4):
        group_copy(k).wait_send()
    for k in range(1, n_gx):
        to = lax.rem(x + k, n_gx)
        remote(row_src, row_buf.at[x], p2_s.at[k], p2_r.at[x], (to, y)).wait_send()


def body(sources, geometry, near_lists, far_lists, bases_in, bases_out, couplings):
    leaf_dev, rhs, panels = sources.shape[2:]
    n_gx, n_gy = lax.axis_size("gx"), lax.axis_size("gy")
    anywhere = pl.BlockSpec(memory_space=pltpu.HBM)
    sems = pltpu.SemaphoreType.DMA
    flat_rows = bases_in.shape[2] * bases_in.shape[3] * leaf_dev
    own, given = pl.pallas_call(
        functools.partial(kernel, n_gx, n_gy),
        out_shape=(
            jax.ShapeDtypeStruct((leaf_dev, rhs, panels), F32),
            jax.ShapeDtypeStruct((2, leaf_dev, rhs, panels), BF16),
        ),
        in_specs=[
            anywhere, anywhere, anywhere, pl.BlockSpec(memory_space=pltpu.SMEM),
            anywhere, anywhere, anywhere,
        ],
        out_specs=(anywhere, anywhere),
        scratch_shapes=[
            pltpu.VMEM((3, leaf_dev, rhs, panels), BF16),
            pltpu.VMEM((6,) + geometry.shape[2:], BF16),
            pltpu.VMEM((6, 8 * leaf_dev, panels), F32),
            pltpu.VMEM((3,) + near_lists.shape[2:], jnp.int32),
            pltpu.VMEM((27, leaf_dev, panels), F32),
            pltpu.VMEM((3 * leaf_dev, panels, FEATURES), BF16),
            pltpu.VMEM((9 * leaf_dev, FEATURES, panels), BF16),
            pltpu.VMEM((3, leaf_dev, rhs, panels), F32),
            pltpu.VMEM((3, leaf_dev, rhs, panels), BF16),
            pltpu.VMEM((leaf_dev, rhs, panels), BF16),
            pltpu.VMEM((flat_rows, panels), BF16),
            pltpu.VMEM((flat_rows, panels), BF16),
            pltpu.VMEM((panels // 128, flat_rows, 128), F32),
            pltpu.VMEM((leaf_dev, 128, panels), BF16),
            pltpu.VMEM((128, rhs), BF16),
            pltpu.VMEM(couplings.shape[2:], F32),
            pltpu.VMEM((32, 32 * n_gy), F32),
            pltpu.VMEM((64, 32 * n_gx), F32),
            pltpu.VMEM((4, 8, max(128, 8 * n_gx)), F32),
            pltpu.VMEM((n_gy, 8, max(128, 8 * n_gx)), F32),
            pltpu.VMEM((8, max(128, 8 * n_gx)), F32),
            pltpu.VMEM((4, 8, max(128, 8 * n_gx)), F32),
            pltpu.VMEM((2, 3 * panels, panels), BF16),
            pltpu.VMEM((64, 2 * rhs), F32),
            pltpu.VMEM((n_gy, 64, 2 * rhs), F32),
            pltpu.VMEM((48, 2 * rhs), F32),
            pltpu.VMEM((n_gx, 48, 2 * rhs), F32),
            pltpu.VMEM((8 * n_gx, rhs), F32),
            pltpu.VMEM((40, 2 * rhs), F32),
            pltpu.VMEM((n_gy, 40, 2 * rhs), F32),
            sems((6,)), sems((leaf_dev,)), sems((2,)),
            sems((6,)), sems((6,)), sems((3,)), sems((3,)),
            sems((3, 2)), sems((3, 2)), sems((3, 2)), sems((3, 2)),
            sems((n_gy,)), sems((n_gy,)),
            sems((n_gx,)), sems((n_gx,)),
            sems((n_gy,)), sems((n_gy,)),
            sems((n_gy,)), sems((n_gy,)),
            sems((4,)), sems((4,)),
        ],
        compiler_params=pltpu.CompilerParams(
            collective_id=0, has_side_effects=True, vmem_limit_bytes=61440 * 1024
        ),
    )(
        sources[0, 0], geometry[0, 0], near_lists[0, 0], far_lists[0, 0],
        bases_in.reshape(flat_rows, panels), bases_out.reshape(flat_rows, panels),
        couplings[0, 0],
    )
    potential = own + (given[0].astype(F32) + given[1].astype(F32))
    return potential.reshape(sources.shape)


def solution(mesh):
    in_specs = (
        P("gx", "gy", None, None, None),
        P("gx", "gy", None, None, None),
        P("gx", "gy", None, None),
        P("gx", "gy", None, None),
        P("gx", "gy", None, None, None, None),
        P("gx", "gy", None, None, None, None),
        P("gx", "gy", None, None, None),
    )
    out_specs = P("gx", "gy", None, None, None)
    return jax.shard_map(body, mesh=mesh, in_specs=in_specs, out_specs=out_specs, check_vma=False)
```

```python
import functools
import math

import jax
import jax.numpy as jnp
from jax import lax
from jax.experimental import pallas as pl
from jax.experimental.pallas import tpu as pltpu
from jax.sharding import PartitionSpec as P

FOUR_PI = 4.0 * math.pi
MESH = pl.DeviceIdType.MESH
BF16 = jnp.bfloat16
F32 = jnp.float32
FEATURES = 48


def dot(a, b, da=1, db=0):
    return lax.dot_general(a, b, (((da,), (db,)), ((), ())), preferred_element_type=F32)


def rounded(v):
    return v.astype(BF16).astype(F32)


def pieces(v):
    high = rounded(v)
    mid = rounded(v - high)
    return high, mid, rounded(v - high - mid)


def total(terms):
    return functools.reduce(jnp.add, terms)


def kernel(
    n_gx, n_gy, src_in, geo_in, near_in, far, in_in, out_in, coup_in, out, rbuf,
    hsrc, gbuf, gf, lists, weight, sfeat, tfeat, acc, res, zeros,
    base_in, base_out, flat, by_leaf, target, coup, level0, level12, blocks, block_buf, group_src, group_buf,
    mats, proj, col_buf, row_src, row_buf, tab3, int_src, int_buf,
    load, out_s, fill_s, geo_s, geo_r, list_s, list_r, src_s, src_r, res_s, res_r,
    p1_s, p1_r, p2_s, p2_r, p3_s, p3_r,
    block_s, block_r, group_s, group_r,
):
    x = lax.axis_index("gx")
    y = lax.axis_index("gy")
    leaf_dev, rhs, panels = out.shape
    middle = leaf_dev // 2
    first = middle + 1
    barrier = pltpu.get_barrier_semaphore()
    for k in range(1, n_gx):
        pl.semaphore_signal(
            barrier, inc=1, device_id=(lax.rem(x + k, n_gx), y), device_id_type=MESH
        )
    for k in range(1, n_gy):
        pl.semaphore_signal(
            barrier, inc=1, device_id=(x, lax.rem(y + k, n_gy)), device_id_type=MESH
        )

    loads = [
        pltpu.make_async_copy(a, b, load.at[i])
        for i, (a, b) in enumerate(
            [
                (src_in, hsrc.at[1]), (in_in, base_in), (coup_in, coup), (geo_in, gbuf.at[1]), (near_in, lists.at[1]),
                (out_in, base_out),
            ]
        )
    ]
    for one in loads:
        one.start()
    acc[...] = jnp.zeros_like(acc)

    def remote(src, dst, send, recv, where):
        return pltpu.make_async_remote_copy(
            src_ref=src, dst_ref=dst, send_sem=send, recv_sem=recv,
            device_id=where, device_id_type=MESH,
        )

    def has(d, at, n):
        return at > 0 if d < 0 else at < n - 1

    sides = (-1, 1)

    def geo_y(d):
        return remote(geo_in, gbuf.at[1 - d], geo_s.at[1 + d], geo_r.at[1 - d], (x, y + d))

    def geo_x(d):
        return remote(
            geo_in, gbuf.at[4 - d], geo_s.at[4 + d], geo_r.at[4 - d], (x + d, y)
        )

    def list_x(d):
        return remote(near_in, lists.at[1 - d], list_s.at[1 + d], list_r.at[1 - d], (x + d, y))

    def src_y(d, h):
        part = pl.ds(first * h, first if h == 0 else leaf_dev - first)
        return remote(
            src_in.at[part], hsrc.at[1 - d, part],
            src_s.at[1 + d, h], src_r.at[1 - d, h], (x, y + d),
        )

    def res_x(d, h):
        part = pl.ds(middle * h, middle)
        return remote(
            res.at[1 + d, part], rbuf.at[(1 - d) // 2, part],
            res_s.at[1 + d, h], res_r.at[1 - d, h], (x + d, y),
        )

    def absent(d):
        return pltpu.make_async_copy(zeros, rbuf.at[(1 + d) // 2], fill_s.at[(1 + d) // 2])

    def store(k):
        return pltpu.make_async_copy(acc.at[1, k], out.at[k], out_s.at[k])

    def arrived(make, d, h=0):
        if make is geo_y:
            c = remote(gbuf.at[1], gbuf.at[1 + d], geo_s.at[1 + d], geo_r.at[1 + d], (x, y + d))
        elif make is geo_x:
            c = remote(gbuf.at[1], gbuf.at[4 + d], geo_s.at[4 + d], geo_r.at[4 + d], (x + d, y))
        elif make is list_x:
            c = remote(
                lists.at[1], lists.at[1 + d], list_s.at[1 + d], list_r.at[1 + d], (x + d, y)
            )
        elif make is src_y:
            part = pl.ds(first * h, first if h == 0 else leaf_dev - first)
            c = remote(
                hsrc.at[1, part], hsrc.at[1 + d, part],
                src_s.at[1 + d, h], src_r.at[1 + d, h], (x, y + d),
            )
        else:
            part = pl.ds(middle * h, middle)
            c = remote(
                res.at[1 + d, part], rbuf.at[(1 + d) // 2, part],
                res_s.at[1 + d, h], res_r.at[1 + d, h], (x + d, y),
            )
        c.wait_recv()

    def column(src, buf, send, recv):
        for k in range(1, n_gy):
            to = lax.rem(y + k, n_gy)
            remote(src, buf.at[y], send.at[k], recv.at[y], (x, to)).start()
        buf[y] = src[...]

    def column_wait(src, buf, send, recv):
        for k in range(1, n_gy):
            peer = lax.rem(y + k, n_gy)
            remote(src, buf.at[peer], send.at[k], recv.at[peer], (x, peer)).wait_recv()

    row_at = lax.broadcasted_iota(jnp.int32, (8, panels), 0)
    quarter = 4 * (y // 4)
    half = rhs
    base = 4 * (x // 4)
    spot = lax.rem(x, 4)
    mine = lax.rem(y, 4)
    wide3 = 32 * (n_gx // 4)

    def product(a, b):
        a_high, b_high = a.astype(BF16), b.astype(BF16)
        a_low = (a - a_high.astype(F32)).astype(BF16)
        b_low = (b - b_high.astype(F32)).astype(BF16)
        return dot(a_high, b_high) + (dot(a_low, b_high) + dot(a_high, b_low))

    def by_cluster(level, clusters):
        shape = (32, 32 * clusters)
        lane = lax.broadcasted_iota(jnp.int32, shape, 1)
        place = lane >> 5
        same = (lane & 31) == lax.broadcasted_iota(jnp.int32, shape, 0)
        pick = [
            jnp.where(jnp.logical_and(same, place == far[level, m]), 1.0, 0.0).astype(BF16)
            for m in range(16)
        ]
        split = jnp.concatenate(pieces(coup[level]), axis=0).astype(BF16)
        v = dot(split, jnp.concatenate(pick, axis=0))
        return (v[0:32] + v[32:64]) + v[64:96]

    def block_copy(k):
        to = lax.rem(y + k, n_gy)
        return remote(
            blocks.at[lax.rem(to, 4)], block_buf.at[y], block_s.at[k], block_r.at[y], (x, to)
        )

    def group_copy(k):
        to = base + lax.rem(spot + k, 4)
        return remote(group_src, group_buf.at[spot], group_s.at[k], group_r.at[spot], (to, y))

    def gather_couplings():
        v = by_cluster(3, n_gx // 4)
        for b in range(4):
            blocks[b, :, 0 : v.shape[1]] = v[8 * b : 8 * b + 8]

    def give_couplings():
        for k in range(1, n_gy):
            block_copy(k).start()
        block_buf[y] = blocks[mine]

    def own_couplings():
        level0[...] = by_cluster(0, n_gy)
        level12[0:32, :] = by_cluster(1, n_gx)
        level12[32:64, :] = by_cluster(2, n_gx)

    def spread(at):
        raw = gbuf[at].astype(F32)
        raw = jnp.concatenate([raw, jnp.zeros((leaf_dev, 4, panels), F32)], axis=1)
        gf[at] = raw.reshape(8 * leaf_dev, panels)

    def source_features(place):
        shift = lax.convert_element_type(place - 1, F32)

        def leaf(k, carry):
            q = gf[place, pl.ds(pl.multiple_of(8 * k, 8), 8), :]
            q = jnp.where(row_at == 1, q + shift, q)
            area = q[3:4]
            factor = FOUR_PI / area
            factor = factor * factor
            square = q[0:1] * q[0:1] + q[1:2] * q[1:2] + q[2:3] * q[2:3] + area
            one = jnp.where(row_at == 4, 1.0, 0.0)
            v = jnp.where(row_at < 3, q, jnp.where(row_at == 3, square, one)) * factor
            a, b, c = pieces(v)
            wide = jnp.concatenate([a, b, c, a, b, a], axis=0)
            sfeat[place * leaf_dev + k] = wide.T.astype(BF16)
            return carry

        lax.fori_loop(0, leaf_dev, leaf, 0, unroll=8)

    def target_features(side, at):
        def leaf(l, carry):
            p = gf[at, pl.ds(pl.multiple_of(8 * l, 8), 8), :]
            p = jnp.where(row_at == 0, p + float(side), p)
            for dz in (-1, 0, 1):
                t = jnp.where(row_at == 2, p - float(dz), p)
                square = t[0:1] * t[0:1] + t[1:2] * t[1:2] + t[2:3] * t[2:3]
                last = jnp.where(row_at == 4, square, 0.0)
                v = jnp.where(row_at < 3, -2.0 * t, jnp.where(row_at == 3, 1.0, last))
                a, b, c = pieces(v)
                wide = jnp.concatenate([a, a, a, b, b, c], axis=0)
                tfeat[((side + 1) * leaf_dev + l) * 3 + dz + 1] = wide.astype(BF16)
            return carry

        lax.fori_loop(0, leaf_dev, leaf, 0, unroll=8)

    def weights(side):
        mine = lists[side + 1]
        leaf = lax.broadcasted_iota(jnp.int32, mine.shape, 0)
        for s in range(3):
            for dz in (-1, 0, 1):
                n = (x * n_gy + y + s - 1) * leaf_dev + dz + leaf
                there = jnp.logical_and(y + s >= 1, y + s <= n_gy)
                hits = jnp.where(jnp.logical_and(mine == n, there), 1.0, 0.0)
                count = jnp.sum(hits, axis=1, keepdims=True)
                weight[((side + 1) * 3 + s) * 3 + dz + 1] = jnp.broadcast_to(
                    count, (leaf_dev, panels)
                )

    def transposed(source, take):
        wide = source[...].astype(F32)
        for h in range(panels // 128):
            flat[h] = wide[:, 128 * h : 128 * (h + 1)]
        for k in range(leaf_dev):
            take(
                k,
                jnp.concatenate(
                    [
                        flat[h, pl.ds(k, 128, stride=leaf_dev), :]
                        for h in range(panels // 128)
                    ],
                    axis=1,
                ).astype(BF16),
            )

    def projections():
        loads[0].wait()
        loads[1].wait()
        parts = []
        transposed(base_in, lambda k, b: parts.append(dot(b, hsrc[1, k], 1, 1)))
        projection = total(parts)
        proj[:, 0:half] = projection[0:64]
        proj[:, half:] = projection[64:128]

    def own_features():
        loads[3].wait()
        loads[4].wait()
        spread(1)
        source_features(1)
        target_features(0, 1)
        weights(0)

    def couplings():
        loads[2].wait()
        gather_couplings()

    def enter():
        pl.semaphore_wait(barrier, n_gx - 1 + n_gy - 1)

    def send_geometry():
        for d in sides:
            @pl.when(has(d, x, n_gx))
            def _():
                geo_x(d).start()
                list_x(d).start()

            @pl.when(has(d, y, n_gy))
            def _():
                geo_y(d).start()

    def send_sources():
        for d in sides:
            @pl.when(has(d, y, n_gy))
            def _():
                src_y(d, 0).start()
                src_y(d, 1).start()

    def send_projections():
        column(proj, col_buf, p1_s, p1_r)

    projections()
    enter()
    send_geometry()
    send_projections()
    couplings()
    give_couplings()
    send_sources()
    own_features()
    lane = lax.broadcasted_iota(jnp.int32, (panels, FEATURES), 1)
    away = jnp.where(lane == 3, 1.0, 0.0).astype(BF16)
    for d in sides:
        @pl.when(jnp.logical_not(has(d, x, n_gx)))
        def _():
            zeros[...] = jnp.zeros(zeros.shape, BF16)
            absent(d).start()

        @pl.when(jnp.logical_not(has(d, y, n_gy)))
        def _():
            hsrc[1 + d] = jnp.zeros(hsrc.shape[1:], BF16)
            for k in range(leaf_dev):
                sfeat[(1 + d) * leaf_dev + k] = away

    def after_first():
        column_wait(proj, col_buf, p1_s, p1_r)
        row_src[0:32, 0:half] = total([col_buf[quarter + g, 32:64, 0:half] for g in range(4)])
        coarse = total([col_buf[g, :, half:] for g in range(n_gy)])
        row_src[0:32, half:] = coarse[0:32]
        row_src[32:48, 0:half] = coarse[32:48]
        row_src[32:48, half:] = coarse[48:64]
        for k in range(1, n_gx):
            to = lax.rem(x + k, n_gx)
            remote(row_src, row_buf.at[x], p2_s.at[k], p2_r.at[x], (to, y)).start()
        row_buf[x] = row_src[...]
        for k in range(1, n_gy):
            peer = lax.rem(y + k, n_gy)
            remote(
                blocks.at[0], block_buf.at[peer], block_s.at[k], block_r.at[peer], (x, peer)
            ).wait_recv()
        group_src[:, 0:wide3] = total([block_buf[g, :, 0:wide3] for g in range(n_gy)])
        for k in range(1, 4):
            group_copy(k).start()
        group_buf[spot] = group_src[...]
        zero = jnp.concatenate([col_buf[g, 0:32, 0:half] for g in range(n_gy)], axis=0)
        target[0:32, :] = product(level0[...], zero).astype(BF16)

    def after_second():
        for k in range(1, n_gx):
            peer = lax.rem(x + k, n_gx)
            remote(row_src, row_buf.at[peer], p2_s.at[k], p2_r.at[peer], (peer, y)).wait_recv()
        for k in range(1, 4):
            peer = lax.rem(spot + k, 4)
            remote(
                group_src, group_buf.at[peer], group_s.at[k], group_r.at[peer], (base + peer, y)
            ).wait_recv()
        fine = jnp.concatenate([row_buf[g, 0:32] for g in range(n_gx)], axis=0)
        both = product(level12[...], fine)
        int_src[0:32, 0:half] = both[0:32, 0:half]
        int_src[0:32, half:] = both[32:64, half:]
        for c in range(n_gx // 4):
            coarse = total([row_buf[4 * c + g, 32:48, :] for g in range(4)])
            tab3[32 * c : 32 * c + 16, :] = coarse[:, 0:half]
            tab3[32 * c + 16 : 32 * c + 32, :] = coarse[:, half:]
        third = total([group_buf[g, :, 0:wide3] for g in range(4)])
        int_src[32:40, 0:half] = product(third, tab3[...])
        int_src[32:40, half:] = jnp.zeros((8, half), F32)
        column(int_src, int_buf, p3_s, p3_r)

    def after_third():
        column_wait(int_src, int_buf, p3_s, p3_r)
        target[32:64, :] = total([int_buf[quarter + g, 0:32, 0:half] for g in range(4)]).astype(BF16)
        target[64:96, :] = total([int_buf[g, 0:32, half:] for g in range(n_gy)]).astype(BF16)
        third = [int_buf[quarter + b, 32:40, 0:half] for b in range(4)]
        target[96:128, :] = jnp.concatenate(third, axis=0).astype(BF16)

    def turn_bases():
        loads[5].wait()

        def take(k, b):
            by_leaf[k] = b

        transposed(base_out, take)

    def from_row():
        for d in sides:
            @pl.when(has(d, x, n_gx))
            def _():
                arrived(geo_x, d)
                arrived(list_x, d)
                spread(4 + d)
                target_features(d, 4 + d)
                weights(d)

    def from_column():
        for d in sides:
            @pl.when(has(d, y, n_gy))
            def _():
                arrived(geo_y, d)
                spread(1 + d)
                source_features(1 + d)
                arrived(src_y, d, 0)

    def rest_of_column():
        for d in sides:
            @pl.when(has(d, y, n_gy))
            def _():
                arrived(src_y, d, 1)

    outer = 2 * lax.rem(x, 2)

    def give(t, h):
        @pl.when(jnp.logical_and(x + t >= 1, x + t <= n_gx))
        def _():
            part = pl.ds(middle * h, middle)
            res[t, part] = acc[t, part].astype(BF16)
            res_x(t - 1, h).start()

    def chunk(t, halves):
        work = [(s, h, i) for s, h in halves for i in range(middle)]

        def leaves(h, i):
            sign = 1 - 2 * h
            l = (leaf_dev - 1) * h + sign * i
            return l, [(l + sign * e, sign * e) for e in (-1, 0, 1) if i + e >= 0]

        def fill(n):
            s, h, i = work[n]
            l, ks = leaves(h, i)
            for at, (k, dz) in enumerate(ks):
                squared = dot(sfeat[s * leaf_dev + k], tfeat[(t * leaf_dev + l) * 3 + dz + 1])
                w = weight[(t * 3 + s) * 3 + dz + 1, pl.ds(l, 1), :]
                mats[n % 4, panels * at : panels * (at + 1), :] = (
                    lax.rsqrt(squared) * w
                ).astype(BF16)

        def apply(n):
            s, h, i = work[n]
            l, ks = leaves(h, i)
            wide = jnp.concatenate([hsrc[s, k] for k, _ in ks], axis=1)
            acc[t, l] += dot(wide, mats[n % 4, 0 : panels * len(ks), :])

        fill(0)
        fill(1)
        for n in range(len(work)):
            if n + 2 < len(work):
                fill(n + 2)
            apply(n)

    own_couplings()

    def step(c, carry):
        stages = {
            1: [from_row],
            2: [after_first],
            3: [turn_bases, from_column],
            4: [lambda: give(outer, 0)],
            5: [lambda: give(2 - outer, 0), rest_of_column, after_second],
            6: [lambda: give(outer, 1)],
            7: [lambda: give(2 - outer, 1)],

        }
        for at, work in stages.items():
            @pl.when(c == at)
            def _():
                for one in work:
                    one()

        own_turn = c < 3
        other = jnp.where(lax.rem(c, 2) == 1, outer, 2 - outer)
        t = jnp.where(jnp.logical_or(c == 0, c > 6), 1, other)
        half_turn = jnp.where(c < 7, (c - 3) // 2, c - 7)
        a = (jnp.where(own_turn, 1, 2), jnp.where(own_turn, 0, half_turn))
        b = (jnp.where(own_turn, 1, 0), jnp.where(own_turn, 1, half_turn))
        at_x = x + t - 1

        @pl.when(jnp.logical_and(at_x >= 0, at_x < n_gx))
        def _():
            chunk(t, [a, b])

        return carry

    lax.fori_loop(0, 9, step, 0)

    after_third()
    turned = target[...].astype(F32).T.astype(BF16)
    for k in range(leaf_dev):
        acc[1, k] += dot(turned, by_leaf[k])
        store(k).start()
    for d in sides:
        @pl.when(has(d, x, n_gx))
        def _():
            arrived(res_x, d, 0)
            arrived(res_x, d, 1)

        @pl.when(jnp.logical_not(has(d, x, n_gx)))
        def _():
            absent(d).wait()
    for k in range(leaf_dev):
        store(k).wait()

    for d in sides:
        @pl.when(has(d, x, n_gx))
        def _():
            geo_x(d).wait_send()
            list_x(d).wait_send()
            res_x(d, 0).wait_send()
            res_x(d, 1).wait_send()

        @pl.when(has(d, y, n_gy))
        def _():
            geo_y(d).wait_send()
            src_y(d, 0).wait_send()
            src_y(d, 1).wait_send()
    for k in range(1, n_gy):
        to = lax.rem(y + k, n_gy)
        remote(proj, col_buf.at[y], p1_s.at[k], p1_r.at[y], (x, to)).wait_send()
        remote(int_src, int_buf.at[y], p3_s.at[k], p3_r.at[y], (x, to)).wait_send()
        block_copy(k).wait_send()
    for k in range(1, 4):
        group_copy(k).wait_send()
    for k in range(1, n_gx):
        to = lax.rem(x + k, n_gx)
        remote(row_src, row_buf.at[x], p2_s.at[k], p2_r.at[x], (to, y)).wait_send()


def body(sources, geometry, near_lists, far_lists, bases_in, bases_out, couplings):
    leaf_dev, rhs, panels = sources.shape[2:]
    n_gx, n_gy = lax.axis_size("gx"), lax.axis_size("gy")
    anywhere = pl.BlockSpec(memory_space=pltpu.HBM)
    sems = pltpu.SemaphoreType.DMA
    flat_rows = bases_in.shape[2] * bases_in.shape[3] * leaf_dev
    own, given = pl.pallas_call(
        functools.partial(kernel, n_gx, n_gy),
        out_shape=(
            jax.ShapeDtypeStruct((leaf_dev, rhs, panels), F32),
            jax.ShapeDtypeStruct((2, leaf_dev, rhs, panels), BF16),
        ),
        in_specs=[
            anywhere, anywhere, anywhere, pl.BlockSpec(memory_space=pltpu.SMEM),
            anywhere, anywhere, anywhere,
        ],
        out_specs=(anywhere, anywhere),
        scratch_shapes=[
            pltpu.VMEM((3, leaf_dev, rhs, panels), BF16),
            pltpu.VMEM((6,) + geometry.shape[2:], BF16),
            pltpu.VMEM((6, 8 * leaf_dev, panels), F32),
            pltpu.VMEM((3,) + near_lists.shape[2:], jnp.int32),
            pltpu.VMEM((27, leaf_dev, panels), F32),
            pltpu.VMEM((3 * leaf_dev, panels, FEATURES), BF16),
            pltpu.VMEM((9 * leaf_dev, FEATURES, panels), BF16),
            pltpu.VMEM((3, leaf_dev, rhs, panels), F32),
            pltpu.VMEM((3, leaf_dev, rhs, panels), BF16),
            pltpu.VMEM((leaf_dev, rhs, panels), BF16),
            pltpu.VMEM((flat_rows, panels), BF16),
            pltpu.VMEM((flat_rows, panels), BF16),
            pltpu.VMEM((panels // 128, flat_rows, 128), F32),
            pltpu.VMEM((leaf_dev, 128, panels), BF16),
            pltpu.VMEM((128, rhs), BF16),
            pltpu.VMEM(couplings.shape[2:], F32),
            pltpu.VMEM((32, 32 * n_gy), F32),
            pltpu.VMEM((64, 32 * n_gx), F32),
            pltpu.VMEM((4, 8, max(128, 8 * n_gx)), F32),
            pltpu.VMEM((n_gy, 8, max(128, 8 * n_gx)), F32),
            pltpu.VMEM((8, max(128, 8 * n_gx)), F32),
            pltpu.VMEM((4, 8, max(128, 8 * n_gx)), F32),
            pltpu.VMEM((4, 3 * panels, panels), BF16),
            pltpu.VMEM((64, 2 * rhs), F32),
            pltpu.VMEM((n_gy, 64, 2 * rhs), F32),
            pltpu.VMEM((48, 2 * rhs), F32),
            pltpu.VMEM((n_gx, 48, 2 * rhs), F32),
            pltpu.VMEM((8 * n_gx, rhs), F32),
            pltpu.VMEM((40, 2 * rhs), F32),
            pltpu.VMEM((n_gy, 40, 2 * rhs), F32),
            sems((6,)), sems((leaf_dev,)), sems((2,)),
            sems((6,)), sems((6,)), sems((3,)), sems((3,)),
            sems((3, 2)), sems((3, 2)), sems((3, 2)), sems((3, 2)),
            sems((n_gy,)), sems((n_gy,)),
            sems((n_gx,)), sems((n_gx,)),
            sems((n_gy,)), sems((n_gy,)),
            sems((n_gy,)), sems((n_gy,)),
            sems((4,)), sems((4,)),
        ],
        compiler_params=pltpu.CompilerParams(
            collective_id=0, has_side_effects=True, vmem_limit_bytes=61440 * 1024
        ),
    )(
        sources[0, 0], geometry[0, 0], near_lists[0, 0], far_lists[0, 0],
        bases_in.reshape(flat_rows, panels), bases_out.reshape(flat_rows, panels),
        couplings[0, 0],
    )
    potential = own + (given[0].astype(F32) + given[1].astype(F32))
    return potential.reshape(sources.shape)


def solution(mesh):
    in_specs = (
        P("gx", "gy", None, None, None),
        P("gx", "gy", None, None, None),
        P("gx", "gy", None, None),
        P("gx", "gy", None, None),
        P("gx", "gy", None, None, None, None),
        P("gx", "gy", None, None, None, None),
        P("gx", "gy", None, None, None),
    )
    out_specs = P("gx", "gy", None, None, None)
    return jax.shard_map(body, mesh=mesh, in_specs=in_specs, out_specs=out_specs, check_vma=False)
```
